32 devices in a mesh: dp: 8 (over z, x), tensor: 4 (over y, core).
Axes of the slice: x: 2, y: 2, z: 4, core: 2. Of those that a mesh axis runs over, the one named last changes fastest.
Arguments:
- tokens: bfloat16 [16, 1024, 768], P('dp', 'tensor'), may hold values from -6 to 6
- type_ids: int32 [16, 2], P('dp'), may hold values from 0 to 1
- boundary: int32 [16], P('dp'), may hold values from 128 to 896
- token_type_rows: float32 [2, 768], replicated, may hold values from -3 to 3
- query_key_value_weight: bfloat16 [768, 3, 768], P(None, None, 'tensor'), may hold values from -0.21875 to 0.21875
- b_qv: float32 [2, 768], P(None, 'tensor'), may hold values from -2 to 2
- output_weight: bfloat16 [768, 768], P('tensor'), may hold values from -0.875 to 0.875
- b_out: float32 [768], replicated, may hold values from -2 to 2
- gain_one: float32 [768], replicated, may hold values from 0.5 to 1.5
- shift_one: float32 [768], replicated, may hold values from -2 to 2
- gate_up_weight: bfloat16 [768, 2, 3072], P(None, None, 'tensor'), may hold values from -0.21875 to 0.21875
- gate_up_bias: float32 [2, 3072], P(None, 'tensor'), may hold values from -2 to 2
- down_weight: bfloat16 [3072, 768], P('tensor'), may hold values from -0.109375 to 0.109375
- b_down: float32 [768], replicated, may hold values from -2 to 2
- gain_two: float32 [768], replicated, may hold values from 0.5 to 1.5
- shift_two: float32 [768], replicated, may hold values from -2 to 2
- cotangent: bfloat16 [16, 1024, 768], P('dp', 'tensor'), may hold values from -6 to 6
Outputs:
- output: bfloat16 [16, 1024, 768], P('dp', 'tensor')
- grad_tokens: float32 [16, 1024, 768], P('dp', 'tensor')
- grad_type_table: float32 [2, 768], replicated
- grad_w_qkv: float32 [768, 3, 768], P(None, None, 'tensor')
- grad_b_qv: float32 [2, 768], P(None, 'tensor')
- grad_w_out: float32 [768, 768], P('tensor')
- grad_b_out: float32 [768], replicated
- grad_gain_one: float32 [768], replicated
- grad_shift_one: float32 [768], replicated
- grad_w_gu: float32 [768, 2, 3072], P(None, None, 'tensor')
- grad_b_gu: float32 [2, 3072], P(None, 'tensor')
- grad_w_down: float32 [3072, 768], P('tensor')
- grad_b_down: float32 [768], replicated
- grad_gain_two: float32 [768], replicated
- grad_shift_two: float32 [768], replicated
The draws below stay inside these ranges and needn't reach their ends.
All inputs are finite; a program needn't handle non-finite values.
Results may differ from the reference program's by a relative error of at most 0.017.
The reference program's roundings to bfloat16 on the way count: a program that leaves them out, or rounds other values in their place, can miss the bound.
Values may be sent and summed in bfloat16 or wider, within the bound.
A program may use at most 192 MiB of HBM per device.

```python
import jax
import jax.numpy as jnp
from jax import lax

D = 768
HEADS = 12
HEAD_DIM = 64
FF = 3072
TYPES = 2
SEQ_LEN = 1024
SEQS = 16


def with_ends(entries, key, least, high):
    spot = [jax.random.randint(jax.random.fold_in(key, axis), (), 0, length) for axis, length in enumerate(entries.shape)]
    main_axis = entries.shape.index(max(entries.shape))
    beside = spot[:main_axis] + [(spot[main_axis] + 1) % entries.shape[main_axis]] + spot[main_axis + 1:]
    return entries.at[tuple(spot)].set(least).at[tuple(beside)].set(high)


def shard_levels(rng, shape, shards, least, top_value):
    gain = 1.0
    for axis_at, shards_of in shards:
        steps = jax.random.uniform(jax.random.fold_in(jax.random.fold_in(rng, 6), axis_at), (shards_of,), jnp.float32, least / len(shards), top_value / len(shards))
        gain = gain * jnp.repeat(jnp.exp(steps), shape[axis_at] // shards_of).reshape((-1,) + (1,) * (len(shape) - 1 - axis_at))
    return gain


def bell_draw(rng, extent, scale, most, pieces=(), held_as=jnp.bfloat16):
    entries = jax.random.normal(rng, extent, jnp.float32) * scale
    if len(pieces) > 0:
        entries = shard_levels(rng, extent, pieces, -0.22, 0.18) * entries
    return jnp.clip(entries, min=-most, max=most).astype(held_as)


def setup_inputs(seed: int = 0) -> dict:
    arg_keys = jax.random.split(jax.random.key(seed), 18)
    tokens = bell_draw(arg_keys[0], (SEQS, SEQ_LEN, D), 1.0, 6.0, ((0, 8), (1, 4)))
    type_ids = with_ends(jax.random.randint(arg_keys[1], (SEQS, 2), 0, TYPES), jax.random.fold_in(arg_keys[1], 1), 0, TYPES - 1).astype(jnp.int32)
    boundary = with_ends(jax.random.randint(arg_keys[2], (SEQS,), SEQ_LEN // 8, SEQ_LEN - SEQ_LEN // 8 + 1), jax.random.fold_in(arg_keys[2], 1), SEQ_LEN // 8, (SEQ_LEN - SEQ_LEN // 8 + 1) - 1).astype(jnp.int32)
    token_type_rows = bell_draw(arg_keys[3], (TYPES, D), 0.5, 3.0, (), jnp.float32)
    query_key_value_weight = bell_draw(arg_keys[4], (D, 3, D), D ** -0.5, 0.21875, ((2, 4),))
    b_qv = bell_draw(arg_keys[5], (2, D), 0.3, 2.0, ((1, 4),), jnp.float32)
    output_weight = bell_draw(arg_keys[6], (D, D), (D // 16) ** -0.5, 0.875, ((0, 4),))
    b_out = bell_draw(arg_keys[7], (D,), 0.3, 2.0, (), jnp.float32)
    gain_one = jnp.clip(1.0 + 0.1 * jax.random.normal(arg_keys[8], (D,), jnp.float32), 0.5, 1.5)
    shift_one = bell_draw(arg_keys[9], (D,), 0.3, 2.0, (), jnp.float32)
    gate_up_weight = bell_draw(arg_keys[10], (D, 2, FF), D ** -0.5, 0.21875, ((2, 4),))
    gate_up_bias = bell_draw(arg_keys[11], (2, FF), 0.3, 2.0, ((1, 4),), jnp.float32)
    down_weight = bell_draw(arg_keys[12], (FF, D), FF ** -0.5, 0.109375, ((0, 4),))
    b_down = bell_draw(arg_keys[13], (D,), 0.3, 2.0, (), jnp.float32)
    gain_two = jnp.clip(1.0 + 0.1 * jax.random.normal(arg_keys[14], (D,), jnp.float32), 0.5, 1.5)
    shift_two = bell_draw(arg_keys[15], (D,), 0.3, 2.0, (), jnp.float32)
    cotangent = bell_draw(arg_keys[16], (SEQS, SEQ_LEN, D), 1.0, 6.0, ((0, 8), (1, 4)))
    return dict(tokens=tokens, type_ids=type_ids, boundary=boundary, token_type_rows=token_type_rows, query_key_value_weight=query_key_value_weight, b_qv=b_qv, output_weight=output_weight, b_out=b_out, gain_one=gain_one, shift_one=shift_one, gate_up_weight=gate_up_weight, gate_up_bias=gate_up_bias, down_weight=down_weight, b_down=b_down, gain_two=gain_two, shift_two=shift_two, cotangent=cotangent)


@jax.custom_vjp
def low(v):
    return lax.optimization_barrier(v.astype(jnp.bfloat16)).astype(jnp.float32)

@jax.custom_vjp
def low_back(v):
    return v

def low_keep(v):
    return (low(v), None)

def low_pass(kept, grad):
    return (grad,)

def back_keep(v):
    return (v, None)

def back_low(kept, grad):
    return (low(grad),)
low.defvjp(low_keep, low_pass)
low_back.defvjp(back_keep, back_low)
FULL_PRECISION = lax.Precision.HIGHEST
EPSILON = 1e-05

def layer_norm(values, scale_vec, shift_vec):
    center = lax.optimization_barrier(jnp.mean(values, axis=-1, keepdims=True))
    centered = values - center
    spread = lax.optimization_barrier(jnp.mean(centered * centered, axis=-1, keepdims=True))
    return centered * lax.rsqrt(spread + EPSILON) * scale_vec + shift_vec

def one_sequence(params, token_matrix, type_pair, bound):
    token_type_rows, query_key_value_weight, b_qv, output_weight, b_out, gain_one, shift_one, gate_up_weight, gate_up_bias, down_weight, b_down, gain_two, shift_two = params
    places = jnp.arange(SEQ_LEN)
    type_range = jnp.arange(TYPES)
    first_row = lax.optimization_barrier(jnp.sum(jnp.where((type_range == type_pair[0])[:, None], token_type_rows, 0.0), axis=0))
    second_row = lax.optimization_barrier(jnp.sum(jnp.where((type_range == type_pair[1])[:, None], token_type_rows, 0.0), axis=0))
    start_rows = jnp.where((places >= bound)[:, None], second_row[None, :], first_row[None, :])
    layer_input = token_matrix + start_rows
    qkv_full = jnp.einsum('ld,dcf->lcf', low(layer_input), query_key_value_weight, precision=FULL_PRECISION)
    bias_three = jnp.stack([b_qv[0], jnp.zeros_like(b_qv[0]), b_qv[1]])
    qkv_low = low(low_back(qkv_full + bias_three))
    queries = qkv_low[:, 0].reshape(SEQ_LEN, HEADS, HEAD_DIM)
    key_rows = qkv_low[:, 1].reshape(SEQ_LEN, HEADS, HEAD_DIM)
    value_rows = qkv_low[:, 2].reshape(SEQ_LEN, HEADS, HEAD_DIM)
    slopes = jnp.exp2(-8.0 * (jnp.arange(HEADS) + 1).astype(jnp.float32) / HEADS)
    distance = jnp.abs(places[:, None] - places[None, :]).astype(jnp.float32)
    scores = jnp.einsum('qhe,khe->hqk', queries, key_rows, precision=FULL_PRECISION) * HEAD_DIM ** (-0.5)
    scores = low_back(scores - slopes[:, None, None] * distance)
    probs = low(jax.nn.softmax(scores, axis=-1))
    context = jnp.einsum('hqk,khe->qhe', probs, value_rows, precision=FULL_PRECISION).reshape(SEQ_LEN, D)
    context = low(low_back(context))
    attn = low_back(jnp.dot(context, output_weight, precision=FULL_PRECISION))
    normed = layer_norm(attn + b_out + layer_input, gain_one, shift_one)
    gate_up = jnp.einsum('ld,dcf->lcf', low(normed), gate_up_weight, precision=FULL_PRECISION) + gate_up_bias
    gate_up = low_back(gate_up)
    hidden = low(jax.nn.gelu(gate_up[:, 0], approximate=False) * gate_up[:, 1])
    ffn_out = low_back(jnp.dot(hidden, down_weight, precision=FULL_PRECISION))
    return layer_norm(ffn_out + b_down + normed, gain_two, shift_two)

def reference(tokens, type_ids, boundary, token_type_rows, query_key_value_weight, b_qv, output_weight, b_out, gain_one, shift_one, gate_up_weight, gate_up_bias, down_weight, b_down, gain_two, shift_two, cotangent):
    params = tuple((item.astype(jnp.float32) for item in (token_type_rows, query_key_value_weight, b_qv, output_weight, b_out, gain_one, shift_one, gate_up_weight, gate_up_bias, down_weight, b_down, gain_two, shift_two)))
    token_matrix = tokens.astype(jnp.float32)
    step_fn = jax.checkpoint(one_sequence)

    def forward(all_rows, weights):

        def advance(carry, blocks):
            return (carry, step_fn(weights, blocks[0], blocks[1], blocks[2]))
        _, outputs = lax.scan(advance, jnp.zeros((), jnp.float32), (all_rows, type_ids, boundary))
        return outputs
    outputs, backward = jax.vjp(forward, token_matrix, params)
    grad_rows, grads = backward(cotangent.astype(jnp.float32))
    return (outputs.astype(jnp.bfloat16), grad_rows, grads[0], grads[1], grads[2], grads[3], grads[4], grads[5], grads[6], grads[7], grads[8], grads[9], grads[10], grads[11], grads[12])
```

```python
from functools import partial

import jax
import jax.numpy as jnp
from jax import lax
from jax.experimental import pallas as pl
from jax.experimental.pallas import tpu as pltpu
from jax.sharding import PartitionSpec as P

HEADS = 12
HEAD_DIM = 64
EPSILON = 1e-05
VMEM_LIMIT = 56 * 2**20
NT = (((1,), (1,)), ((), ()))
TN = (((0,), (0,)), ((), ()))
NN = (((1,), (0,)), ((), ()))


def dot(a, b, dims=NN):
    return lax.dot_general(a, b, dims, preferred_element_type=jnp.float32)


def fill_distance(base_ref, dist_ref):
    blocks = base_ref.shape[0]
    keys, queries = dist_ref.shape
    size = keys // blocks
    for kb in range(blocks):
        for qb in range(queries // size):
            row = lax.broadcasted_iota(jnp.int32, (size, size), 0) + base_ref[kb]
            col = lax.broadcasted_iota(jnp.int32, (size, size), 1) + base_ref[qb]
            dist_ref[kb * size : (kb + 1) * size, qb * size : (qb + 1) * size] = jnp.abs(
                row - col
            ).astype(jnp.float32)


def head_mask(shape, h):
    lane = lax.broadcasted_iota(jnp.int32, shape, 1)
    return (lane // HEAD_DIM) == h


def attention_forward_kernel(slope_ref, base_ref, q_ref, k_ref, v_ref, o_ref, lse_ref, dist_ref):
    pair = pl.program_id(0)

    @pl.when(pair == 0)
    def _():
        fill_distance(base_ref, dist_ref)

    k = k_ref[...]
    v = v_ref[...]
    q = q_ref[...]
    outs = []
    for h in range(2):
        qm = jnp.where(head_mask(q.shape, h), q, jnp.zeros_like(q)) * jnp.bfloat16(HEAD_DIM**-0.5)
        scores = dot(k, qm, NT) - slope_ref[2 * pair + h] * dist_ref[...]
        top = jnp.max(scores, axis=0, keepdims=True)
        p = jnp.exp(scores - top)
        total = jnp.sum(p, axis=0, keepdims=True)
        out = dot(v, p.astype(jnp.bfloat16), TN)
        outs.append(out[h * HEAD_DIM : (h + 1) * HEAD_DIM] / total)
        lse_ref[0, h : h + 1, :] = top + jnp.log(total)
    o_ref[...] = jnp.concatenate(outs, axis=0).T.astype(jnp.bfloat16)


def attention_forward(slopes, bases, q, k, v):
    rows, width = q.shape
    keys = k.shape[0]
    lanes = 2 * HEAD_DIM
    pairs = width // lanes
    return pl.pallas_call(
        attention_forward_kernel,
        grid=(pairs,),
        in_specs=[
            pl.BlockSpec(memory_space=pltpu.SMEM),
            pl.BlockSpec(memory_space=pltpu.SMEM),
            pl.BlockSpec((rows, lanes), lambda p: (0, p)),
            pl.BlockSpec((keys, lanes), lambda p: (0, p)),
            pl.BlockSpec((keys, lanes), lambda p: (0, p)),
        ],
        out_specs=[
            pl.BlockSpec((rows, lanes), lambda p: (0, p)),
            pl.BlockSpec((1, 2, rows), lambda p: (p, 0, 0)),
        ],
        out_shape=[
            jax.ShapeDtypeStruct((rows, width), jnp.bfloat16),
            jax.ShapeDtypeStruct((pairs, 2, rows), jnp.float32),
        ],
        scratch_shapes=[pltpu.VMEM((keys, rows), jnp.float32)],
        compiler_params=pltpu.CompilerParams(vmem_limit_bytes=VMEM_LIMIT),
        cost_estimate=pl.CostEstimate(
            flops=16 * rows * keys * width, bytes_accessed=12 * keys * width, transcendentals=0
        ),
    )(slopes, bases, q, k, v)


def attention_backward_kernel(
    slope_ref, base_ref, q_ref, k_ref, v_ref, do_ref, lse_ref, dq_ref, dk_ref, dv_ref, dist_ref
):
    pair = pl.program_id(0)

    @pl.when(pair == 0)
    def _():
        fill_distance(base_ref, dist_ref)

    k = k_ref[...]
    v = v_ref[...]
    q = q_ref[...]
    do = do_ref[...]
    dqs = []
    for h in range(2):
        mask = head_mask(q.shape, h)
        qm = jnp.where(mask, q, jnp.zeros_like(q)) * jnp.bfloat16(HEAD_DIM**-0.5)
        dom = jnp.where(mask, do, jnp.zeros_like(do))
        scores = dot(k, qm, NT) - slope_ref[2 * pair + h] * dist_ref[...]
        p = jnp.exp(scores - lse_ref[0, h : h + 1, :])
        dp = dot(v, dom, NT)
        inner = jnp.sum(p * dp, axis=0, keepdims=True)
        ds = (p * (dp - inner)).astype(jnp.bfloat16)
        dv = dot(p.astype(jnp.bfloat16), dom)
        dk = dot(ds, qm)
        if h == 0:
            dv_ref[...] = dv
            dk_ref[...] = dk
        else:
            dv_ref[...] += dv
            dk_ref[...] += dk
        dqs.append(dot(k, ds, TN)[h * HEAD_DIM : (h + 1) * HEAD_DIM])
    dq = jnp.concatenate(dqs, axis=0).T * (HEAD_DIM**-0.5)
    dq_ref[...] = dq.astype(jnp.bfloat16)


def attention_backward(slopes, bases, q, k, v, do, lse):
    rows, width = q.shape
    keys = k.shape[0]
    lanes = 2 * HEAD_DIM
    pairs = width // lanes
    row_spec = pl.BlockSpec((rows, lanes), lambda p: (0, p))
    key_spec = pl.BlockSpec((keys, lanes), lambda p: (0, p))
    return pl.pallas_call(
        attention_backward_kernel,
        grid=(pairs,),
        in_specs=[
            pl.BlockSpec(memory_space=pltpu.SMEM),
            pl.BlockSpec(memory_space=pltpu.SMEM),
            row_spec,
            key_spec,
            key_spec,
            row_spec,
            pl.BlockSpec((1, 2, rows), lambda p: (p, 0, 0)),
        ],
        out_specs=[row_spec, key_spec, key_spec],
        out_shape=[
            jax.ShapeDtypeStruct((rows, width), jnp.bfloat16),
            jax.ShapeDtypeStruct((keys, width), jnp.float32),
            jax.ShapeDtypeStruct((keys, width), jnp.float32),
        ],
        scratch_shapes=[pltpu.VMEM((keys, rows), jnp.float32)],
        compiler_params=pltpu.CompilerParams(vmem_limit_bytes=VMEM_LIMIT),
        cost_estimate=pl.CostEstimate(
            flops=40 * rows * keys * width, bytes_accessed=24 * keys * width, transcendentals=0
        ),
    )(slopes, bases, q, k, v, do, lse)


MESH = pl.DeviceIdType.MESH
UNITS = 8
WINDOW = 1


class Links:
    def __init__(self, ndp):
        self.ndp = ndp
        self.na = ndp // 2
        self.dp = lax.axis_index("dp")
        self.t = lax.axis_index("tensor")
        self.a = self.dp // 2
        self.b = lax.rem(self.dp, 2)
        self.y = self.t // 2
        self.c = lax.rem(self.t, 2)
        self.core = (self.dp, 2 * self.y + 1 - self.c)
        self.far = (self.dp, 2 * (1 - self.y) + self.c)
        self.pair = (2 * self.a + 1 - self.b, self.t)

    def up(self, off):
        return lax.rem(self.a + off, self.na)

    def down(self, off):
        return lax.rem(self.a + self.na - off, self.na)

    def column(self, off):
        return (2 * self.up(off) + self.b, self.t)

    def partners(self):
        return [self.core, self.far, self.pair] + [self.column(o) for o in range(1, self.na)]

    def greet(self):
        barrier = pltpu.get_barrier_semaphore()
        others = self.partners()
        for other in others:
            pl.semaphore_signal(barrier, inc=1, device_id=other, device_id_type=MESH)
        pl.semaphore_wait(barrier, len(others))


def remote(src, dst, send, recv, to):
    return pltpu.make_async_remote_copy(
        src_ref=src, dst_ref=dst, send_sem=send, recv_sem=recv, device_id=to, device_id_type=MESH
    )


def chunk_rows(ndp, rows):
    return -(-rows // (16 * ndp)) * 16


class Reducer:
    def __init__(self, links, refs, sems, rows, cols):
        self.l = links
        self.near, self.far, self.ybuf, self.xbuf, self.zbuf, self.own, self.fin = refs
        self.s = sems
        self.rows = rows
        self.cr = chunk_rows(links.ndp, rows)

    def clear_padding(self):
        padded = self.cr * self.l.ndp
        if padded > self.rows:
            self.near[:, self.rows :, :] = jnp.zeros_like(self.near[:, self.rows :, :])

    def at(self, ref, u, d):
        return ref.at[u, pl.ds(pl.multiple_of(d * self.cr, self.cr), self.cr)]

    def copy_y(self, u):
        s, r = self.s["y"]
        return remote(self.far.at[u], self.ybuf.at[u], s.at[u], r.at[u], self.l.far)

    def copy_x(self, u, i):
        s, r = self.s["x"]
        src = self.at(self.near, u, 2 * i + 1 - self.l.b)
        return remote(src, self.xbuf.at[u, i], s.at[u, i], r.at[u, i], self.l.pair)

    def copy_z(self, u, off):
        s, r = self.s["z"]
        src = self.at(self.near, u, 2 * self.l.up(off) + self.l.b)
        return remote(src, self.zbuf.at[u, off - 1], s.at[u, off - 1], r.at[u, off - 1], self.l.column(off))

    def copy_gz(self, u, off):
        s, r = self.s["gz"]
        dst = self.at(self.fin, u, self.l.dp)
        return remote(self.own.at[u], dst, s.at[u, off - 1], r.at[u, off - 1], self.l.column(off))

    def copy_gx(self, u, off):
        s, r = self.s["gx"]
        if off == 0:
            src, dst = self.own.at[u], self.at(self.fin, u, self.l.dp)
        else:
            d = 2 * self.l.down(off) + self.l.b
            src = dst = self.at(self.fin, u, d)
        return remote(src, dst, s.at[u, off], r.at[u, off], self.l.pair)

    def copy_own(self, u):
        return pltpu.make_async_copy(self.own.at[u], self.at(self.fin, u, self.l.dp), self.s["own"].at[u])

    def start_y(self, u):
        self.copy_y(u).start()

    def step_x(self, u):
        self.copy_y(u).wait_recv()
        if u + WINDOW < UNITS:
            self.start_y(u + WINDOW)
        f32 = jnp.float32
        rows = slice(0, self.rows)
        total = self.near[u, rows].astype(f32) + self.ybuf[u].astype(f32)
        self.near[u, rows] = total.astype(self.near.dtype)
        for i in range(self.l.na):
            self.copy_x(u, i).start()

    def step_z(self, u):
        f32 = jnp.float32
        for i in range(self.l.na):
            self.copy_x(u, i).wait_recv()
        for i in range(self.l.na):
            ref = self.at(self.near, u, 2 * i + self.l.b)
            ref[...] = (ref[...].astype(f32) + self.xbuf[u, i].astype(f32)).astype(self.near.dtype)
        for off in range(1, self.l.na):
            self.copy_z(u, off).start()

    def step_own(self, u):
        f32 = jnp.float32
        total = self.at(self.near, u, self.l.dp)[...].astype(f32)
        for off in range(1, self.l.na):
            self.copy_z(u, off).wait_recv()
            total = total + self.zbuf[u, off - 1].astype(f32)
        self.own[u] = total.astype(self.own.dtype)
        self.copy_gx(u, 0).start()
        for off in range(1, self.l.na):
            self.copy_gz(u, off).start()
        self.copy_own(u).start()

    def step_on(self, u):
        for off in range(1, self.l.na):
            self.copy_gz(u, off).wait_recv()
            self.copy_gx(u, off).start()

    def finish(self, u):
        self.copy_y(u).wait_send()
        for i in range(self.l.na):
            self.copy_x(u, i).wait_send()
        for off in range(1, self.l.na):
            self.copy_z(u, off).wait_send()
            self.copy_gz(u, off).wait_send()
        for off in range(self.l.na):
            self.copy_gx(u, off).wait()
        self.copy_own(u).wait()


def reducer_scratch(ndp, rows, cols, units=UNITS):
    bf = jnp.bfloat16
    na = ndp // 2
    cr, cc = chunk_rows(ndp, rows), cols
    dma = pltpu.SemaphoreType.DMA
    bufs = [
        pltpu.VMEM((units, cr * ndp, cols), bf),
        pltpu.VMEM((units, rows, cols), bf),
        pltpu.VMEM((units, rows, cols), bf),
        pltpu.VMEM((units, na, cr, cc), bf),
        pltpu.VMEM((units, na - 1, cr, cc), bf),
        pltpu.VMEM((units, cr, cc), bf),
    ]
    shapes = {"y": (units,), "x": (units, na), "z": (units, na - 1), "gz": (units, na - 1), "gx": (units, na)}
    sems = []
    for shape in shapes.values():
        sems += [dma(shape), dma(shape)]
    sems.append(dma((units,)))
    return bufs, sems, list(shapes)


class SmallSum:
    def __init__(self, links, mine, got, column, sems):
        self.l, self.mine, self.got, self.col = links, mine, got, column
        self.ss, self.rs = sems

    def swap(self, i):
        to = (self.l.core, self.l.far, self.l.pair)[i]
        return remote(self.mine.at[i], self.got.at[i], self.ss.at[i], self.rs.at[i], to)

    def spread(self, off):
        at = self.col.at[self.l.a]
        i = 2 + off
        return remote(at, at, self.ss.at[i], self.rs.at[i], self.l.column(off))

    def start(self, i):
        self.swap(i).start()

    def add(self, i):
        self.swap(i).wait_recv()
        total = self.mine[i] + self.got[i]
        if i < 2:
            self.mine[i + 1] = total
            self.start(i + 1)
        else:
            self.col[pl.ds(self.l.a, 1)] = total[None]
            for off in range(1, self.l.na):
                self.spread(off).start()

    def result(self):
        for off in range(1, self.l.na):
            self.spread(off).wait_recv()
        total = self.col[0]
        for i in range(1, self.l.na):
            total = total + self.col[i]
        return total

    def finish(self):
        for i in range(3):
            self.swap(i).wait_send()
        for off in range(1, self.l.na):
            self.spread(off).wait_send()


def small_scratch(ndp, rows, cols):
    f32 = jnp.float32
    na = ndp // 2
    dma = pltpu.SemaphoreType.DMA
    return [
        pltpu.VMEM((3, rows, cols), f32),
        pltpu.VMEM((3, rows, cols), f32),
        pltpu.VMEM((na, rows, cols), f32),
        dma((2 + na,)),
        dma((2 + na,)),
    ]


def reduce_kernel(ndp, rows, cols, parts, small_in, fin, small_out, *scratch):
    near, far, ybuf, xbuf, zbuf, own, cbuf = scratch[:7]
    names = ["y", "x", "z", "gz", "gx"]
    sems = {n: (scratch[7 + 2 * i], scratch[8 + 2 * i]) for i, n in enumerate(names)}
    sems["own"] = scratch[17]
    cs, cr, ld = scratch[18:21]
    sm = scratch[21:]
    l = Links(ndp)
    red = Reducer(l, (near, far, ybuf, xbuf, zbuf, own, fin), sems, rows, cols)
    small = SmallSum(l, sm[0], sm[1], sm[2], sm[3:5])
    f32 = jnp.float32

    def ccopy(u, i):
        return remote(parts.at[2 * i + 1, u], cbuf.at[u, i], cs.at[u, i], cr.at[u, i], l.core)

    def load(u, i):
        to = (near, far)[i].at[u, pl.ds(0, rows)]
        return pltpu.make_async_copy(parts.at[2 * i, u], to, ld.at[u, i])

    small.mine[0] = small_in[...]
    red.clear_padding()
    for u in range(UNITS):
        for i in (1, 0):
            load(u, i).start()
    l.greet()
    for u in range(UNITS):
        for i in (1, 0):
            ccopy(u, i).start()
    small.start(0)

    def merge(u, i):
        ref = (near, far)[i]
        load(u, i).wait()
        ccopy(u, i).wait_recv()
        total = ref[u, :rows].astype(f32) + cbuf[u, i].astype(f32)
        ref[u, :rows] = total.astype(ref.dtype)

    for u in range(UNITS):
        merge(u, 1)
        if u < WINDOW:
            red.start_y(u)
    for u in range(UNITS):
        merge(u, 0)
    for i in range(3):
        small.add(i)
    small_out[...] = small.result()
    for u in range(UNITS + 1):
        if u < UNITS:
            red.step_x(u)
        if u >= 1:
            red.step_own(u - 1)
        if u < UNITS:
            red.step_z(u)
        if u >= 1:
            red.step_on(u - 1)
    for u in range(UNITS):
        red.finish(u)
        for i in range(2):
            ccopy(u, i).wait_send()
    small.finish()


def reduce_gradients(ndp, parts, small):
    _, units, rows, cols = parts.shape
    bufs, sems, _ = reducer_scratch(ndp, rows, cols)
    dma = pltpu.SemaphoreType.DMA
    bf = jnp.bfloat16
    return pl.pallas_call(
        partial(reduce_kernel, ndp, rows, cols),
        in_specs=[pl.BlockSpec(memory_space=pl.ANY), pl.BlockSpec(memory_space=pltpu.VMEM)],
        out_specs=[pl.BlockSpec(memory_space=pl.ANY), pl.BlockSpec(memory_space=pltpu.VMEM)],
        out_shape=[
            jax.ShapeDtypeStruct((units, chunk_rows(ndp, rows) * ndp, cols), bf),
            jax.ShapeDtypeStruct(small.shape, jnp.float32),
        ],
        scratch_shapes=[
            *bufs,
            pltpu.VMEM((units, 2, rows, cols), bf),
            *sems,
            dma((units, 2)),
            dma((units, 2)),
            dma((units, 2)),
            *small_scratch(ndp, *small.shape),
        ],
        compiler_params=pltpu.CompilerParams(
            collective_id=1, has_side_effects=True, vmem_limit_bytes=VMEM_LIMIT
        ),
    )(parts, small)


def norm_forward(values):
    center = jnp.mean(values, axis=-1, keepdims=True)
    centered = values - center
    spread = jnp.mean(centered * centered, axis=-1, keepdims=True)
    scale = lax.rsqrt(spread + EPSILON)
    return centered * scale, scale


def norm_backward(grad, unit, scale, gain):
    n = grad * gain
    mean_n = jnp.mean(n, axis=-1, keepdims=True)
    mean_nx = jnp.mean(n * unit, axis=-1, keepdims=True)
    return scale * (n - mean_n - unit * mean_nx)


def gelu_parts(gate):
    cdf = 0.5 * (1.0 + lax.erf(gate * (0.5**0.5)))
    pdf = jnp.exp(-0.5 * gate * gate) * ((0.5 / jnp.pi) ** 0.5)
    return cdf, pdf


def per_device(
    tokens,
    type_ids,
    boundary,
    token_type_rows,
    query_key_value_weight,
    b_qv,
    output_weight,
    b_out,
    gain_one,
    shift_one,
    gate_up_weight,
    gate_up_bias,
    down_weight,
    b_down,
    gain_two,
    shift_two,
    cotangent,
):
    bf = jnp.bfloat16
    f32 = jnp.float32
    nt = lax.axis_size("tensor")
    ndp = lax.axis_size("dp")
    t = lax.axis_index("tensor")
    dp = lax.axis_index("dp")
    y = t // 2
    c = t % 2
    rows_dev = tokens.shape[1]
    width = tokens.shape[2]
    qcols = query_key_value_weight.shape[2]
    heads_dev = qcols // HEAD_DIM
    ff_dev = down_weight.shape[0]
    flip_y = [(i, i ^ 2) for i in range(nt)]
    flip_c = [(i, i ^ 1) for i in range(nt)]

    def over_y(a):
        return lax.ppermute(a, "tensor", flip_y)

    def over_c(a):
        return lax.ppermute(a, "tensor", flip_c)

    def pick(a, i):
        return lax.dynamic_index_in_dim(a, i, 0, keepdims=False)

    tok_other = over_y(pick(tokens, 1 - y))
    tok_rows = jnp.concatenate([pick(tokens, y), tok_other], axis=0)

    def gather_quarters(w):
        n = w.shape[0] // ndp
        if w.shape[0] % ndp:
            far = over_y(w)
            return w, over_c(w), far, over_c(far)
        part = over_y(lax.dynamic_slice_in_dim(w, dp * n, n, 0))
        far = lax.all_gather(part, "dp", axis=0, tiled=True)
        return w, over_c(w), far, over_c(far)

    w_qkv = gather_quarters(query_key_value_weight.reshape(width, 3 * qcols))
    w_out = gather_quarters(output_weight)
    w_gu = gather_quarters(gate_up_weight.reshape(width, 2 * ff_dev))
    w_down = gather_quarters(down_weight)
    cot_other = over_y(pick(cotangent, 1 - y))
    cot = jnp.concatenate([pick(cotangent, y), cot_other], axis=0).astype(f32)

    bqv_all = lax.all_gather(b_qv, "tensor", axis=0)
    bgu_all = lax.all_gather(gate_up_bias, "tensor", axis=0)
    bqv = [pick(bqv_all, t ^ s) for s in range(nt)]
    bgu = [pick(bgu_all, t ^ s) for s in range(nt)]

    pos_own = (2 * y + c) * rows_dev
    pos_far = (2 * (1 - y) + c) * rows_dev
    pos_own_p = (2 * y + 1 - c) * rows_dev
    pos_far_p = (2 * (1 - y) + 1 - c) * rows_dev
    bases = jnp.stack([pos_own, pos_far, pos_own_p, pos_far_p]).astype(jnp.int32)
    place = jnp.concatenate([pos_own + jnp.arange(rows_dev), pos_far + jnp.arange(rows_dev)])
    pair = pick(type_ids, y)
    bound = pick(boundary, y)
    kind = jnp.where(place >= bound, pair[1], pair[0])
    table0, table1 = token_type_rows[0], token_type_rows[1]
    entered = tok_rows.astype(f32) + jnp.where((kind == 1)[:, None], table1, table0)
    entered_low = entered.astype(bf)

    head_ids = jnp.concatenate(
        [(t ^ s) * heads_dev + jnp.arange(heads_dev) for s in range(nt)]
    )
    slopes = jnp.exp2(-8.0 * (head_ids + 1).astype(f32) / HEADS)

    qs, ks, vs = [], [], []
    for s in range(nt):
        bias = jnp.concatenate([bqv[s][0], jnp.zeros_like(bqv[s][0]), bqv[s][1]])
        part = (dot(entered_low, w_qkv[s]) + bias).astype(bf)
        qs.append(part[:, :qcols])
        ks.append(part[:, qcols : 2 * qcols])
        vs.append(part[:, 2 * qcols :])
    kv_send = jnp.concatenate([*(ks[s ^ 1] for s in range(nt)), *(vs[s ^ 1] for s in range(nt))], axis=1)
    kv_own = jnp.concatenate([*ks, *vs], axis=1)
    kv = jnp.concatenate([kv_own, over_c(kv_send)], axis=0)
    q = jnp.concatenate(qs, axis=1)
    k, v = kv[:, :width], kv[:, width:]
    context, lse = attention_forward(slopes, bases, q, k, v)
    w_out_full = jnp.concatenate(w_out, axis=0)
    attn = dot(context, w_out_full)
    unit_one, scale_one = norm_forward(attn + b_out + entered)
    h1 = unit_one * gain_one + shift_one
    h1_low = h1.astype(bf)
    gates, ups, hiddens = [], [], []
    ffn = 0.0
    for s in range(nt):
        gu = dot(h1_low, w_gu[s]) + bgu[s].reshape(-1)
        gate, up = gu[:, :ff_dev], gu[:, ff_dev:]
        cdf, _ = gelu_parts(gate)
        hidden = (gate * cdf * up).astype(bf)
        gates.append(gate)
        ups.append(up)
        hiddens.append(hidden)
        ffn = ffn + dot(hidden, w_down[s])
    unit_two, scale_two = norm_forward(ffn + b_down + h1)
    output = (unit_two * gain_two + shift_two).astype(bf)

    g_second = norm_backward(cot, unit_two, scale_two, gain_two)
    grad_gain_two = jnp.sum(cot * unit_two, axis=0)
    grad_shift_two = jnp.sum(cot, axis=0)
    grad_b_down = jnp.sum(g_second, axis=0)
    g_ffn = g_second.astype(bf)
    g_h1 = g_second
    grad_down, grad_gu, grad_bgu = [], [], []
    for s in range(nt):
        g_hidden = dot(g_ffn, w_down[s], NT)
        grad_down.append(dot(g_ffn, hiddens[s], TN).astype(bf))
        cdf, pdf = gelu_parts(gates[s])
        g_gate = g_hidden * ups[s] * (cdf + gates[s] * pdf)
        g_up = g_hidden * (gates[s] * cdf)
        g_gu = jnp.concatenate([g_gate, g_up], axis=1).astype(bf)
        grad_bgu.append(jnp.sum(g_gu.astype(f32), axis=0))
        grad_gu.append(dot(h1_low, g_gu, TN).astype(bf))
        g_h1 = g_h1 + dot(g_gu, w_gu[s], NT)
    g_mixed = norm_backward(g_h1, unit_one, scale_one, gain_one)
    grad_gain_one = jnp.sum(g_h1 * unit_one, axis=0)
    grad_shift_one = jnp.sum(g_h1, axis=0)
    grad_b_out = jnp.sum(g_mixed, axis=0)
    g_attn = g_mixed.astype(bf)
    grad_out_all = dot(g_attn, context, TN).astype(bf)
    grad_out = [grad_out_all[:, s * qcols : (s + 1) * qcols] for s in range(nt)]
    g_context = dot(g_attn, w_out_full, NT).astype(bf)
    dq, dk, dv = attention_backward(slopes, bases, q, k, v, g_context, lse)
    rows = q.shape[0]
    dkv_other = jnp.concatenate(
        [a[rows:, (s ^ 1) * qcols : ((s ^ 1) + 1) * qcols] for a in (dk, dv) for s in range(nt)], axis=1
    ).astype(bf)
    dkv = jnp.concatenate([dk[:rows], dv[:rows]], axis=1) + over_c(dkv_other).astype(f32)
    dkv = dkv.astype(bf)
    grad_qkv, grad_bqv = [], []
    g_entered = g_mixed
    for s in range(nt):
        cols = slice(s * qcols, (s + 1) * qcols)
        g_part = jnp.concatenate([dq[:, cols], dkv[:, :width][:, cols], dkv[:, width:][:, cols]], axis=1)
        grad_qkv.append(dot(entered_low, g_part, TN).astype(bf))
        sums = jnp.sum(g_part.astype(f32), axis=0)
        grad_bqv.append(jnp.stack([sums[:qcols], sums[2 * qcols :]]))
        g_entered = g_entered + dot(g_part, w_qkv[s], NT)
    second = (kind == 1).astype(f32)[:, None]
    sum_all = jnp.sum(g_entered, axis=0)
    sum_second = jnp.sum(g_entered * second, axis=0)
    grad_table = jnp.stack([sum_all - sum_second, sum_second])

    half = ff_dev // 2
    units = []
    for s in range(nt):
        mats = [grad_down[s], grad_gu[s][:, :ff_dev], grad_gu[s][:, ff_dev:], jnp.concatenate([grad_qkv[s], grad_out[s]], axis=1)]
        units.append(jnp.stack([m[:, i * half : (i + 1) * half] for m in mats for i in range(2)]))

    def by_quarter(parts):
        stacked = jnp.stack(parts)
        return jnp.stack([pick(stacked, t ^ s) for s in range(nt)])

    bq = by_quarter(grad_bqv)
    vectors = jnp.concatenate(
        [
            grad_table,
            jnp.stack([grad_b_out, grad_gain_one, grad_shift_one, grad_b_down, grad_gain_two, grad_shift_two]),
            by_quarter(grad_bgu).reshape(2 * nt, ff_dev),
            jnp.pad(bq.reshape(nt, 2 * qcols), ((0, 0), (0, width - 2 * qcols))),
        ],
        axis=0,
    )
    vectors = jnp.pad(vectors, ((0, -vectors.shape[0] % 8), (0, 0)))
    done, sums = reduce_gradients(ndp, jnp.stack(units), vectors)
    done = done[:, :width].astype(f32)
    full = [jnp.concatenate([done[2 * i], done[2 * i + 1]], axis=1) for i in range(4)]
    g_w_down = full[0].T
    g_w_gu = jnp.stack([full[1], full[2]], axis=1)
    g_w_qkv = full[3][:, : 3 * qcols].reshape(query_key_value_weight.shape)
    g_w_out = full[3][:, 3 * qcols :].T
    g_table = sums[:2]
    first = 8
    g_bgu = lax.dynamic_slice_in_dim(sums, first + 2 * t, 2, 0)
    g_bqv = pick(sums, first + 2 * nt + t)[: 2 * qcols].reshape(2, qcols)
    sums = [g_table, *(sums[i] for i in range(2, 8))]

    def back(rows_all):
        own = rows_all[:rows_dev]
        other = over_y(rows_all[rows_dev:].astype(bf)).astype(own.dtype)
        both = jnp.stack([own, other])
        return jnp.stack([pick(both, y), pick(both, 1 - y)])

    return (
        back(output),
        back(g_entered),
        sums[0],
        g_w_qkv,
        g_bqv,
        g_w_out,
        sums[1],
        sums[2],
        sums[3],
        g_w_gu,
        g_bgu,
        g_w_down,
        sums[4],
        sums[5],
        sums[6],
    )


def solution(mesh):
    in_specs = (
        P("dp", "tensor", None),
        P("dp", None),
        P("dp"),
        P(),
        P(None, None, "tensor"),
        P(None, "tensor"),
        P("tensor", None),
        P(),
        P(),
        P(),
        P(None, None, "tensor"),
        P(None, "tensor"),
        P("tensor", None),
        P(),
        P(),
        P(),
        P("dp", "tensor", None),
    )
    out_specs = (
        P("dp", "tensor", None),
        P("dp", "tensor", None),
        P(),
        P(None, None, "tensor"),
        P(None, "tensor"),
        P("tensor", None),
        P(),
        P(),
        P(),
        P(None, None, "tensor"),
        P(None, "tensor"),
        P("tensor", None),
        P(),
        P(),
        P(),
    )
    return jax.shard_map(
        per_device, mesh=mesh, in_specs=in_specs, out_specs=out_specs, check_vma=False
    )
```

```python
from functools import partial

import jax
import jax.numpy as jnp
from jax import lax
from jax.experimental import pallas as pl
from jax.experimental.pallas import tpu as pltpu
from jax.sharding import PartitionSpec as P

HEADS = 12
HEAD_DIM = 64
EPSILON = 1e-05
VMEM_LIMIT = 127 * 2**19
MESH = pl.DeviceIdType.MESH
BF = jnp.bfloat16
F32 = jnp.float32
NT = (((1,), (1,)), ((), ()))
TN = (((0,), (0,)), ((), ()))
NN = (((1,), (0,)), ((), ()))
DIRECT = (3,)


def dot(a, b, dims=NN):
    return lax.dot_general(a, b, dims, preferred_element_type=F32)


def remote(src, dst, send, recv, to):
    return pltpu.make_async_remote_copy(
        src_ref=src, dst_ref=dst, send_sem=send, recv_sem=recv, device_id=to, device_id_type=MESH
    )


def local(src, dst, sem):
    return pltpu.make_async_copy(src, dst, sem)


def dma(*shape):
    return pltpu.SemaphoreType.DMA(shape)


def chunk_rows(ndp, rows):
    return -(-rows // (16 * ndp)) * 16


class Links:
    def __init__(self, ndp):
        self.ndp = ndp
        self.na = ndp // 2
        self.dp = lax.axis_index("dp")
        self.t = lax.axis_index("tensor")
        self.a = self.dp // 2
        self.b = lax.rem(self.dp, 2)
        self.y = self.t // 2
        self.c = lax.rem(self.t, 2)
        self.core = (self.dp, 2 * self.y + 1 - self.c)
        self.far = (self.dp, 2 * (1 - self.y) + self.c)
        self.cross = (self.dp, 2 * (1 - self.y) + 1 - self.c)
        self.pair = (2 * self.a + 1 - self.b, self.t)

    def up(self, off):
        return lax.rem(self.a + off, self.na)

    def down(self, off):
        return lax.rem(self.a + self.na - off, self.na)

    def column(self, off):
        return (2 * self.up(off) + self.b, self.t)

    def quarter(self, s):
        return 2 * lax.rem(self.y + s // 2, 2) + lax.rem(self.c + s % 2, 2)

    def greet(self):
        barrier = pltpu.get_barrier_semaphore()
        others = [self.core, self.far, self.cross, self.pair]
        others += [self.column(o) for o in range(1, self.na)]
        for other in others:
            pl.semaphore_signal(barrier, inc=1, device_id=other, device_id_type=MESH)
        pl.semaphore_wait(barrier, len(others))


class Gather:
    def __init__(self, links, own, place, sems, rows):
        self.l, self.own, self.place, self.s = links, own, place, sems
        self.cr = rows // links.ndp
        self.fits = rows % (16 * links.ndp) == 0

    def relayed(self, m):
        return self.fits and m not in DIRECT

    def share(self, ref, d):
        return ref.at[pl.ds(pl.multiple_of(d * self.cr, 16), self.cr)]

    def pair_of(self, name, m, i=None):
        s, r = self.s[name]
        return (s.at[m], r.at[m]) if i is None else (s.at[m, i], r.at[m, i])

    def core(self, m):
        return remote(self.own.at[m], self.place(m, 1), *self.pair_of("c", m), self.l.core)

    def core_far(self, m):
        return remote(self.place(m, 2), self.place(m, 3), *self.pair_of("cf", m), self.l.core)

    def over_y(self, m):
        src, dst = self.own.at[m], self.place(m, 2)
        if self.relayed(m):
            src, dst = self.share(src, self.l.dp), self.share(dst, self.l.dp)
        return remote(src, dst, *self.pair_of("y", m), self.l.far)

    def over_x(self, m, off):
        at = self.share(self.place(m, 2), 2 * self.l.down(off) + self.l.b)
        return remote(at, at, *self.pair_of("x", m, off), self.l.pair)

    def over_z(self, m, off):
        at = self.share(self.place(m, 2), self.l.dp)
        return remote(at, at, *self.pair_of("z", m, off - 1), self.l.column(off))

    def step_spread(self, m):
        if self.relayed(m):
            self.over_y(m).wait_recv()
            self.over_x(m, 0).start()
            for off in range(1, self.l.na):
                self.over_z(m, off).start()

    def step_on(self, m):
        if self.relayed(m):
            for off in range(1, self.l.na):
                self.over_z(m, off).wait_recv()
                self.over_x(m, off).start()

    def step_core(self, m):
        if self.relayed(m):
            for off in range(self.l.na):
                self.over_x(m, off).wait_recv()
        else:
            self.over_y(m).wait_recv()
        self.core_far(m).start()

    def finish(self, m):
        self.core(m).wait_send()
        self.over_y(m).wait_send()
        self.core_far(m).wait_send()
        if self.relayed(m):
            for off in range(self.l.na):
                self.over_x(m, off).wait_send()
            for off in range(1, self.l.na):
                self.over_z(m, off).wait_send()


class Reducer:
    def __init__(self, links, refs, sems, rows, split):
        self.l = links
        self.near, self.far, self.ybuf, self.xbuf, self.zbuf, self.own, self.fin = refs
        self.s = sems
        self.split = split
        self.rows = rows // split
        self.cr = chunk_rows(links.ndp, self.rows)
        self.units = refs[3].shape[0]

    def clear_padding(self):
        used = self.rows * self.split
        if self.cr * self.l.ndp > self.rows:
            self.near[:, used:, :] = jnp.zeros_like(self.near[:, used:, :])

    def block(self, u):
        return u // self.split, u % self.split * self.rows

    def unit(self, ref, u):
        k, first = self.block(u)
        return ref.at[k, pl.ds(first, self.rows)]

    def at(self, ref, u, d):
        k, first = self.block(u)
        return ref.at[k, pl.ds(pl.multiple_of(first + d * self.cr, 16), self.cr)]

    def copy_y(self, u):
        s, r = self.s["y"]
        return remote(self.unit(self.far, u), self.unit(self.ybuf, u), s.at[u], r.at[u], self.l.far)

    def copy_x(self, u, i):
        s, r = self.s["x"]
        src = self.at(self.near, u, 2 * i + 1 - self.l.b)
        return remote(src, self.xbuf.at[u, i], s.at[u, i], r.at[u, i], self.l.pair)

    def copy_z(self, u, off):
        s, r = self.s["z"]
        src = self.at(self.near, u, 2 * self.l.up(off) + self.l.b)
        return remote(src, self.zbuf.at[u, off - 1], s.at[u, off - 1], r.at[u, off - 1], self.l.column(off))

    def copy_gz(self, u, off):
        s, r = self.s["gz"]
        dst = self.at(self.fin, u, self.l.dp)
        return remote(self.own.at[u], dst, s.at[u, off - 1], r.at[u, off - 1], self.l.column(off))

    def copy_gx(self, u, off):
        s, r = self.s["gx"]
        if off == 0:
            src, dst = self.own.at[u], self.at(self.fin, u, self.l.dp)
        else:
            src = dst = self.at(self.fin, u, 2 * self.l.down(off) + self.l.b)
        return remote(src, dst, s.at[u, off], r.at[u, off], self.l.pair)

    def copy_own(self, u):
        return local(self.own.at[u], self.at(self.fin, u, self.l.dp), self.s["own"].at[u])

    def start_y(self, u):
        if u < self.units:
            self.copy_y(u).start()

    def step_x(self, u):
        self.copy_y(u).wait_recv()
        ref = self.unit(self.near, u)
        ref[...] = (ref[...].astype(F32) + self.unit(self.ybuf, u)[...].astype(F32)).astype(BF)
        for i in range(self.l.na):
            self.copy_x(u, i).start()

    def step_z(self, u):
        for i in range(self.l.na):
            self.copy_x(u, i).wait_recv()
        for i in range(self.l.na):
            ref = self.at(self.near, u, 2 * i + self.l.b)
            ref[...] = (ref[...].astype(F32) + self.xbuf[u, i].astype(F32)).astype(BF)
        for off in range(1, self.l.na):
            self.copy_z(u, off).start()

    def step_own(self, u):
        total = self.at(self.near, u, self.l.dp)[...].astype(F32)
        for off in range(1, self.l.na):
            self.copy_z(u, off).wait_recv()
            total = total + self.zbuf[u, off - 1].astype(F32)
        self.own[u] = total.astype(BF)
        self.copy_gx(u, 0).start()
        for off in range(1, self.l.na):
            self.copy_gz(u, off).start()
        self.copy_own(u).start()

    def step_on(self, u):
        for off in range(1, self.l.na):
            self.copy_gz(u, off).wait_recv()
            self.copy_gx(u, off).start()

    def finish(self, u):
        self.copy_y(u).wait_send()
        for i in range(self.l.na):
            self.copy_x(u, i).wait_send()
        for off in range(1, self.l.na):
            self.copy_z(u, off).wait_send()
            self.copy_gz(u, off).wait_send()
        for off in range(self.l.na):
            self.copy_gx(u, off).wait()
        self.copy_own(u).wait()


class SmallSum:
    def __init__(self, links, mine, got, sems):
        self.l, self.mine, self.got = links, mine, got
        self.ss, self.rs = sems
        self.levels = got.shape[0]

    def partner(self, i):
        if i < 3:
            return (self.l.core, self.l.far, self.l.pair)[i]
        step = 2 ** (i - 3)
        a = self.l.a + step - 2 * step * lax.rem(self.l.a // step, 2)
        return (2 * a + self.l.b, self.l.t)

    def swap(self, i):
        return remote(self.mine.at[i], self.got.at[i], self.ss.at[i], self.rs.at[i], self.partner(i))

    def start(self, i):
        self.swap(i).start()

    def add(self, i):
        self.swap(i).wait_recv()
        total = self.mine[i] + self.got[i]
        if i + 1 < self.levels:
            self.mine[i + 1] = total
            self.start(i + 1)
        return total

    def finish(self):
        for i in range(self.levels):
            self.swap(i).wait_send()


def positions(links, size):
    y, c = links.y, links.c
    return [(2 * y + c) * size, (2 * (1 - y) + c) * size, (2 * y + 1 - c) * size, (2 * (1 - y) + 1 - c) * size]


def fill_distance(firsts, size, dist_ref):
    for kb, key in enumerate(firsts):
        for qb, query in enumerate(firsts[:2]):
            row = lax.broadcasted_iota(jnp.int32, (size, size), 0) + key
            col = lax.broadcasted_iota(jnp.int32, (size, size), 1) + query
            dist_ref[kb * size : (kb + 1) * size, qb * size : (qb + 1) * size] = jnp.abs(row - col).astype(F32)


def second_segment(firsts, size, kind_ref, block):
    place = lax.broadcasted_iota(jnp.int32, (size, 1), 0) + firsts[block]
    return jnp.where(place >= kind_ref[2], kind_ref[1], kind_ref[0]) == 1


def mean(a):
    return jnp.mean(a, axis=-1, keepdims=True)


def norm_forward(values):
    centered = values - mean(values)
    scale = lax.rsqrt(mean(centered * centered) + EPSILON)
    return centered * scale, scale


def norm_backward(grad, unit, scale, gain):
    n = grad * gain
    return scale * (n - mean(n) - unit * mean(n * unit))


def gelu_parts(gate):
    e = jnp.exp(gate * gate * -0.5)
    t = 1.0 / (1.0 + jnp.abs(gate) * (0.3275911 * 0.5**0.5))
    poly = t * (
        0.5 * 0.254829592
        + t * (0.5 * -0.284496736 + t * (0.5 * 1.421413741 + t * (0.5 * -1.453152027 + t * (0.5 * 1.061405429))))
    )
    tail = poly * e
    return jnp.where(gate < 0, tail, 1.0 - tail), e * 0.3989422804014327


class Names:
    def __init__(self):
        self.names, self.shapes = [], []

    def add(self, name, shape):
        self.names.append(name)
        self.shapes.append(shape)

    def pair(self, name, *shape):
        self.add(name + "_s", dma(*shape))
        self.add(name + "_r", dma(*shape))


ANY = pl.BlockSpec(memory_space=pl.ANY)
VMEM = pl.BlockSpec(memory_space=pltpu.VMEM)
SMEM = pl.BlockSpec(memory_space=pltpu.SMEM)


class Refs:
    def __init__(self, names, refs):
        self.__dict__.update(zip(names, refs))

    def sems(self, name):
        return getattr(self, name + "_s"), getattr(self, name + "_r")


ENTER_IN = ["tokens", "w4", "bias", "table", "kinds", "slopes"]
ENTER_OUT = ["x", "qkv", "kvp", "ctx", "lse", "wall", "biases"]


def enter_kernel(ndp, names, *refs):
    r = Refs(names, refs)
    l = Links(ndp)
    nm, width = r.w4.shape[0], r.w4.shape[1]
    size = r.tokens.shape[1]
    rows = 2 * size
    heads_dev = HEADS // 4
    qk = heads_dev * HEAD_DIM
    firsts = positions(l, size)

    def place(m, s):
        return r.wa.at[s] if m == 0 else r.wall.at[m, s]

    g = Gather(l, r.w4, place, {n: r.sems("g" + n) for n in ("c", "cf", "y", "x", "z")}, width)
    tok_own = local(r.tokens.at[l.y], r.tok.at[pl.ds(0, size)], r.ld.at[0])
    wa_own = local(r.w4.at[0], r.wa.at[0], r.ld.at[1])
    copies = [local(r.w4.at[m], r.wall.at[m, 0], r.ld.at[1 + m]) for m in range(1, nm)]
    tok_own.start()
    wa_own.start()
    tok_far = remote(r.tokens.at[1 - l.y], r.tok.at[pl.ds(size, size)], *(a.at[0] for a in r.sems("tk")), l.far)
    bias_to = [
        remote(r.bias, r.biases.at[s], *(a.at[s] for a in r.sems("bi")), to)
        for s, to in ((1, l.core), (2, l.far), (3, l.cross))
    ]

    def kv_send(s):
        other = s + 1 - 2 * (s % 2)
        src = r.qkvb.at[s, pl.ds(qk, 2 * qk)]
        return remote(src, r.kvb.at[other], *(a.at[s] for a in r.sems("kv")), l.core)

    def kv_wait(s):
        other = s + 1 - 2 * (s % 2)
        src = r.qkvb.at[other, pl.ds(qk, 2 * qk)]
        return remote(src, r.kvb.at[s], *(a.at[other] for a in r.sems("kv")), l.core)

    l.greet()
    g.over_y(0).start()
    tok_far.start()
    for b in bias_to:
        b.start()
    g.core(0).start()
    r.biases[0] = r.bias[...]

    def enter(block):
        at = pl.ds(block * size, size)
        second = second_segment(firsts, size, r.kinds, block)
        x = r.tok[at].astype(F32) + jnp.where(second, r.table[1:2], r.table[0:1])
        r.xb[at] = x
        r.xl[at] = x.astype(BF)

    def project(s, block):
        at = slice(block * size, (block + 1) * size)
        column = r.biases[s].T[: 3 * qk, 0:1]
        part = dot(r.wa[s, : 3 * qk], r.xl[at], NT) + column
        r.qkvb[s, :, at] = part.astype(BF)

    tok_own.wait()
    enter(0)
    wa_own.wait()
    project(0, 0)
    fill_distance(firsts, size, r.dist)
    g.step_spread(0)
    for b in bias_to:
        b.wait_recv()
    g.core(0).wait_recv()
    project(1, 0)
    tok_far.wait_recv()
    for m in range(1, nm):
        g.over_y(m).start()
    enter(1)
    x_out = local(r.xb, r.x, r.ld.at[4])
    x_out.start()
    for s in (0, 1):
        project(s, 1)
        kv_send(s).start()
    g.step_on(0)
    for m in range(1, nm):
        g.core(m).start()
        copies[m - 1].start()
    for m in range(1, nm):
        g.step_spread(m)
    g.step_core(0)
    for m in range(1, nm):
        g.step_on(m)
    g.core_far(0).wait_recv()
    for s in (2, 3):
        project(s, 0)
        project(s, 1)
        kv_send(s).start()
    wa_out = local(r.wa, r.wall.at[0], r.ld.at[5])
    wa_out.start()

    def head(h, carry):
        s, j = h // heads_dev, h % heads_dev

        @pl.when(j == 0)
        def _():
            kv_wait(s).wait_recv()

        def lines(ref, first):
            return ref[s, pl.ds(pl.multiple_of(first + j * HEAD_DIM, HEAD_DIM), HEAD_DIM), :]

        q = lines(r.qkvb, 0) * BF(HEAD_DIM**-0.5)
        slope = r.slopes[h]
        scores = [
            dot(key, q, TN) - slope * r.dist[i * rows : (i + 1) * rows]
            for i, key in enumerate((lines(r.qkvb, qk), lines(r.kvb, 0)))
        ]
        top = jnp.maximum(*(jnp.max(a, axis=0, keepdims=True) for a in scores))
        probs = [jnp.exp(a - top) for a in scores]
        total = sum(jnp.sum(a, axis=0, keepdims=True) for a in probs)
        values = (lines(r.qkvb, 2 * qk), lines(r.kvb, qk))
        out = sum(dot(v, p.astype(BF)) for v, p in zip(values, probs))
        r.ctxb[s, pl.ds(pl.multiple_of(j * HEAD_DIM, HEAD_DIM), HEAD_DIM), :] = (out * (1.0 / total)).astype(BF)
        r.lse[pl.ds(h, 1), :] = top + jnp.log(total)
        return carry

    lax.fori_loop(0, HEADS, head, 0)
    outs = [
        local(r.qkvb, r.qkv, r.ld.at[6]),
        local(r.kvb, r.kvp, r.ld.at[7]),
        local(r.ctxb, r.ctx, r.ld.at[8]),
    ]
    for o in outs:
        o.start()
    for m in range(1, nm):
        g.step_core(m)
    for m in range(1, nm):
        g.core(m).wait_recv()
        g.core_far(m).wait_recv()
        copies[m - 1].wait()
    for m in range(nm):
        g.finish(m)
    for s in range(4):
        kv_send(s).wait_send()
    tok_far.wait_send()
    for b in bias_to:
        b.wait_send()
    for o in outs + [x_out, wa_out]:
        o.wait()


def enter_layer(ndp, tokens, w4, bias, table, kinds, slopes):
    nm, width = w4.shape[0], w4.shape[1]
    size = tokens.shape[1]
    rows = 2 * size
    qk = HEADS // 4 * HEAD_DIM
    na = ndp // 2
    n = Names()
    n.add("wa", pltpu.VMEM((4, width, width), BF))
    n.add("tok", pltpu.VMEM((rows, width), BF))
    n.add("xb", pltpu.VMEM((rows, width), F32))
    n.add("xl", pltpu.VMEM((rows, width), BF))
    n.add("qkvb", pltpu.VMEM((4, 3 * qk, rows), BF))
    n.add("kvb", pltpu.VMEM((4, 2 * qk, rows), BF))
    n.add("ctxb", pltpu.VMEM((4, qk, rows), BF))
    n.add("dist", pltpu.VMEM((2 * rows, rows), F32))
    n.add("ld", dma(9))
    n.pair("tk", 1)
    n.pair("bi", 4)
    n.pair("kv", 4)
    n.pair("gc", nm)
    n.pair("gcf", nm)
    n.pair("gy", nm)
    n.pair("gx", nm, na)
    n.pair("gz", nm, na - 1)
    shape = jax.ShapeDtypeStruct
    return pl.pallas_call(
        partial(enter_kernel, ndp, ENTER_IN + ENTER_OUT + n.names),
        in_specs=[ANY, ANY, VMEM, VMEM, SMEM, SMEM],
        out_specs=[ANY, ANY, ANY, ANY, VMEM, ANY, VMEM],
        out_shape=[
            shape((rows, width), F32),
            shape((4, 3 * qk, rows), BF),
            shape((4, 2 * qk, rows), BF),
            shape((4, qk, rows), BF),
            shape((HEADS, rows), F32),
            shape((nm, 4, width, width), BF),
            shape((4, *bias.shape), F32),
        ],
        scratch_shapes=n.shapes,
        compiler_params=pltpu.CompilerParams(
            collective_id=0, has_side_effects=True, vmem_limit_bytes=VMEM_LIMIT
        ),
    )(tokens, w4, bias, table, kinds, slopes)


LEAVE_IN = ["x", "qkv", "kvp", "ctx", "lse", "wall", "biases", "vecs", "cot", "kinds", "slopes"]
LEAVE_OUT = ["fin", "sums", "out", "gtok", "cbuf"]
B_OUT, GAIN_ONE, SHIFT_ONE, B_DOWN, GAIN_TWO, SHIFT_TWO = range(6)
DOWN, GATE, UP, ATTN = range(4)
ROW_GU, ROW_QV, SMALL_ROWS = 8, 16, 24


def leave_kernel(ndp, names, split, *refs):
    r = Refs(names, refs)
    l = Links(ndp)
    rows, width = r.x.shape
    size = rows // 2
    heads_dev = HEADS // 4
    qk = heads_dev * HEAD_DIM
    firsts = positions(l, size)
    stages = r.cstage.shape[0]
    red = Reducer(
        l,
        (r.near, r.far, r.ybuf, r.xbuf, r.zbuf, r.own, r.fin),
        {**{n: r.sems("r" + n) for n in ("y", "x", "z", "gz", "gx")}, "own": r.rown},
        width,
        split,
    )
    ticks, tail = schedule(red.units)
    small = SmallSum(l, r.smine, r.sgot, r.sems("sm"))
    sv = r.smine.at[0]

    def vec(i):
        return r.vecs[i : i + 1, :]

    def core_copy(k, i):
        src = r.cstage.at[k % stages, i]
        return remote(src, r.cbuf.at[k, i], *(a.at[k, i] for a in r.sems("co")), l.core)

    def fetch(k, i):
        return local(r.cbuf.at[k, i], r.cload, r.cl.at[0])

    def room(k, i):
        if k >= stages:
            core_copy(k - stages, i).wait_send()

    def start_fetch(k, i):
        core_copy(k, i).wait_recv()
        fetch(k, i).start()

    def merge(k, i, first, value):
        at = pl.ds(first, value.shape[0])
        total = value + r.cload[at].astype(F32)
        (r.near, r.far)[i][k, at] = total.astype(BF)

    def load_weights(s, buf):
        return local(r.wall.at[pl.ds(1, 3), s], r.wbuf.at[buf], r.wl.at[buf])

    cot_own = local(r.cot.at[l.y], r.cotb.at[pl.ds(0, size)], r.ld.at[0])
    cot_far = remote(r.cot.at[1 - l.y], r.cotb.at[pl.ds(size, size)], *(a.at[0] for a in r.sems("ct")), l.far)

    def order(i):
        return 2 * (i % 2) + i // 2

    def ffn_phase(wo, gh, a_ref, b_ref, hid, unit, hl, ht, gs, r1):
        xb, acc, gf = gh, r.gm, hl
        lx = local(r.x, xb, r.ld.at[1])
        lo = local(r.wall.at[0, pl.ds(0, 4), pl.ds(3 * qk, qk)], wo, r.ld.at[2])
        lc = local(r.ctx, r.ctxb, r.ld.at[3])
        for c in (lc, lo, lx, load_weights(0, 0), load_weights(2, 1), cot_own):
            c.start()
        l.greet()
        cot_far.start()
        red.clear_padding()
        sv[...] = jnp.zeros_like(sv)
        lc.wait()
        lo.wait()
        lx.wait()
        for s in range(4):
            part = dot(r.ctxb[s], wo[s], TN)
            if s == 0:
                acc[...] = part + xb[...] + vec(B_OUT)
            else:
                acc[...] += part
        u1, s1 = norm_forward(acc[...])
        unit[...] = u1
        r1[...] = s1
        h1 = u1 * vec(GAIN_ONE) + vec(SHIFT_ONE)
        acc[...] = h1 + vec(B_DOWN)
        hl[...] = h1.astype(BF)
        ht[...] = h1.T.astype(BF)

        def forward(i, carry):
            s, buf = order(i), i % 2
            load_weights(s, buf).wait()
            for half in range(2):
                at = slice(half * size, (half + 1) * size)
                gate = dot(hl[at], r.wbuf[buf, 0]) + r.biases[s, 1:2, :]
                up = dot(hl[at], r.wbuf[buf, 1]) + r.biases[s, 2:3, :]
                cdf, pdf = gelu_parts(gate)
                act = gate * cdf
                a_ref[s, at] = act.astype(BF)
                b_ref[s, at] = (up * (cdf + gate * pdf)).astype(BF)
                hidden = (act * up).astype(BF)
                hid[s, at] = hidden
                acc[at] += dot(hidden, r.wbuf[buf, 2])

            @pl.when(i < 2)
            def _():
                load_weights(order(i + 2), buf).start()

            return carry

        lax.fori_loop(0, 4, forward, 0)
        u2, s2 = norm_forward(acc[...])
        out = u2 * vec(GAIN_TWO) + vec(SHIFT_TWO)
        r.outb[...] = out.astype(BF)
        cot_own.wait()
        cot_far.wait_recv()
        cot = r.cotb[...].astype(F32)
        g2 = norm_backward(cot, u2, s2, vec(GAIN_TWO))
        sv[6:7, :] = jnp.sum(cot * u2, axis=0, keepdims=True)
        sv[7:8, :] = jnp.sum(cot, axis=0, keepdims=True)
        sv[5:6, :] = jnp.sum(g2, axis=0, keepdims=True)
        gh[...] = g2
        gf[...] = g2.astype(BF)
        gs[...] = g2.T.astype(BF)

        for i, s in ((1, 3), (0, 1)):
            r.cstage[DOWN % stages, i] = dot(gs[...], hid[s]).astype(BF)
            core_copy(DOWN, i).start()

        def backward(s, buf):
            load = None
            g_hidden = dot(gf[...], r.wbuf[buf, 2], NT)
            g_gate = (g_hidden * b_ref[s].astype(F32)).astype(BF)
            g_up = (g_hidden * a_ref[s].astype(F32)).astype(BF)
            row = ROW_GU + 2 * l.quarter(s)
            sv[pl.ds(row, 1), :] = jnp.sum(g_gate.astype(F32), axis=0, keepdims=True)
            sv[pl.ds(row + 1, 1), :] = jnp.sum(g_up.astype(F32), axis=0, keepdims=True)
            gh[...] += dot(g_gate, r.wbuf[buf, 0], NT)
            gh[...] += dot(g_up, r.wbuf[buf, 1], NT)
            return g_gate, g_up

        for i, s, buf in ((1, 3, 1), (0, 1, 0)):
            g_gate, g_up = backward(s, buf)
            load_weights(s - 1, buf).start()
            for k, g in ((GATE, g_gate), (UP, g_up)):
                room(k, i)
                r.cstage[k % stages, i] = dot(ht[...], g).astype(BF)
                core_copy(k, i).start()
            start_fetch(DOWN, i)
            value = dot(gs[...], hid[s - 1])
            fetch(DOWN, i).wait()
            merge(DOWN, i, 0, value)
            if i == 1:
                red.start_y(0)
                red.start_y(1)
        for i, s, buf in ((1, 2, 1), (0, 0, 0)):
            load_weights(s, buf).wait()
            g_gate, g_up = backward(s, buf)
            for k, g in ((GATE, g_gate), (UP, g_up)):
                start_fetch(k, i)
                value = dot(ht[...], g)
                fetch(k, i).wait()
                merge(k, i, 0, value)
        g_h1 = gh[...]
        unit_one = unit[...]
        sv[3:4, :] = jnp.sum(g_h1 * unit_one, axis=0, keepdims=True)
        sv[4:5, :] = jnp.sum(g_h1, axis=0, keepdims=True)
        gm = norm_backward(g_h1, unit_one, r1[...], vec(GAIN_ONE))
        sv[2:3, :] = jnp.sum(gm, axis=0, keepdims=True)
        r.gm[...] = gm
        ga = gm.astype(BF)
        r.cotb[...] = ga
        for s in range(4):
            r.gctx[s] = dot(wo[s], ga, NT).astype(BF)

    v = pltpu.VMEM
    pl.run_scoped(
        ffn_phase,
        v((4, qk, width), BF),
        v((rows, width), F32),
        v((4, rows, width), BF),
        v((4, rows, width), BF),
        v((4, rows, width), BF),
        v((rows, width), F32),
        v((rows, width), BF),
        v((width, rows), BF),
        v((width, rows), BF),
        v((rows, 1), F32),
    )

    def attention_phase(wq, qkvb, kvb, xb, xl, dist, dqkv, dkvo, dkvs):
        lq = local(r.qkv, qkvb, r.ld.at[4])
        lk = local(r.kvp, kvb, r.ld.at[5])
        lw = local(r.wall.at[0, pl.ds(0, 4), pl.ds(0, 3 * qk)], wq, r.ld.at[6])
        lx = local(r.x, xb, r.ld.at[7])
        for c in (lq, lk, lw, lx):
            c.start()
        fill_distance(firsts, size, dist)

        def other(s):
            return s + 1 - 2 * (s % 2)

        def send(s):
            return remote(dkvs.at[s], r.dkvr.at[other(s)], *(a.at[s] for a in r.sems("dk")), l.core)

        def arrived(s):
            return remote(dkvs.at[other(s)], r.dkvr.at[s], *(a.at[other(s)] for a in r.sems("dk")), l.core)

        lq.wait()
        lk.wait()

        def head(h, carry):
            s, j = h // heads_dev, h % heads_dev

            def span(first):
                return pl.ds(pl.multiple_of(first + j * HEAD_DIM, HEAD_DIM), HEAD_DIM)

            qt = qkvb[s, span(0), :] * BF(HEAD_DIM**-0.5)
            q = qt.T
            dot_t = r.gctx[s, span(0), :]
            do = dot_t.T
            slope = r.slopes[h]
            lse = r.lse[pl.ds(h, 1), :]
            keys = (qkvb[s, span(qk), :], kvb[s, span(0), :])
            values = (qkvb[s, span(2 * qk), :], kvb[s, span(qk), :])
            probs = [
                jnp.exp(dot(key, qt, TN) - slope * dist[i * rows : (i + 1) * rows] - lse)
                for i, key in enumerate(keys)
            ]
            g_probs = [dot(value, dot_t, TN) for value in values]
            inner = sum(jnp.sum(p * g, axis=0, keepdims=True) for p, g in zip(probs, g_probs))
            g_scores = [(p * (g - inner)).astype(BF) for p, g in zip(probs, g_probs)]
            dq = sum(dot(key, g) for key, g in zip(keys, g_scores))
            dqkv[s, span(0), :] = (dq * HEAD_DIM**-0.5).astype(BF)
            dk = [dot(g, q).T for g in g_scores]
            dv = [dot(p.astype(BF), do).T for p in probs]
            dkvo[s, span(0), :] = dk[0]
            dkvo[s, span(qk), :] = dv[0]
            dkvs[s, span(0), :] = dk[1].astype(BF)
            dkvs[s, span(qk), :] = dv[1].astype(BF)

            @pl.when(j == heads_dev - 1)
            def _():
                send(s).start()

            for at, steps in ticks.items():

                @pl.when(h == at)
                def _(steps=steps):
                    for name, u in steps:
                        getattr(red, name)(u)

            return carry

        lax.fori_loop(0, HEADS, head, 0)
        lw.wait()
        lx.wait()
        xl[...] = xb[...].astype(BF)
        ones = jnp.ones((8, rows), BF)
        for s in range(4):
            arrived(s).wait_recv()
            dqkv[s, qk:, :] = (dkvo[s] + r.dkvr[s].astype(F32)).astype(BF)
            g = dqkv[s]
            sv[pl.ds(ROW_QV + l.quarter(s), 1), : 3 * qk] = dot(ones, g, NT)[0:1]
            r.gm[...] += dot(g, wq[s], TN)
        g_entered = r.gm[...]
        total = jnp.sum(g_entered, axis=0, keepdims=True)
        second = sum(
            jnp.sum(
                jnp.where(second_segment(firsts, size, r.kinds, i), g_entered[i * size : (i + 1) * size], 0.0),
                axis=0,
                keepdims=True,
            )
            for i in range(2)
        )
        sv[0:1, :] = total - second
        sv[1:2, :] = second
        small.start(0)
        r.gfar[...] = g_entered[size:].astype(BF)

        def attn_parts(s):
            return ((0, dot(dqkv[s], xl[...])), (3 * qk, dot(r.ctxb[s], r.cotb[...])))

        for i, s in ((1, 3), (0, 1)):
            room(ATTN, i)
            for first, value in attn_parts(s):
                r.cstage[ATTN % stages, i, pl.ds(first, value.shape[0])] = value.astype(BF)
            core_copy(ATTN, i).start()
        small.add(0)
        for i, s in ((1, 2), (0, 0)):
            start_fetch(ATTN, i)
            parts = attn_parts(s)
            fetch(ATTN, i).wait()
            for first, value in parts:
                merge(ATTN, i, first, value)
        small.add(1)
        for s in range(4):
            send(s).wait_send()

    pl.run_scoped(
        attention_phase,
        v((4, 3 * qk, width), BF),
        v((4, 3 * qk, rows), BF),
        v((4, 2 * qk, rows), BF),
        v((rows, width), F32),
        v((rows, width), BF),
        v((2 * rows, rows), F32),
        v((4, 3 * qk, rows), BF),
        v((4, 2 * qk, rows), F32),
        v((4, 2 * qk, rows), BF),
    )

    out_own = local(r.outb.at[pl.ds(0, size)], r.out.at[l.y], r.ld.at[8])
    out_far = remote(r.outb.at[pl.ds(size, size)], r.out.at[l.y], *(a.at[0] for a in r.sems("ou")), l.far)
    tok_own = local(r.gm.at[pl.ds(0, size)], r.gtok.at[l.y], r.ld.at[9])
    tok_far = remote(r.gfar, r.ggot, *(a.at[0] for a in r.sems("gt")), l.far)
    out_own.start()
    tok_own.start()
    total = small.add(2)
    for name, u in tail:
        if name == "rows":
            out_far.start()
            tok_far.start()
        else:
            getattr(red, name)(u)
    for i in range(3, small.levels):
        total = small.add(i)
    r.sums[...] = total
    tok_far.wait_recv()
    r.gm[size:] = r.ggot[...].astype(F32)
    tok_got = local(r.gm.at[pl.ds(size, size)], r.gtok.at[1 - l.y], r.ld.at[10])
    tok_got.start()
    for u in range(red.units):
        red.finish(u)
    for k in range(4 - stages, 4):
        for i in range(2):
            core_copy(k, i).wait_send()
    small.finish()
    cot_far.wait_send()
    out_far.wait()
    tok_far.wait_send()
    for c in (out_own, tok_own, tok_got):
        c.wait()


def schedule(units):
    if units < 8:
        names = ("step_x", "step_z", "step_own", "step_on")
        first = [("start_y", u) for u in range(2, units)]
        return {}, first + [(n, u) for u in range(units) for n in names] + [("rows", 0)]
    ticks = {2: [("step_x", 0), ("step_x", 1), ("start_y", 2), ("start_y", 3)],
             5: [("step_z", 0), ("step_z", 1)],
             8: [("step_own", 0), ("step_own", 1)],
             11: [("step_on", 0), ("step_on", 1)]}
    tail = [("step_x", 2), ("start_y", 4), ("step_x", 3)]
    for u in range(4, units + 3):
        tail += [("step_z", u - 2)] if u - 2 < units else []
        tail += [("step_x", u), ("start_y", u + 1)] if u < units else []
        tail += [("rows", 0)] if u == units - 1 else []
        tail += [("step_own", u - 2)] if u - 2 < units else []
        tail += [("step_on", u - 3)] if 2 <= u - 3 < units else []
    return ticks, tail


def leave_layer(ndp, inputs, cot):
    x, wall = inputs[0], inputs[5]
    rows, width = x.shape
    nm = wall.shape[0]
    size = rows // 2
    qk = HEADS // 4 * HEAD_DIM
    na = ndp // 2
    split = 2 if width % (32 * ndp) == 0 else 1
    stages = 2 if split == 2 else 1
    units = nm * split
    cr = chunk_rows(ndp, width // split)
    padded = max(width, cr * ndp + width - width // split)
    n = Names()
    v = pltpu.VMEM
    n.add("near", v((nm, padded, width), BF))
    n.add("far", v((nm, width, width), BF))
    n.add("ybuf", v((nm, width, width), BF))
    n.add("xbuf", v((units, na, cr, width), BF))
    n.add("zbuf", v((units, na - 1, cr, width), BF))
    n.add("own", v((units, cr, width), BF))
    n.add("cstage", v((stages, 2, width, width), BF))
    n.add("cload", v((width, width), BF))
    n.add("wbuf", v((2, 3, width, width), BF))
    n.add("ctxb", v((4, qk, rows), BF))
    n.add("gctx", v((4, qk, rows), BF))
    n.add("cotb", v((rows, width), BF))
    n.add("outb", v((rows, width), BF))
    n.add("gm", v((rows, width), F32))
    n.add("gfar", v((size, width), BF))
    n.add("ggot", v((size, width), BF))
    n.add("dkvr", v((4, 2 * qk, rows), BF))
    levels = 3 + (na - 1).bit_length()
    n.add("smine", v((levels, SMALL_ROWS, width), F32))
    n.add("sgot", v((levels, SMALL_ROWS, width), F32))
    n.add("ld", dma(11))
    n.add("cl", dma(1))
    n.add("wl", dma(2))
    n.add("rown", dma(units))
    n.pair("co", nm, 2)
    n.pair("ct", 1)
    n.pair("ou", 1)
    n.pair("gt", 1)
    n.pair("dk", 4)
    n.pair("sm", levels)
    n.pair("ry", units)
    n.pair("rx", units, na)
    n.pair("rz", units, na - 1)
    n.pair("rgz", units, na - 1)
    n.pair("rgx", units, na)
    shape = jax.ShapeDtypeStruct
    return pl.pallas_call(
        partial(leave_kernel, ndp, LEAVE_IN + LEAVE_OUT + n.names, split),
        in_specs=[ANY, ANY, ANY, ANY, VMEM, ANY, VMEM, VMEM, ANY, SMEM, SMEM],
        out_specs=[ANY, VMEM, ANY, ANY, ANY],
        out_shape=[
            shape((nm, padded, width), BF),
            shape((SMALL_ROWS, width), F32),
            shape(cot.shape, BF),
            shape(cot.shape, F32),
            shape((nm, 2, width, width), BF),
        ],
        scratch_shapes=n.shapes,
        compiler_params=pltpu.CompilerParams(
            collective_id=1, has_side_effects=True, vmem_limit_bytes=VMEM_LIMIT
        ),
    )(*inputs)


def per_device(
    tokens,
    type_ids,
    boundary,
    token_type_rows,
    query_key_value_weight,
    b_qv,
    output_weight,
    b_out,
    gain_one,
    shift_one,
    gate_up_weight,
    gate_up_bias,
    down_weight,
    b_down,
    gain_two,
    shift_two,
    cotangent,
):
    nt = lax.axis_size("tensor")
    ndp = lax.axis_size("dp")
    t = lax.axis_index("tensor")
    y = t // 2
    width = tokens.shape[2]
    qk = query_key_value_weight.shape[2]
    heads_dev = qk // HEAD_DIM
    attn = jnp.concatenate(
        [query_key_value_weight.transpose(1, 2, 0).reshape(3 * qk, width), output_weight], axis=0
    )
    w4 = jnp.stack([attn, gate_up_weight[:, 0], gate_up_weight[:, 1], down_weight])
    zeros = jnp.zeros((qk,), F32)
    bias = jnp.stack([jnp.concatenate([b_qv[0], zeros, b_qv[1], zeros]), gate_up_bias[0], gate_up_bias[1]])
    bias = jnp.pad(bias, ((0, 5), (0, 0)))
    vecs = jnp.stack([b_out, gain_one, shift_one, b_down, gain_two, shift_two, b_down, b_down])
    pair = lax.dynamic_index_in_dim(type_ids, y, 0, keepdims=False)
    bound = lax.dynamic_index_in_dim(boundary, y, 0, keepdims=False)
    kinds = jnp.stack([pair[0], pair[1], bound])
    head_ids = jnp.concatenate([(t ^ s) * heads_dev + jnp.arange(heads_dev) for s in range(nt)])
    slopes = jnp.exp2(-8.0 * (head_ids + 1).astype(F32) / HEADS)

    first = enter_layer(ndp, tokens, w4, bias, token_type_rows, kinds, slopes)
    fin, sums, out, gtok, _ = leave_layer(ndp, (*first, vecs, cotangent, kinds, slopes), cotangent)
    fin = fin[:, :width].astype(F32)
    g_qkv = fin[ATTN, : 3 * qk].T.reshape(query_key_value_weight.shape)
    g_gu = jnp.stack([fin[GATE], fin[UP]], axis=1)
    g_bgu = lax.dynamic_slice_in_dim(sums, ROW_GU + 2 * t, 2, 0)
    g_bqv = lax.dynamic_index_in_dim(sums, ROW_QV + t, 0, keepdims=False)
    g_bqv = jnp.stack([g_bqv[:qk], g_bqv[2 * qk : 3 * qk]])
    return (
        out,
        gtok,
        sums[:2],
        g_qkv,
        g_bqv,
        fin[ATTN, 3 * qk :],
        sums[2],
        sums[3],
        sums[4],
        g_gu,
        g_bgu,
        fin[DOWN].T,
        sums[5],
        sums[6],
        sums[7],
    )


def solution(mesh):
    in_specs = (
        P("dp", "tensor", None),
        P("dp", None),
        P("dp"),
        P(),
        P(None, None, "tensor"),
        P(None, "tensor"),
        P("tensor", None),
        P(),
        P(),
        P(),
        P(None, None, "tensor"),
        P(None, "tensor"),
        P("tensor", None),
        P(),
        P(),
        P(),
        P("dp", "tensor", None),
    )
    out_specs = (
        P("dp", "tensor", None),
        P("dp", "tensor", None),
        P(),
        P(None, None, "tensor"),
        P(None, "tensor"),
        P("tensor", None),
        P(),
        P(),
        P(),
        P(None, None, "tensor"),
        P(None, "tensor"),
        P("tensor", None),
        P(),
        P(),
        P(),
    )
    return jax.shard_map(
        per_device, mesh=mesh, in_specs=in_specs, out_specs=out_specs, check_vma=False
    )
```

```python
from functools import partial

import jax
import jax.numpy as jnp
from jax import lax
from jax.experimental import pallas as pl
from jax.experimental.pallas import tpu as pltpu
from jax.sharding import PartitionSpec as P

HEADS = 12
HEAD_DIM = 64
EPSILON = 1e-05
VMEM_LIMIT = 255 * 2**18
MESH = pl.DeviceIdType.MESH
BF = jnp.bfloat16
F32 = jnp.float32
NT = (((1,), (1,)), ((), ()))
TN = (((0,), (0,)), ((), ()))
NN = (((1,), (0,)), ((), ()))
DIRECT = (3,)


def dot(a, b, dims=NN):
    return lax.dot_general(a, b, dims, preferred_element_type=F32)


def remote(src, dst, send, recv, to):
    return pltpu.make_async_remote_copy(
        src_ref=src, dst_ref=dst, send_sem=send, recv_sem=recv, device_id=to, device_id_type=MESH
    )


def local(src, dst, sem):
    return pltpu.make_async_copy(src, dst, sem)


def dma(*shape):
    return pltpu.SemaphoreType.DMA(shape)


def chunk_rows(ndp, rows):
    return -(-rows // (16 * ndp)) * 16


class Links:
    def __init__(self, ndp):
        self.ndp = ndp
        self.na = ndp // 2
        self.dp = lax.axis_index("dp")
        self.t = lax.axis_index("tensor")
        self.a = self.dp // 2
        self.b = lax.rem(self.dp, 2)
        self.y = self.t // 2
        self.c = lax.rem(self.t, 2)
        self.core = (self.dp, 2 * self.y + 1 - self.c)
        self.far = (self.dp, 2 * (1 - self.y) + self.c)
        self.cross = (self.dp, 2 * (1 - self.y) + 1 - self.c)
        self.pair = (2 * self.a + 1 - self.b, self.t)

    def up(self, off):
        return lax.rem(self.a + off, self.na)

    def down(self, off):
        return lax.rem(self.a + self.na - off, self.na)

    def column(self, off):
        return (2 * self.up(off) + self.b, self.t)

    def quarter(self, s):
        return 2 * lax.rem(self.y + s // 2, 2) + lax.rem(self.c + s % 2, 2)

    def greet(self):
        barrier = pltpu.get_barrier_semaphore()
        others = [self.core, self.far, self.cross, self.pair]
        others += [self.column(o) for o in range(1, self.na)]
        for other in others:
            pl.semaphore_signal(barrier, inc=1, device_id=other, device_id_type=MESH)
        pl.semaphore_wait(barrier, len(others))


class Gather:
    def __init__(self, links, own, place, sems, rows):
        self.l, self.own, self.place, self.s = links, own, place, sems
        self.cr = rows // links.ndp
        self.fits = rows % (16 * links.ndp) == 0

    def relayed(self, m):
        return self.fits and m not in DIRECT

    def share(self, ref, d):
        return ref.at[pl.ds(pl.multiple_of(d * self.cr, 16), self.cr)]

    def pair_of(self, name, m, i=None):
        s, r = self.s[name]
        return (s.at[m], r.at[m]) if i is None else (s.at[m, i], r.at[m, i])

    def core(self, m):
        return remote(self.own(m), self.place(m, 1), *self.pair_of("c", m), self.l.core)

    def core_far(self, m):
        return remote(self.place(m, 2), self.place(m, 3), *self.pair_of("cf", m), self.l.core)

    def over_y(self, m):
        src, dst = self.own(m), self.place(m, 2)
        if self.relayed(m):
            src, dst = self.share(src, self.l.dp), self.share(dst, self.l.dp)
        return remote(src, dst, *self.pair_of("y", m), self.l.far)

    def over_x(self, m, off):
        at = self.share(self.place(m, 2), 2 * self.l.down(off) + self.l.b)
        return remote(at, at, *self.pair_of("x", m, off), self.l.pair)

    def over_z(self, m, off):
        at = self.share(self.place(m, 2), self.l.dp)
        return remote(at, at, *self.pair_of("z", m, off - 1), self.l.column(off))

    def step_spread(self, m):
        if self.relayed(m):
            self.over_y(m).wait_recv()
            self.over_x(m, 0).start()
            for off in range(1, self.l.na):
                self.over_z(m, off).start()

    def step_on(self, m):
        if self.relayed(m):
            for off in range(1, self.l.na):
                self.over_z(m, off).wait_recv()
                self.over_x(m, off).start()

    def step_core(self, m):
        if self.relayed(m):
            for off in range(self.l.na):
                self.over_x(m, off).wait_recv()
        else:
            self.over_y(m).wait_recv()
        self.core_far(m).start()

    def finish(self, m):
        self.core(m).wait_send()
        self.over_y(m).wait_send()
        self.core_far(m).wait_send()
        if self.relayed(m):
            for off in range(self.l.na):
                self.over_x(m, off).wait_send()
            for off in range(1, self.l.na):
                self.over_z(m, off).wait_send()


class Reducer:
    def __init__(self, links, refs, sems):
        self.l = links
        self.near, self.far, self.ybuf, self.xbuf, self.zbuf, self.own, self.fin = refs
        self.s = sems
        self.split = self.near.shape[1]
        self.cr = self.near.shape[4]
        self.rows = self.far.shape[2]
        self.units = self.near.shape[0] * self.split

    def block(self, u):
        return u // self.split, u % self.split

    def shares(self, first, count):
        for row in range(first, first + count, self.cr):
            j, inside = row // self.rows, row % self.rows // self.cr
            yield j, inside // 2, inside % 2, row

    def put_near(self, k, first, value):
        for j, i, b, row in self.shares(first, value.shape[0]):
            self.near[k, j, i, b] = value[row - first : row - first + self.cr].astype(BF)

    def put_far(self, k, first, value):
        for row in range(first, first + value.shape[0], self.cr):
            at = pl.ds(row % self.rows, self.cr)
            self.far[k, row // self.rows, at] = value[row - first : row - first + self.cr].astype(BF)

    def clear_padding(self):
        for i in range(self.rows // self.cr // 2, self.l.na):
            self.near[:, :, i] = jnp.zeros_like(self.near[:, :, i])

    def copy_y(self, u):
        s, r = self.s["y"]
        return remote(self.far.at[self.block(u)], self.ybuf.at[self.block(u)], s.at[u], r.at[u], self.l.far)

    def copy_x(self, u):
        s, r = self.s["x"]
        k, j = self.block(u)
        return remote(self.near.at[k, j, :, 1 - self.l.b], self.xbuf.at[u], s.at[u], r.at[u], self.l.pair)

    def copy_z(self, u, off):
        s, r = self.s["z"]
        k, j = self.block(u)
        src = self.near.at[k, j, self.l.up(off), self.l.b]
        return remote(src, self.zbuf.at[u, off - 1], s.at[u, off - 1], r.at[u, off - 1], self.l.column(off))

    def place(self, u):
        k, j = self.block(u)
        return self.fin.at[k, j, self.l.a, self.l.b]

    def copy_gz(self, u, off):
        s, r = self.s["gz"]
        return remote(self.own.at[u], self.place(u), s.at[u, off - 1], r.at[u, off - 1], self.l.column(off))

    def copy_gx(self, u):
        s, r = self.s["gx"]
        k, j = self.block(u)
        at = self.fin.at[k, j, :, self.l.b]
        return remote(at, at, s.at[u], r.at[u], self.l.pair)

    def copy_own(self, u):
        return local(self.own.at[u], self.place(u), self.s["own"].at[u])

    def start_y(self, u):
        self.copy_y(u).start()

    def step_x(self, u):
        self.copy_y(u).wait_recv()
        k, j = self.block(u)
        for row in range(0, self.rows, self.cr):
            i = row // self.cr
            share = self.near.at[k, j, i // 2, i % 2]
            share[...] = (share[...].astype(F32) + self.ybuf[k, j, row : row + self.cr].astype(F32)).astype(BF)
        self.copy_x(u).start()

    def step_z(self, u):
        self.copy_x(u).wait_recv()
        k, j = self.block(u)
        for i in range(self.l.na):
            share = self.near.at[k, j, i, self.l.b]
            share[...] = (share[...].astype(F32) + self.xbuf[u, i].astype(F32)).astype(BF)
        for off in range(1, self.l.na):
            self.copy_z(u, off).start()

    def step_own(self, u):
        k, j = self.block(u)
        total = self.near[k, j, self.l.a, self.l.b].astype(F32)
        for off in range(1, self.l.na):
            self.copy_z(u, off).wait_recv()
            total = total + self.zbuf[u, off - 1].astype(F32)
        self.own[u] = total.astype(BF)
        for off in range(1, self.l.na):
            self.copy_gz(u, off).start()
        self.copy_own(u).start()

    def step_on(self, u):
        self.copy_own(u).wait()
        for off in range(1, self.l.na):
            self.copy_gz(u, off).wait_recv()
        self.copy_gx(u).start()

    def finish(self, u):
        self.copy_y(u).wait_send()
        self.copy_x(u).wait_send()
        for off in range(1, self.l.na):
            self.copy_z(u, off).wait_send()
            self.copy_gz(u, off).wait_send()
        self.copy_gx(u).wait()


class SmallSum:
    def __init__(self, links, mine, got, sems):
        self.l, self.mine, self.got = links, mine, got
        self.ss, self.rs = sems
        self.levels = got.shape[0]

    def partner(self, i):
        if i < 3:
            return (self.l.core, self.l.far, self.l.pair)[i]
        step = 2 ** (i - 3)
        a = self.l.a + step - 2 * step * lax.rem(self.l.a // step, 2)
        return (2 * a + self.l.b, self.l.t)

    def swap(self, i):
        return remote(self.mine.at[i], self.got.at[i], self.ss.at[i], self.rs.at[i], self.partner(i))

    def start(self, i):
        self.swap(i).start()

    def add(self, i):
        self.swap(i).wait_recv()
        total = self.mine[i] + self.got[i]
        if i + 1 < self.levels:
            self.mine[i + 1] = total
            self.start(i + 1)
        return total

    def finish(self):
        for i in range(self.levels):
            self.swap(i).wait_send()


def positions(links, size):
    y, c = links.y, links.c
    return [(2 * y + c) * size, (2 * (1 - y) + c) * size, (2 * y + 1 - c) * size, (2 * (1 - y) + 1 - c) * size]


def fill_distance(firsts, size, dist_ref):
    for kb, key in enumerate(firsts):
        for qb, query in enumerate(firsts[:2]):
            row = lax.broadcasted_iota(jnp.int32, (size, size), 0) + key
            col = lax.broadcasted_iota(jnp.int32, (size, size), 1) + query
            dist_ref[kb * size : (kb + 1) * size, qb * size : (qb + 1) * size] = jnp.abs(row - col).astype(F32)


def second_segment(links, size, r, block):
    y = links.y
    place = lax.broadcasted_iota(jnp.int32, (size, 1), 0) + positions(links, size)[block]
    return jnp.where(place >= r.boundary[y], r.type_ids[y, 1], r.type_ids[y, 0]) == 1


def mean(a):
    return jnp.mean(a, axis=-1, keepdims=True)


def norm_forward(values):
    centered = values - mean(values)
    scale = lax.rsqrt(mean(centered * centered) + EPSILON)
    return centered * scale, scale


def norm_backward(grad, unit, scale, gain):
    n = grad * gain
    return scale * (n - mean(n) - unit * mean(n * unit))


def gelu_parts(gate):
    e = jnp.exp(gate * gate * -0.5)
    t = 1.0 / (1.0 + jnp.abs(gate) * (0.3275911 * 0.5**0.5))
    poly = t * (
        0.5 * 0.254829592
        + t * (0.5 * -0.284496736 + t * (0.5 * 1.421413741 + t * (0.5 * -1.453152027 + t * (0.5 * 1.061405429))))
    )
    tail = poly * e
    return jnp.where(gate < 0, tail, 1.0 - tail), e * 0.3989422804014327


class Names:
    def __init__(self):
        self.names, self.shapes = [], []

    def add(self, name, shape):
        self.names.append(name)
        self.shapes.append(shape)

    def pair(self, name, *shape):
        self.add(name + "_s", dma(*shape))
        self.add(name + "_r", dma(*shape))


ANY = pl.BlockSpec(memory_space=pl.ANY)
VMEM = pl.BlockSpec(memory_space=pltpu.VMEM)
SMEM = pl.BlockSpec(memory_space=pltpu.SMEM)


class Refs:
    def __init__(self, names, refs):
        self.__dict__.update(zip(names, refs))

    def sems(self, name):
        return getattr(self, name + "_s"), getattr(self, name + "_r")


ENTER_IN = ["tokens", "wqkv", "wout", "wgu", "wdown", "b_qv", "b_gu", "table", "type_ids", "boundary", "slopes"]
ENTER_OUT = ["x", "qkv", "kvp", "ctx", "lse", "wall", "biases"]
MATRICES = 4


def enter_kernel(ndp, names, *refs):
    r = Refs(names, refs)
    l = Links(ndp)
    nm, width = MATRICES, r.wdown.shape[1]
    size = r.tokens.shape[1]
    rows = 2 * size
    heads_dev = HEADS // 4
    qk = heads_dev * HEAD_DIM
    firsts = positions(l, size)

    def place(m, s):
        return r.wa.at[s] if m == 0 else r.wall.at[m, s]

    def own(m):
        return (r.wa.at[0], r.gu.at[0], r.gu.at[1], r.wdown)[m]

    g = Gather(l, own, place, {n: r.sems("g" + n) for n in ("c", "cf", "y", "x", "z")}, width)
    tok_own = local(r.tokens.at[l.y], r.tok.at[pl.ds(0, size)], r.ld.at[0])
    wa_own = [
        local(r.wqkv, r.wa.at[0, pl.ds(0, 3 * qk)], r.ld.at[1]),
        local(r.wout, r.wa.at[0, pl.ds(3 * qk, qk)], r.ld.at[2]),
    ]
    gu_own = local(r.wgu, r.graw, r.ld.at[3])
    for c in (*wa_own, tok_own, gu_own):
        c.start()
    tok_far = remote(r.tokens.at[1 - l.y], r.tok.at[pl.ds(size, size)], *(a.at[0] for a in r.sems("tk")), l.far)
    bias_to = [
        remote(r.biases.at[0], r.biases.at[s], *(a.at[s] for a in r.sems("bi")), to)
        for s, to in ((1, l.core), (2, l.far), (3, l.cross))
    ]

    def kv_send(s):
        other = s + 1 - 2 * (s % 2)
        src = r.qkvb.at[s, pl.ds(qk, 2 * qk)]
        return remote(src, r.kvb.at[other], *(a.at[s] for a in r.sems("kv")), l.core)

    def kv_wait(s):
        other = s + 1 - 2 * (s % 2)
        src = r.qkvb.at[other, pl.ds(qk, 2 * qk)]
        return remote(src, r.kvb.at[s], *(a.at[other] for a in r.sems("kv")), l.core)

    r.biases[0] = jnp.zeros_like(r.biases[0])
    r.biases[0, 0:1, :qk] = r.b_qv[0:1]
    r.biases[0, 0:1, 2 * qk : 3 * qk] = r.b_qv[1:2]
    r.biases[0, 1:3, :] = r.b_gu[...]
    l.greet()
    for c in wa_own:
        c.wait()
    g.over_y(0).start()
    g.core(0).start()
    for b in bias_to:
        b.start()
    tok_far.start()

    def enter(block):
        at = pl.ds(block * size, size)
        second = second_segment(l, size, r, block)
        x = r.tok[at].astype(F32) + jnp.where(second, r.table[1:2], r.table[0:1])
        r.xb[at] = x
        r.xl[at] = x.astype(BF)

    def project(s, block):
        at = slice(block * size, (block + 1) * size)
        column = r.biases[s].T[: 3 * qk, 0:1]
        part = dot(r.wa[s, : 3 * qk], r.xl[at], NT) + column
        r.qkvb[s, :, at] = part.astype(BF)

    tok_own.wait()
    enter(0)
    project(0, 0)
    for b in bias_to:
        b.wait_recv()
    g.core(0).wait_recv()
    project(1, 0)
    g.step_spread(0)
    gu_own.wait()
    for i in range(2):
        r.gu[i] = r.graw[:, i, :]
    gu_out = local(r.gu, r.wall.at[pl.ds(1, 2), 0], r.ld.at[4])
    gu_out.start()
    fill_distance(firsts, size, r.dist)
    tok_far.wait_recv()
    for m in (1, 2):
        g.over_y(m).start()
    enter(1)
    x_out = local(r.xb, r.x, r.ld.at[5])
    x_out.start()
    for s in (0, 1):
        project(s, 1)
        kv_send(s).start()
    g.step_on(0)
    for m in range(1, nm):
        g.core(m).start()

    def head(ticks, h, carry):
        s, j = h // heads_dev, h % heads_dev

        @pl.when(j == 0)
        def _():
            kv_wait(s).wait_recv()

        def lines(ref, first):
            return ref[s, pl.ds(pl.multiple_of(first + j * HEAD_DIM, HEAD_DIM), HEAD_DIM), :]

        q = lines(r.qkvb, 0) * BF(HEAD_DIM**-0.5)
        slope = r.slopes[l.quarter(s) * heads_dev + j]
        scores = [
            dot(key, q, TN) - slope * r.dist[i * rows : (i + 1) * rows]
            for i, key in enumerate((lines(r.qkvb, qk), lines(r.kvb, 0)))
        ]
        top = jnp.maximum(*(jnp.max(a, axis=0, keepdims=True) for a in scores))
        probs = [jnp.exp(a - top) for a in scores]
        total = sum(jnp.sum(a, axis=0, keepdims=True) for a in probs)
        values = (lines(r.qkvb, 2 * qk), lines(r.kvb, qk))
        out = sum(dot(v, p.astype(BF)) for v, p in zip(values, probs))
        r.ctxb[s, pl.ds(pl.multiple_of(j * HEAD_DIM, HEAD_DIM), HEAD_DIM), :] = (out * (1.0 / total)).astype(BF)
        r.lse[pl.ds(h, 1), :] = top + jnp.log(total)
        for at, steps in ticks.items():

            @pl.when(h == at)
            def _(steps=steps):
                for step in steps:
                    step()

        return carry

    def whole_down():
        g.over_y(3).start()

    lax.fori_loop(
        0,
        HEADS // 2,
        partial(
            head,
            {
                1: [partial(g.step_spread, 1), partial(g.step_spread, 2), whole_down],
                4: [partial(g.step_core, 0)],
            },
        ),
        0,
    )
    g.core_far(0).wait_recv()
    for s in (2, 3):
        for block in range(2):
            project(s, block)
        kv_send(s).start()
    wa_out = local(r.wa, r.wall.at[0], r.ld.at[6])
    wa_out.start()
    g.step_on(1)
    lax.fori_loop(
        HEADS // 2,
        HEADS,
        partial(head, {8: [partial(g.step_on, 2)], 10: [partial(g.step_core, 1)]}),
        0,
    )
    outs = [
        local(r.qkvb, r.qkv, r.ld.at[7]),
        local(r.kvb, r.kvp, r.ld.at[8]),
        local(r.ctxb, r.ctx, r.ld.at[9]),
    ]
    for o in outs:
        o.start()
    for m in (2, 3):
        g.step_core(m)
    for m in range(1, nm):
        g.core(m).wait_recv()
        g.core_far(m).wait_recv()
    for m in range(nm):
        g.finish(m)
    for s in range(4):
        kv_send(s).wait_send()
    tok_far.wait_send()
    for b in bias_to:
        b.wait_send()
    for o in outs + [gu_out, x_out, wa_out]:
        o.wait()


def enter_layer(ndp, inputs):
    tokens, width = inputs[0], inputs[0].shape[2]
    size = tokens.shape[1]
    rows = 2 * size
    qk = HEADS // 4 * HEAD_DIM
    na = ndp // 2
    nm = MATRICES
    n = Names()
    n.add("wa", pltpu.VMEM((4, width, width), BF))
    n.add("graw", pltpu.VMEM((width, 2, width), BF))
    n.add("gu", pltpu.VMEM((2, width, width), BF))
    n.add("tok", pltpu.VMEM((rows, width), BF))
    n.add("xb", pltpu.VMEM((rows, width), F32))
    n.add("xl", pltpu.VMEM((rows, width), BF))
    n.add("qkvb", pltpu.VMEM((4, 3 * qk, rows), BF))
    n.add("kvb", pltpu.VMEM((4, 2 * qk, rows), BF))
    n.add("ctxb", pltpu.VMEM((4, qk, rows), BF))
    n.add("dist", pltpu.VMEM((2 * rows, rows), F32))
    n.add("ld", dma(10))
    n.pair("tk", 1)
    n.pair("bi", 4)
    n.pair("kv", 4)
    n.pair("gc", nm)
    n.pair("gcf", nm)
    n.pair("gy", nm)
    n.pair("gx", nm, na)
    n.pair("gz", nm, na - 1)
    shape = jax.ShapeDtypeStruct
    return pl.pallas_call(
        partial(enter_kernel, ndp, ENTER_IN + ENTER_OUT + n.names),
        in_specs=[ANY, ANY, ANY, ANY, ANY, VMEM, VMEM, VMEM, SMEM, SMEM, SMEM],
        out_specs=[ANY, ANY, ANY, ANY, VMEM, ANY, VMEM],
        out_shape=[
            shape((rows, width), F32),
            shape((4, 3 * qk, rows), BF),
            shape((4, 2 * qk, rows), BF),
            shape((4, qk, rows), BF),
            shape((HEADS, rows), F32),
            shape((nm, 4, width, width), BF),
            shape((4, 8, width), F32),
        ],
        scratch_shapes=n.shapes,
        compiler_params=pltpu.CompilerParams(
            collective_id=0, has_side_effects=True, vmem_limit_bytes=VMEM_LIMIT
        ),
    )(*inputs)


LEAVE_IN = ["x", "qkv", "kvp", "ctx", "lse", "wall", "biases", "wdown"]
LEAVE_IN += ["b_out", "gain_one", "shift_one", "b_down", "gain_two", "shift_two"]
LEAVE_IN += ["cot", "type_ids", "boundary", "slopes"]
LEAVE_OUT = ["fin", "sums", "out", "gtok", "cbuf"]
DOWN, GATE, UP, ATTN = range(4)
ROW_GU, ROW_QV, SMALL_ROWS = 8, 16, 24


def leave_kernel(ndp, names, *refs):
    r = Refs(names, refs)
    l = Links(ndp)
    rows, width = r.x.shape
    size = rows // 2
    heads_dev = HEADS // 4
    qk = heads_dev * HEAD_DIM
    firsts = positions(l, size)
    stages = r.cstage.shape[0]
    red = Reducer(
        l,
        (r.near, r.far, r.ybuf, r.xbuf, r.zbuf, r.own, r.fin),
        {**{n: r.sems("r" + n) for n in ("y", "x", "z", "gz", "gx")}, "own": r.rown},
    )
    pump = Pump(red, schedule(red.units))
    small = SmallSum(l, r.smine, r.sgot, r.sems("sm"))
    sv = r.smine.at[0]

    def vec(ref):
        return ref[...].reshape(1, width)

    def core_copy(k, i):
        src = r.cstage.at[k % stages, i]
        return remote(src, r.cbuf.at[k, i], *(a.at[k, i] for a in r.sems("co")), l.core)

    def fetch(k, i):
        slot = (1 - i, 0, 1, 1 - i)[k]
        return local(r.cbuf.at[k, i], r.cload.at[slot], r.cl.at[slot])

    def room(k, i):
        if k >= stages:
            core_copy(k - stages, i).wait_send()

    def start_fetch(k, i):
        core_copy(k, i).wait_recv()
        fetch(k, i).start()

    def merge(k, i, first, value):
        slot = (1 - i, 0, 1, 1 - i)[k]
        total = value + r.cload[slot, pl.ds(first, value.shape[0])].astype(F32)
        (red.put_near, red.put_far)[i](k, first, total)

    def load_weights(s, buf):
        return local(r.wall.at[pl.ds(1, 3), s], r.wbuf.at[buf], r.wl.at[buf])

    def start_weights(s, buf):
        if s:
            load_weights(s, buf).start()
        else:
            local(r.wall.at[pl.ds(1, 2), 0], r.wbuf.at[buf, pl.ds(0, 2)], r.wl.at[buf]).start()
            local(r.wdown, r.wbuf.at[buf, 2], r.wl.at[buf]).start()

    out_own = local(r.outb.at[pl.ds(0, size)], r.out.at[l.y], r.ld.at[8])
    out_far = remote(r.outb.at[pl.ds(size, size)], r.out.at[l.y], *(a.at[0] for a in r.sems("ou")), l.far)
    cot_own = local(r.cot.at[l.y], r.cotb.at[pl.ds(0, size)], r.ld.at[0])
    cot_far = remote(r.cot.at[1 - l.y], r.cotb.at[pl.ds(size, size)], *(a.at[0] for a in r.sems("ct")), l.far)

    def order(i):
        return 2 * (i % 2) + i // 2

    def ffn_phase(wo, gh, a_ref, b_ref, hid, unit, hl, ht, r1):
        xb, acc, gf = gh, r.gm, hl
        lx = local(r.x, xb, r.ld.at[1])
        lo = local(r.wall.at[0, pl.ds(0, 4), pl.ds(3 * qk, qk)], wo, r.ld.at[2])
        lc = local(r.ctx, r.ctxb, r.ld.at[3])
        for c in (lc, lo, lx, cot_own):
            c.start()
        start_weights(0, 0)
        start_weights(2, 1)
        l.greet()
        cot_far.start()
        red.clear_padding()
        sv[...] = jnp.zeros_like(sv)
        lc.wait()
        lo.wait()
        lx.wait()
        for s in range(4):
            part = dot(r.ctxb[s], wo[s], TN)
            if s == 0:
                acc[...] = part + xb[...] + vec(r.b_out)
            else:
                acc[...] += part
        u1, s1 = norm_forward(acc[...])
        unit[...] = u1
        r1[...] = s1
        h1 = u1 * vec(r.gain_one) + vec(r.shift_one)
        acc[...] = h1 + vec(r.b_down)
        hl[...] = h1.astype(BF)
        ht[...] = h1.T.astype(BF)

        def forward(i, carry):
            s, buf = order(i), i % 2
            load_weights(s, buf).wait()
            for half in range(2):
                at = slice(half * size, (half + 1) * size)
                gate = dot(hl[at], r.wbuf[buf, 0]) + r.biases[s, 1:2, :]
                up = dot(hl[at], r.wbuf[buf, 1]) + r.biases[s, 2:3, :]
                cdf, pdf = gelu_parts(gate)
                act = gate * cdf
                a_ref[s, at] = act.astype(BF)
                b_ref[s, at] = (up * (cdf + gate * pdf)).astype(BF)
                hidden = (act * up).astype(BF)
                hid[s, at] = hidden
                acc[at] += dot(hidden, r.wbuf[buf, 2])

            @pl.when(i < 2)
            def _():
                load_weights(order(i + 2), buf).start()

            return carry

        lax.fori_loop(0, 4, forward, 0)
        u2, s2 = norm_forward(acc[...])
        out = u2 * vec(r.gain_two) + vec(r.shift_two)
        r.outb[...] = out.astype(BF)
        cot_own.wait()
        cot_far.wait_recv()
        cot = r.cotb[...].astype(F32)
        g2 = norm_backward(cot, u2, s2, vec(r.gain_two))
        sv[6:7, :] = jnp.sum(cot * u2, axis=0, keepdims=True)
        sv[7:8, :] = jnp.sum(cot, axis=0, keepdims=True)
        sv[5:6, :] = jnp.sum(g2, axis=0, keepdims=True)
        gh[...] = g2
        gf[...] = g2.astype(BF)
        for i, s in ((1, 3), (0, 1)):
            r.cstage[DOWN % stages, i] = dot(hid[s], gf[...], TN).astype(BF)
            core_copy(DOWN, i).start()

        def backward(s, buf):
            load = None
            g_hidden = dot(gf[...], r.wbuf[buf, 2], NT)
            g_gate = (g_hidden * b_ref[s].astype(F32)).astype(BF)
            g_up = (g_hidden * a_ref[s].astype(F32)).astype(BF)
            row = ROW_GU + 2 * l.quarter(s)
            sv[pl.ds(row, 1), :] = jnp.sum(g_gate.astype(F32), axis=0, keepdims=True)
            sv[pl.ds(row + 1, 1), :] = jnp.sum(g_up.astype(F32), axis=0, keepdims=True)
            gh[...] += dot(g_gate, r.wbuf[buf, 0], NT)
            gh[...] += dot(g_up, r.wbuf[buf, 1], NT)
            return g_gate, g_up

        for i, s, buf in ((1, 3, 1), (0, 1, 0)):
            g_gate, g_up = backward(s, buf)
            start_weights(s - 1, buf)
            for k, g in ((GATE, g_gate), (UP, g_up)):
                room(k, i)
                r.cstage[k % stages, i] = dot(ht[...], g).astype(BF)
                core_copy(k, i).start()
            start_fetch(DOWN, i)
            value = dot(hid[s - 1], gf[...], TN)
            fetch(DOWN, i).wait()
            merge(DOWN, i, 0, value)
            if i == 1:
                for u in range(min(AHEAD, red.split)):
                    red.start_y(u)
        for i, s, buf in ((1, 2, 1), (0, 0, 0)):
            load_weights(s, buf).wait()
            for k in (GATE, UP):
                start_fetch(k, i)
            g_gate, g_up = backward(s, buf)
            for k, g in ((GATE, g_gate), (UP, g_up)):
                value = dot(ht[...], g)
                fetch(k, i).wait()
                merge(k, i, 0, value)
            pump.until(POINTS[1 - i])
        g_h1 = gh[...]
        unit_one = unit[...]
        sv[3:4, :] = jnp.sum(g_h1 * unit_one, axis=0, keepdims=True)
        sv[4:5, :] = jnp.sum(g_h1, axis=0, keepdims=True)
        gm = norm_backward(g_h1, unit_one, r1[...], vec(r.gain_one))
        sv[2:3, :] = jnp.sum(gm, axis=0, keepdims=True)
        r.gm[...] = gm
        ga = gm.astype(BF)
        r.cotb[...] = ga
        for s in range(4):
            r.gctx[s] = dot(wo[s], ga, NT).astype(BF)

    v = pltpu.VMEM
    pl.run_scoped(
        ffn_phase,
        v((4, qk, width), BF),
        v((rows, width), F32),
        v((4, rows, width), BF),
        v((4, rows, width), BF),
        v((4, rows, width), BF),
        v((rows, width), F32),
        v((rows, width), BF),
        v((width, rows), BF),
        v((rows, 1), F32),
    )

    def attention_phase(wq, qkvb, kvb, xb, xl, dist, dqkv, dkvo, dkvs):
        lq = local(r.qkv, qkvb, r.ld.at[4])
        lk = local(r.kvp, kvb, r.ld.at[5])
        lw = local(r.wall.at[0, pl.ds(0, 4), pl.ds(0, 3 * qk)], wq, r.ld.at[6])
        lx = local(r.x, xb, r.ld.at[7])
        lq.start()
        lk.start()
        fill_distance(firsts, size, dist)

        def other(s):
            return s + 1 - 2 * (s % 2)

        def send(s):
            return remote(dkvs.at[s], r.dkvr.at[other(s)], *(a.at[s] for a in r.sems("dk")), l.core)

        def arrived(s):
            return remote(dkvs.at[other(s)], r.dkvr.at[s], *(a.at[other(s)] for a in r.sems("dk")), l.core)

        lq.wait()
        lk.wait()

        def head(h, carry):
            s, j = h // heads_dev, h % heads_dev

            def span(first):
                return pl.ds(pl.multiple_of(first + j * HEAD_DIM, HEAD_DIM), HEAD_DIM)

            qt = qkvb[s, span(0), :] * BF(HEAD_DIM**-0.5)
            q = qt.T
            dot_t = r.gctx[s, span(0), :]
            do = dot_t.T
            slope = r.slopes[l.quarter(s) * heads_dev + j]
            lse = r.lse[pl.ds(h, 1), :]
            keys = (qkvb[s, span(qk), :], kvb[s, span(0), :])
            values = (qkvb[s, span(2 * qk), :], kvb[s, span(qk), :])
            probs = [
                jnp.exp(dot(key, qt, TN) - slope * dist[i * rows : (i + 1) * rows] - lse)
                for i, key in enumerate(keys)
            ]
            g_probs = [dot(value, dot_t, TN) for value in values]
            inner = sum(jnp.sum(p * g, axis=0, keepdims=True) for p, g in zip(probs, g_probs))
            g_scores = [(p * (g - inner)).astype(BF) for p, g in zip(probs, g_probs)]
            dq = sum(dot(key, g) for key, g in zip(keys, g_scores))
            dqkv[s, span(0), :] = (dq * HEAD_DIM**-0.5).astype(BF)
            dk = [dot(g, q).T for g in g_scores]
            dv = [dot(p.astype(BF), do).T for p in probs]
            dkvo[s, span(0), :] = dk[0]
            dkvo[s, span(qk), :] = dv[0]
            dkvs[s, span(0), :] = dk[1].astype(BF)
            dkvs[s, span(qk), :] = dv[1].astype(BF)

            @pl.when(j == heads_dev - 1)
            def _():
                send(s).start()

            @pl.when(h == 0)
            def _():
                lw.start()
                lx.start()

            for at in range(HEADS):
                if pump.due(HEAD_TIMES[0] + HEAD_TIMES[1] * (at + 1)):

                    @pl.when(h == at)
                    def _(at=at):
                        pump.until(HEAD_TIMES[0] + HEAD_TIMES[1] * (at + 1))

            return carry

        lax.fori_loop(0, HEADS, head, 0)
        lw.wait()
        lx.wait()
        xl[...] = xb[...].astype(BF)
        ones = jnp.ones((8, rows), BF)
        for s in range(4):
            arrived(s).wait_recv()
            dqkv[s, qk:, :] = (dkvo[s] + r.dkvr[s].astype(F32)).astype(BF)
            g = dqkv[s]
            sv[pl.ds(ROW_QV + l.quarter(s), 1), : 3 * qk] = dot(ones, g, NT)[0:1]
            r.gm[...] += dot(g, wq[s], TN)
        pump.until(POINTS[2])
        g_entered = r.gm[...]
        total = jnp.sum(g_entered, axis=0, keepdims=True)
        second = sum(
            jnp.sum(
                jnp.where(second_segment(l, size, r, i), g_entered[i * size : (i + 1) * size], 0.0),
                axis=0,
                keepdims=True,
            )
            for i in range(2)
        )
        sv[0:1, :] = total - second
        sv[1:2, :] = second
        small.start(0)

        def attn_parts(s):
            return ((0, dot(dqkv[s], xl[...])), (3 * qk, dot(r.ctxb[s], r.cotb[...])))

        for i, s in ((1, 3), (0, 1)):
            room(ATTN, i)
            for first, value in attn_parts(s):
                r.cstage[ATTN % stages, i, pl.ds(first, value.shape[0])] = value.astype(BF)
            core_copy(ATTN, i).start()
        pump.until(POINTS[3])
        for i, s in ((1, 2), (0, 0)):
            start_fetch(ATTN, i)
            parts = attn_parts(s)
            fetch(ATTN, i).wait()
            for first, value in parts:
                merge(ATTN, i, first, value)
        for s in range(4):
            send(s).wait_send()

    pl.run_scoped(
        attention_phase,
        v((4, 3 * qk, width), BF),
        v((4, 3 * qk, rows), BF),
        v((4, 2 * qk, rows), BF),
        v((rows, width), F32),
        v((rows, width), BF),
        v((2 * rows, rows), F32),
        v((4, 3 * qk, rows), BF),
        v((4, 2 * qk, rows), F32),
        v((4, 2 * qk, rows), BF),
    )

    tok_own = local(r.gm.at[pl.ds(0, size)], r.gtok.at[l.y], r.ld.at[9])
    r.cload[0, :size] = r.gm[size:].astype(BF)
    tok_far = remote(r.cload.at[0, pl.ds(0, size)], r.ggot, *(a.at[0] for a in r.sems("gt")), l.far)
    out_own.start()
    tok_own.start()
    pump.after_y = lambda: (out_far.start(), tok_far.start())
    for i in range(small.levels):
        total = small.add(i)
        pump.until(POINTS[3] + 12.0 * (i + 1))
    pump.until(None)
    r.sums[...] = total
    tok_far.wait_recv()
    r.gm[size:] = r.ggot[...].astype(F32)
    tok_got = local(r.gm.at[pl.ds(size, size)], r.gtok.at[1 - l.y], r.ld.at[10])
    tok_got.start()
    for u in range(red.units):
        red.finish(u)
    for k in range(4 - stages, 4):
        for i in range(2):
            core_copy(k, i).wait_send()
    small.finish()
    cot_far.wait_send()
    out_far.wait()
    tok_far.wait_send()
    for c in (out_own, tok_own, tok_got):
        c.wait()


AHEAD = 2
HEAD_TIMES = (32.4, 2.16)
POINTS = (19.2, 25.2, 58.8, 63.6)
READY = (7.2, 18.0, 19.2, 67.2)


def schedule(units):
    unit = 102.0 / units
    free = {"y": 0.0, "x": 0.0, "z": 0.0}
    waiting, order = [], []
    split = units // 4

    def use(link, at, cost):
        free[link] = max(free[link], at) + cost
        return free[link] + 2.5

    def start_y(u, at):
        waiting.append((use("y", max(at, READY[u // split]), unit), u, "step_x"))

    for u in range(min(AHEAD, units)):
        start_y(u, 0.0)
        if u >= split:
            order.append((READY[u // split], "start_y", u))
    now = 0.0
    while waiting:
        waiting.sort()
        at, u, step = waiting.pop(0)
        now = max(now, at)
        order.append((now, step, u))
        now += 0.5
        if step == "step_x":
            if u + AHEAD < units:
                order.append((max(now, READY[(u + AHEAD) // split]), "start_y", u + AHEAD))
                start_y(u + AHEAD, now)
            waiting.append((use("x", now, unit / 2), u, "step_z"))
        elif step == "step_z":
            waiting.append((use("z", now, unit / 2), u, "step_own"))
        elif step == "step_own":
            waiting.append((use("z", now, unit / 2), u, "step_on"))
        else:
            use("x", now, unit / 2)
    return sorted(order, key=lambda o: o[0])


class Pump:
    def __init__(self, red, order):
        self.red, self.order, self.after_y = red, list(order), None

    def due(self, time):
        return bool(self.order) and (time is None or self.order[0][0] <= time)

    def until(self, time):
        while self.due(time):
            _, step, u = self.order.pop(0)
            getattr(self.red, step)(u)
            if step == "step_x" and u == self.red.units - 1:
                self.after_y()


def leave_layer(ndp, inputs, cot):
    x, wall = inputs[0], inputs[5]
    rows, width = x.shape
    nm = wall.shape[0]
    size = rows // 2
    qk = HEADS // 4 * HEAD_DIM
    na = ndp // 2
    split = 3 if width % (48 * ndp) == 0 else 1
    stages = 2 if split > 1 else 1
    units = nm * split
    unit = width // split
    cr = chunk_rows(ndp, unit)
    n = Names()
    v = pltpu.VMEM
    n.add("near", v((nm, split, na, 2, cr, width), BF))
    n.add("far", v((nm, split, unit, width), BF))
    n.add("ybuf", v((nm, split, unit, width), BF))
    n.add("xbuf", v((units, na, cr, width), BF))
    n.add("zbuf", v((units, na - 1, cr, width), BF))
    n.add("own", v((units, cr, width), BF))
    n.add("cstage", v((stages, 2, width, width), BF))
    n.add("cload", v((2, width, width), BF))
    n.add("wbuf", v((2, 3, width, width), BF))
    n.add("ctxb", v((4, qk, rows), BF))
    n.add("gctx", v((4, qk, rows), BF))
    n.add("cotb", v((rows, width), BF))
    n.add("outb", v((rows, width), BF))
    n.add("gm", v((rows, width), F32))
    n.add("ggot", v((size, width), BF))
    n.add("dkvr", v((4, 2 * qk, rows), BF))
    levels = 3 + (na - 1).bit_length()
    n.add("smine", v((levels, SMALL_ROWS, width), F32))
    n.add("sgot", v((levels, SMALL_ROWS, width), F32))
    n.add("ld", dma(11))
    n.add("cl", dma(2))
    n.add("wl", dma(2))
    n.add("rown", dma(units))
    n.pair("co", nm, 2)
    n.pair("ct", 1)
    n.pair("ou", 1)
    n.pair("gt", 1)
    n.pair("dk", 4)
    n.pair("sm", levels)
    n.pair("ry", units)
    n.pair("rx", units)
    n.pair("rz", units, na - 1)
    n.pair("rgz", units, na - 1)
    n.pair("rgx", units)
    shape = jax.ShapeDtypeStruct
    fin, *others = pl.pallas_call(
        partial(leave_kernel, ndp, LEAVE_IN + LEAVE_OUT + n.names),
        in_specs=[ANY, ANY, ANY, ANY, VMEM, ANY, VMEM, ANY, *[VMEM] * 6, ANY, SMEM, SMEM, SMEM],
        out_specs=[ANY, VMEM, ANY, ANY, ANY],
        out_shape=[
            shape((nm, split, na, 2, cr, width), BF),
            shape((SMALL_ROWS, width), F32),
            shape(cot.shape, BF),
            shape(cot.shape, F32),
            shape((nm, 2, width, width), BF),
        ],
        scratch_shapes=n.shapes,
        compiler_params=pltpu.CompilerParams(
            collective_id=1, has_side_effects=True, vmem_limit_bytes=VMEM_LIMIT
        ),
    )(*inputs)
    return fin.reshape(nm, -1, width), *others


FINISH_IN = ["fin", "sums", "got", "gtok"]
FINISH_OUT = ["output", "g_tokens", "table", "g_qkv", "g_bqv", "g_out", "g_bout", "g_gain1", "g_shift1"]
FINISH_OUT += ["g_gu", "g_bgu", "g_down", "g_bdown", "g_gain2", "g_shift2"]
SUM_ROWS = {"g_bout": 2, "g_gain1": 3, "g_shift1": 4, "g_bdown": 5, "g_gain2": 6, "g_shift2": 7}


def finish_kernel(*refs):
    r = Refs(FINISH_IN + FINISH_OUT, refs)
    step, last = pl.program_id(0), pl.num_programs(0) - 1
    t = lax.axis_index("tensor")
    qk = r.g_out.shape[0]
    r.output[...] = r.got[...]
    r.g_tokens[...] = r.gtok[...]
    r.g_gu[:, 0, :] = r.fin[GATE].astype(F32)
    r.g_gu[:, 1, :] = r.fin[UP].astype(F32)
    r.g_down[...] = r.fin[DOWN].astype(F32)

    @pl.when(step < last)
    def _():
        r.g_qkv[...] = r.fin[ATTN].astype(F32)

    @pl.when(step == last)
    def _():
        r.g_out[...] = r.fin[ATTN].astype(F32)
        r.table[...] = r.sums[0:2, :]
        for name, row in SUM_ROWS.items():
            getattr(r, name)[...] = r.sums[row]

    for quarter in range(4):

        @pl.when((step == last) & (t == quarter))
        def _(quarter=quarter):
            first, row = ROW_GU + 2 * quarter, ROW_QV + quarter
            r.g_bgu[...] = r.sums[first : first + 2, :]
            r.g_bqv[0:1, :] = r.sums[row : row + 1, :qk]
            r.g_bqv[1:2, :] = r.sums[row : row + 1, 2 * qk : 3 * qk]


def finish_layer(fin, sums, out, gtok):
    nm, width = fin.shape[0], fin.shape[2]
    seqs, size = out.shape[:2]
    qk = width // 4
    shape = jax.ShapeDtypeStruct
    whole = lambda *dims: pl.BlockSpec(dims, lambda i: (0,) * len(dims))
    rows_of = lambda: pl.BlockSpec((seqs, size // 4, width), lambda i: (0, i, 0))
    vector = (whole(width), shape((width,), F32))
    outs = {
        "output": (rows_of(), shape(out.shape, out.dtype)),
        "g_tokens": (rows_of(), shape(gtok.shape, gtok.dtype)),
        "table": (whole(2, width), shape((2, width), F32)),
        "g_qkv": (pl.BlockSpec((qk, width), lambda i: (jnp.minimum(i, 2), 0)), shape((3 * qk, width), F32)),
        "g_bqv": (whole(2, qk), shape((2, qk), F32)),
        "g_out": (whole(qk, width), shape((qk, width), F32)),
        "g_gu": (pl.BlockSpec((qk, 2, width), lambda i: (i, 0, 0)), shape((width, 2, width), F32)),
        "g_bgu": (whole(2, width), shape((2, width), F32)),
        "g_down": (pl.BlockSpec((qk, width), lambda i: (i, 0)), shape((width, width), F32)),
        **{name: vector for name in SUM_ROWS},
    }
    return pl.pallas_call(
        finish_kernel,
        grid=(4,),
        in_specs=[
            pl.BlockSpec((nm, qk, width), lambda i: (0, i, 0)),
            whole(*sums.shape),
            rows_of(),
            rows_of(),
        ],
        out_specs=[outs[name][0] for name in FINISH_OUT],
        out_shape=[outs[name][1] for name in FINISH_OUT],
        compiler_params=pltpu.CompilerParams(vmem_limit_bytes=VMEM_LIMIT),
    )(fin, sums, out, gtok)


def per_device(
    tokens,
    type_ids,
    boundary,
    token_type_rows,
    query_key_value_weight,
    b_qv,
    output_weight,
    b_out,
    gain_one,
    shift_one,
    gate_up_weight,
    gate_up_bias,
    down_weight,
    b_down,
    gain_two,
    shift_two,
    cotangent,
):
    ndp = lax.axis_size("dp")
    width, three, qk = query_key_value_weight.shape
    wqkv = query_key_value_weight.transpose(1, 2, 0).reshape(three * qk, width)
    slopes = jnp.asarray([2.0 ** (-8.0 * (h + 1) / HEADS) for h in range(HEADS)], F32)
    first = enter_layer(
        ndp,
        (
            tokens,
            wqkv,
            output_weight,
            gate_up_weight,
            down_weight,
            b_qv,
            gate_up_bias,
            token_type_rows,
            type_ids,
            boundary,
            slopes,
        ),
    )
    vectors = (b_out, gain_one, shift_one, b_down, gain_two, shift_two)
    fin, sums, out, gtok, _ = leave_layer(
        ndp, (*first, down_weight, *vectors, cotangent, type_ids, boundary, slopes), cotangent
    )
    results = list(finish_layer(fin, sums, out, gtok))
    at = FINISH_OUT.index("g_qkv")
    results[at] = results[at].reshape(three, qk, width).transpose(2, 0, 1)
    return tuple(results)


def solution(mesh):
    in_specs = (
        P("dp", "tensor", None),
        P("dp", None),
        P("dp"),
        P(),
        P(None, None, "tensor"),
        P(None, "tensor"),
        P("tensor", None),
        P(),
        P(),
        P(),
        P(None, None, "tensor"),
        P(None, "tensor"),
        P("tensor", None),
        P(),
        P(),
        P(),
        P("dp", "tensor", None),
    )
    out_specs = (
        P("dp", "tensor", None),
        P("dp", "tensor", None),
        P(),
        P(None, None, "tensor"),
        P(None, "tensor"),
        P("tensor", None),
        P(),
        P(),
        P(),
        P(None, None, "tensor"),
        P(None, "tensor"),
        P("tensor", None),
        P(),
        P(),
        P(),
    )
    return jax.shard_map(
        per_device, mesh=mesh, in_specs=in_specs, out_specs=out_specs, check_vma=False
    )
```

```python
from functools import partial

import jax
import jax.numpy as jnp
from jax import lax
from jax.experimental import pallas as pl
from jax.experimental.pallas import tpu as pltpu
from jax.sharding import PartitionSpec as P

HEADS = 12
HEAD_DIM = 64
EPSILON = 1e-05
VMEM_LIMIT = 255 * 2**18
MESH = pl.DeviceIdType.MESH
BF = jnp.bfloat16
F32 = jnp.float32
NT = (((1,), (1,)), ((), ()))
TN = (((0,), (0,)), ((), ()))
NN = (((1,), (0,)), ((), ()))
DIRECT = (3,)


def dot(a, b, dims=NN):
    return lax.dot_general(a, b, dims, preferred_element_type=F32)


def remote(src, dst, send, recv, to):
    return pltpu.make_async_remote_copy(
        src_ref=src, dst_ref=dst, send_sem=send, recv_sem=recv, device_id=to, device_id_type=MESH
    )


def local(src, dst, sem):
    return pltpu.make_async_copy(src, dst, sem)


def dma(*shape):
    return pltpu.SemaphoreType.DMA(shape)


def chunk_rows(ndp, rows):
    return -(-rows // (16 * ndp)) * 16


class Links:
    def __init__(self, ndp):
        self.ndp = ndp
        self.na = ndp // 2
        self.dp = lax.axis_index("dp")
        self.t = lax.axis_index("tensor")
        self.a = self.dp // 2
        self.b = lax.rem(self.dp, 2)
        self.y = self.t // 2
        self.c = lax.rem(self.t, 2)
        self.core = (self.dp, 2 * self.y + 1 - self.c)
        self.far = (self.dp, 2 * (1 - self.y) + self.c)
        self.cross = (self.dp, 2 * (1 - self.y) + 1 - self.c)
        self.pair = (2 * self.a + 1 - self.b, self.t)

    def up(self, off):
        return lax.rem(self.a + off, self.na)

    def down(self, off):
        return lax.rem(self.a + self.na - off, self.na)

    def column(self, off):
        return (2 * self.up(off) + self.b, self.t)

    def quarter(self, s):
        return 2 * lax.rem(self.y + s // 2, 2) + lax.rem(self.c + s % 2, 2)

    def greet(self):
        barrier = pltpu.get_barrier_semaphore()
        others = [self.core, self.far, self.cross, self.pair]
        others += [self.column(o) for o in range(1, self.na)]
        for other in others:
            pl.semaphore_signal(barrier, inc=1, device_id=other, device_id_type=MESH)
        pl.semaphore_wait(barrier, len(others))


class Gather:
    def __init__(self, links, own, place, sems, rows):
        self.l, self.own, self.place, self.s = links, own, place, sems
        self.cr = rows // links.ndp
        self.fits = rows % (16 * links.ndp) == 0

    def relayed(self, m):
        return self.fits and m not in DIRECT

    def share(self, ref, d):
        return ref.at[pl.ds(pl.multiple_of(d * self.cr, 16), self.cr)]

    def pair_of(self, name, m, i=None):
        s, r = self.s[name]
        return (s.at[m], r.at[m]) if i is None else (s.at[m, i], r.at[m, i])

    def core(self, m):
        return remote(self.own(m), self.place(m, 1), *self.pair_of("c", m), self.l.core)

    def core_far(self, m):
        return remote(self.place(m, 2), self.place(m, 3), *self.pair_of("cf", m), self.l.core)

    def over_y(self, m):
        src, dst = self.own(m), self.place(m, 2)
        if self.relayed(m):
            src, dst = self.share(src, self.l.dp), self.share(dst, self.l.dp)
        return remote(src, dst, *self.pair_of("y", m), self.l.far)

    def over_x(self, m, off):
        at = self.share(self.place(m, 2), 2 * self.l.down(off) + self.l.b)
        return remote(at, at, *self.pair_of("x", m, off), self.l.pair)

    def over_z(self, m, off):
        at = self.share(self.place(m, 2), self.l.dp)
        return remote(at, at, *self.pair_of("z", m, off - 1), self.l.column(off))

    def step_spread(self, m):
        if self.relayed(m):
            self.over_y(m).wait_recv()
            self.over_x(m, 0).start()
            for off in range(1, self.l.na):
                self.over_z(m, off).start()

    def step_on(self, m):
        if self.relayed(m):
            for off in range(1, self.l.na):
                self.over_z(m, off).wait_recv()
                self.over_x(m, off).start()

    def step_core(self, m):
        if self.relayed(m):
            for off in range(self.l.na):
                self.over_x(m, off).wait_recv()
        else:
            self.over_y(m).wait_recv()
        self.core_far(m).start()

    def finish(self, m):
        self.core(m).wait_send()
        self.over_y(m).wait_send()
        self.core_far(m).wait_send()
        if self.relayed(m):
            for off in range(self.l.na):
                self.over_x(m, off).wait_send()
            for off in range(1, self.l.na):
                self.over_z(m, off).wait_send()


class Reducer:
    def __init__(self, links, refs, sems):
        self.l = links
        self.near, self.far, self.ybuf, self.xbuf, self.zbuf, self.own, self.fin = refs
        self.s = sems
        self.split = self.near.shape[1]
        self.cr = self.near.shape[4]
        self.rows = self.far.shape[2]
        self.units = self.near.shape[0] * self.split

    def block(self, u):
        return u // self.split, u % self.split

    def shares(self, first, count):
        for row in range(first, first + count, self.cr):
            j, inside = row // self.rows, row % self.rows // self.cr
            yield j, inside // 2, inside % 2, row

    def put_near(self, k, first, value):
        for j, i, b, row in self.shares(first, value.shape[0]):
            self.near[k, j, i, b] = value[row - first : row - first + self.cr].astype(BF)

    def put_far(self, k, first, value):
        for row in range(first, first + value.shape[0], self.cr):
            at = pl.ds(row % self.rows, self.cr)
            self.far[k, row // self.rows, at] = value[row - first : row - first + self.cr].astype(BF)

    def clear_padding(self):
        for i in range(self.rows // self.cr // 2, self.l.na):
            self.near[:, :, i] = jnp.zeros_like(self.near[:, :, i])

    def copy_y(self, u):
        s, r = self.s["y"]
        return remote(self.far.at[self.block(u)], self.ybuf.at[self.block(u)], s.at[u], r.at[u], self.l.far)

    def copy_x(self, u):
        s, r = self.s["x"]
        k, j = self.block(u)
        return remote(self.near.at[k, j, :, 1 - self.l.b], self.xbuf.at[u], s.at[u], r.at[u], self.l.pair)

    def copy_z(self, u, off):
        s, r = self.s["z"]
        k, j = self.block(u)
        src = self.near.at[k, j, self.l.up(off), self.l.b]
        return remote(src, self.zbuf.at[u, off - 1], s.at[u, off - 1], r.at[u, off - 1], self.l.column(off))

    def place(self, u):
        k, j = self.block(u)
        return self.fin.at[k, j, self.l.a, self.l.b]

    def copy_gz(self, u, off):
        s, r = self.s["gz"]
        return remote(self.own.at[u], self.place(u), s.at[u, off - 1], r.at[u, off - 1], self.l.column(off))

    def copy_gx(self, u):
        s, r = self.s["gx"]
        k, j = self.block(u)
        at = self.fin.at[k, j, :, self.l.b]
        return remote(at, at, s.at[u], r.at[u], self.l.pair)

    def copy_own(self, u):
        return local(self.own.at[u], self.place(u), self.s["own"].at[u])

    def start_y(self, u):
        self.copy_y(u).start()

    def step_x(self, u):
        self.copy_y(u).wait_recv()
        k, j = self.block(u)
        for row in range(0, self.rows, self.cr):
            i = row // self.cr
            share = self.near.at[k, j, i // 2, i % 2]
            share[...] = (share[...].astype(F32) + self.ybuf[k, j, row : row + self.cr].astype(F32)).astype(BF)
        self.copy_x(u).start()

    def step_z(self, u):
        self.copy_x(u).wait_recv()
        k, j = self.block(u)
        for i in range(self.l.na):
            share = self.near.at[k, j, i, self.l.b]
            share[...] = (share[...].astype(F32) + self.xbuf[u, i].astype(F32)).astype(BF)
        for off in range(1, self.l.na):
            self.copy_z(u, off).start()

    def step_own(self, u):
        k, j = self.block(u)
        total = self.near[k, j, self.l.a, self.l.b].astype(F32)
        for off in range(1, self.l.na):
            self.copy_z(u, off).wait_recv()
            total = total + self.zbuf[u, off - 1].astype(F32)
        self.spread(u, total)

    def spread(self, u, total):
        self.own[u] = total.astype(BF)
        for off in range(1, self.l.na):
            self.copy_gz(u, off).start()
        self.copy_own(u).start()

    def step_on(self, u):
        self.copy_own(u).wait()
        for off in range(1, self.l.na):
            self.copy_gz(u, off).wait_recv()
        self.copy_gx(u).start()

    def finish(self, u):
        self.copy_y(u).wait_send()
        self.copy_x(u).wait_send()
        for off in range(1, self.l.na):
            self.copy_z(u, off).wait_send()
            self.copy_gz(u, off).wait_send()
        self.copy_gx(u).wait()


class SmallSum:
    def __init__(self, links, mine, got, sems):
        self.l, self.mine, self.got = links, mine, got
        self.ss, self.rs = sems
        self.levels = got.shape[0]

    def partner(self, i):
        if i < 3:
            return (self.l.core, self.l.far, self.l.pair)[i]
        step = 2 ** (i - 3)
        a = self.l.a + step - 2 * step * lax.rem(self.l.a // step, 2)
        return (2 * a + self.l.b, self.l.t)

    def swap(self, i):
        return remote(self.mine.at[i], self.got.at[i], self.ss.at[i], self.rs.at[i], self.partner(i))

    def start(self, i):
        self.swap(i).start()

    def add(self, i):
        self.swap(i).wait_recv()
        total = self.mine[i] + self.got[i]
        if i + 1 < self.levels:
            self.mine[i + 1] = total
            self.start(i + 1)
        return total

    def finish(self):
        for i in range(self.levels):
            self.swap(i).wait_send()


def positions(links, size):
    y, c = links.y, links.c
    return [(2 * y + c) * size, (2 * (1 - y) + c) * size, (2 * y + 1 - c) * size, (2 * (1 - y) + 1 - c) * size]


def fill_distance(firsts, size, dist_ref):
    for kb, key in enumerate(firsts):
        for qb, query in enumerate(firsts[:2]):
            row = lax.broadcasted_iota(jnp.int32, (size, size), 0) + key
            col = lax.broadcasted_iota(jnp.int32, (size, size), 1) + query
            dist_ref[kb * size : (kb + 1) * size, qb * size : (qb + 1) * size] = jnp.abs(row - col).astype(F32)


def second_segment(links, size, r, block):
    y = links.y
    place = lax.broadcasted_iota(jnp.int32, (size, 1), 0) + positions(links, size)[block]
    return jnp.where(place >= r.boundary[y], r.type_ids[y, 1], r.type_ids[y, 0]) == 1


def mean(a):
    return jnp.mean(a, axis=-1, keepdims=True)


def norm_forward(values):
    centered = values - mean(values)
    scale = lax.rsqrt(mean(centered * centered) + EPSILON)
    return centered * scale, scale


def norm_backward(grad, unit, scale, gain):
    n = grad * gain
    return scale * (n - mean(n) - unit * mean(n * unit))


def gelu_parts(gate):
    e = jnp.exp(gate * gate * -0.5)
    t = 1.0 / (1.0 + jnp.abs(gate) * (0.3275911 * 0.5**0.5))
    poly = t * (
        0.5 * 0.254829592
        + t * (0.5 * -0.284496736 + t * (0.5 * 1.421413741 + t * (0.5 * -1.453152027 + t * (0.5 * 1.061405429))))
    )
    tail = poly * e
    return jnp.where(gate < 0, tail, 1.0 - tail), e * 0.3989422804014327


class Names:
    def __init__(self):
        self.names, self.shapes = [], []

    def add(self, name, shape):
        self.names.append(name)
        self.shapes.append(shape)

    def pair(self, name, *shape):
        self.add(name + "_s", dma(*shape))
        self.add(name + "_r", dma(*shape))


ANY = pl.BlockSpec(memory_space=pl.ANY)
VMEM = pl.BlockSpec(memory_space=pltpu.VMEM)
SMEM = pl.BlockSpec(memory_space=pltpu.SMEM)


class Refs:
    def __init__(self, names, refs):
        self.__dict__.update(zip(names, refs))

    def sems(self, name):
        return getattr(self, name + "_s"), getattr(self, name + "_r")


ENTER_IN = ["tokens", "wqkv", "wout", "wgu", "wdown", "b_qv", "b_gu", "b_out", "table"]
ENTER_IN += ["type_ids", "boundary", "slopes"]
ENTER_OUT = ["mixed", "xlow", "qkv", "kvp", "ctx", "lse", "wall", "biases"]
MATRICES = 4


def enter_kernel(ndp, names, *refs):
    r = Refs(names, refs)
    l = Links(ndp)
    nm, width = MATRICES, r.wdown.shape[1]
    size = r.tokens.shape[1]
    rows = 2 * size
    heads_dev = HEADS // 4
    qk = heads_dev * HEAD_DIM
    firsts = positions(l, size)

    def place(m, s):
        return r.wa.at[s] if m == 0 else r.wall.at[m, s]

    def own(m):
        return (r.wa.at[0], r.gu.at[0], r.gu.at[1], r.wdown)[m]

    g = Gather(l, own, place, {n: r.sems("g" + n) for n in ("c", "cf", "y", "x", "z")}, width)
    tok_own = local(r.tokens.at[l.y], r.tok.at[pl.ds(0, size)], r.ld.at[0])
    wa_own = [
        local(r.wqkv, r.wa.at[0, pl.ds(0, 3 * qk)], r.ld.at[1]),
        local(r.wout, r.wa.at[0, pl.ds(3 * qk, qk)], r.ld.at[2]),
    ]
    gu_own = local(r.wgu, r.graw, r.ld.at[3])
    for c in (*wa_own, tok_own, gu_own):
        c.start()
    tok_far = remote(r.tokens.at[1 - l.y], r.tok.at[pl.ds(size, size)], *(a.at[0] for a in r.sems("tk")), l.far)
    bias_to = [
        remote(r.biases.at[0], r.biases.at[s], *(a.at[s] for a in r.sems("bi")), to)
        for s, to in ((1, l.core), (2, l.far), (3, l.cross))
    ]

    def kv_send(s):
        other = s + 1 - 2 * (s % 2)
        src = r.qkvb.at[s, pl.ds(qk, 2 * qk)]
        return remote(src, r.kvb.at[other], *(a.at[s] for a in r.sems("kv")), l.core)

    def kv_wait(s):
        other = s + 1 - 2 * (s % 2)
        src = r.qkvb.at[other, pl.ds(qk, 2 * qk)]
        return remote(src, r.kvb.at[s], *(a.at[other] for a in r.sems("kv")), l.core)

    r.biases[0] = jnp.zeros_like(r.biases[0])
    r.biases[0, 0:1, :qk] = r.b_qv[0:1]
    r.biases[0, 0:1, 2 * qk : 3 * qk] = r.b_qv[1:2]
    r.biases[0, 1:3, :] = r.b_gu[...]
    l.greet()
    for c in wa_own:
        c.wait()
    g.over_y(0).start()
    g.core(0).start()
    for b in bias_to:
        b.start()

    def enter(block):
        at = pl.ds(block * size, size)
        second = second_segment(l, size, r, block)
        x = r.tok[at].astype(F32) + jnp.where(second, r.table[1:2], r.table[0:1])
        r.xb[at] = x
        r.xl[at] = x.astype(BF)

    def project(s, block):
        at = slice(block * size, (block + 1) * size)
        column = r.biases[s].T[: 3 * qk, 0:1]
        part = dot(r.wa[s, : 3 * qk], r.xl[at], NT) + column
        r.qkvb[s, :, at] = part.astype(BF)

    tok_own.wait()
    enter(0)
    project(0, 0)
    tok_far.start()
    for b in bias_to:
        b.wait_recv()
    g.core(0).wait_recv()
    project(1, 0)
    g.step_spread(0)
    gu_own.wait()
    for i in range(2):
        r.gu[i] = r.graw[:, i, :]
    gu_out = local(r.gu, r.wall.at[pl.ds(1, 2), 0], r.ld.at[4])
    gu_out.start()
    for m in (1, 2):
        g.over_y(m).start()
    fill_distance(firsts, size, r.dist)
    tok_far.wait_recv()
    g.over_y(3).start()
    enter(1)
    x_out = local(r.xl, r.xlow, r.ld.at[5])
    x_out.start()
    for s in (0, 1):
        project(s, 1)
        kv_send(s).start()
    g.step_on(0)
    for m in range(1, nm):
        g.core(m).start()

    def head(ticks, h, carry):
        s, j = h // heads_dev, h % heads_dev

        @pl.when(j == 0)
        def _():
            kv_wait(s).wait_recv()

        def lines(ref, first):
            return ref[s, pl.ds(pl.multiple_of(first + j * HEAD_DIM, HEAD_DIM), HEAD_DIM), :]

        q = lines(r.qkvb, 0) * BF(HEAD_DIM**-0.5)
        slope = r.slopes[l.quarter(s) * heads_dev + j]
        scores = [
            dot(key, q, TN) - slope * r.dist[i * rows : (i + 1) * rows]
            for i, key in enumerate((lines(r.qkvb, qk), lines(r.kvb, 0)))
        ]
        top = jnp.maximum(*(jnp.max(a, axis=0, keepdims=True) for a in scores))
        probs = [jnp.exp(a - top) for a in scores]
        total = sum(jnp.sum(a, axis=0, keepdims=True) for a in probs)
        values = (lines(r.qkvb, 2 * qk), lines(r.kvb, qk))
        out = sum(dot(v, p.astype(BF)) for v, p in zip(values, probs))
        r.ctxb[s, pl.ds(pl.multiple_of(j * HEAD_DIM, HEAD_DIM), HEAD_DIM), :] = (out * (1.0 / total)).astype(BF)
        r.lse[pl.ds(h, 1), :] = top + jnp.log(total)
        for at, steps in ticks.items():

            @pl.when(h == at)
            def _(steps=steps):
                for step in steps:
                    step()

        return carry

    lax.fori_loop(
        0,
        HEADS // 2,
        partial(
            head,
            {
                3: [partial(g.step_spread, 1), partial(g.step_spread, 2)],
                5: [partial(g.step_core, 0)],
            },
        ),
        0,
    )
    g.core_far(0).wait_recv()
    for s in (2, 3):
        for block in range(2):
            project(s, block)
        kv_send(s).start()
    wa_out = local(r.wa, r.wall.at[0], r.ld.at[6])
    wa_out.start()
    lax.fori_loop(
        HEADS // 2,
        HEADS,
        partial(head, {8: [partial(g.step_on, 1)], 9: [partial(g.step_on, 2)]}),
        0,
    )
    outs = [
        local(r.qkvb, r.qkv, r.ld.at[7]),
        local(r.kvb, r.kvp, r.ld.at[8]),
        local(r.ctxb, r.ctx, r.ld.at[9]),
    ]
    for o in outs:
        o.start()
    g.step_core(3)
    for s in range(4):
        part = dot(r.ctxb[s], r.wa[s, 3 * qk :], TN)
        r.xb[...] += part + r.b_out[...].reshape(1, width) if s == 0 else part
    mixed_out = local(r.xb, r.mixed, r.ld.at[10])
    mixed_out.start()
    g.step_core(1)
    g.step_core(2)
    for m in range(1, nm):
        g.core(m).wait_recv()
        g.core_far(m).wait_recv()
    for m in range(nm):
        g.finish(m)
    for s in range(4):
        kv_send(s).wait_send()
    tok_far.wait_send()
    for b in bias_to:
        b.wait_send()
    for o in outs + [gu_out, x_out, wa_out, mixed_out]:
        o.wait()


def enter_layer(ndp, inputs):
    tokens, width = inputs[0], inputs[0].shape[2]
    size = tokens.shape[1]
    rows = 2 * size
    qk = HEADS // 4 * HEAD_DIM
    na = ndp // 2
    nm = MATRICES
    n = Names()
    n.add("wa", pltpu.VMEM((4, width, width), BF))
    n.add("graw", pltpu.VMEM((width, 2, width), BF))
    n.add("gu", pltpu.VMEM((2, width, width), BF))
    n.add("tok", pltpu.VMEM((rows, width), BF))
    n.add("xb", pltpu.VMEM((rows, width), F32))
    n.add("xl", pltpu.VMEM((rows, width), BF))
    n.add("qkvb", pltpu.VMEM((4, 3 * qk, rows), BF))
    n.add("kvb", pltpu.VMEM((4, 2 * qk, rows), BF))
    n.add("ctxb", pltpu.VMEM((4, qk, rows), BF))
    n.add("dist", pltpu.VMEM((2 * rows, rows), F32))
    n.add("ld", dma(11))
    n.pair("tk", 1)
    n.pair("bi", 4)
    n.pair("kv", 4)
    n.pair("gc", nm)
    n.pair("gcf", nm)
    n.pair("gy", nm)
    n.pair("gx", nm, na)
    n.pair("gz", nm, na - 1)
    shape = jax.ShapeDtypeStruct
    return pl.pallas_call(
        partial(enter_kernel, ndp, ENTER_IN + ENTER_OUT + n.names),
        in_specs=[ANY, ANY, ANY, ANY, ANY, VMEM, VMEM, VMEM, VMEM, SMEM, SMEM, SMEM],
        out_specs=[ANY, ANY, ANY, ANY, ANY, VMEM, ANY, VMEM],
        out_shape=[
            shape((rows, width), F32),
            shape((rows, width), BF),
            shape((4, 3 * qk, rows), BF),
            shape((4, 2 * qk, rows), BF),
            shape((4, qk, rows), BF),
            shape((HEADS, rows), F32),
            shape((nm, 4, width, width), BF),
            shape((4, 8, width), F32),
        ],
        scratch_shapes=n.shapes,
        compiler_params=pltpu.CompilerParams(
            collective_id=0, has_side_effects=True, vmem_limit_bytes=VMEM_LIMIT
        ),
    )(*inputs)


LEAVE_IN = ["mixed", "xlow", "qkv", "kvp", "ctx", "lse", "wall", "biases", "wdown"]
LEAVE_IN += ["gain_one", "shift_one", "b_down", "gain_two", "shift_two"]
LEAVE_IN += ["cot", "type_ids", "boundary", "slopes"]
LEAVE_OUT = ["fin", "sums", "out", "gtok", "cbuf"]
DOWN, GATE, UP, ATTN = range(4)
ROW_GU, ROW_QV, SMALL_ROWS = 8, 16, 24


def leave_kernel(ndp, names, *refs):
    r = Refs(names, refs)
    l = Links(ndp)
    rows, width = r.mixed.shape
    size = rows // 2
    heads_dev = HEADS // 4
    qk = heads_dev * HEAD_DIM
    firsts = positions(l, size)
    stages = r.cstage.shape[0]
    red = Reducer(
        l,
        (r.near, r.far, r.ybuf, r.xbuf, r.zbuf, r.own, r.fin),
        {**{n: r.sems("r" + n) for n in ("y", "x", "z", "gz", "gx")}, "own": r.rown},
    )
    pump = Pump(red, schedule(red.units))
    small = SmallSum(l, r.smine, r.sgot, r.sems("sm"))
    sv = r.smine.at[0]

    def vec(ref):
        return ref[...].reshape(1, width)

    def core_copy(k, i):
        src = r.cstage.at[k % stages, i]
        return remote(src, r.cbuf.at[k, i], *(a.at[k, i] for a in r.sems("co")), l.core)

    def fetch(k, i):
        slot = (1 - i, 0, 1, 1 - i)[k]
        return local(r.cbuf.at[k, i], r.cload.at[slot], r.cl.at[slot])

    def room(k, i):
        if k >= stages:
            core_copy(k - stages, i).wait_send()

    def start_fetch(k, i):
        core_copy(k, i).wait_recv()
        fetch(k, i).start()

    def merge(k, i, first, value):
        slot = (1 - i, 0, 1, 1 - i)[k]
        total = value + r.cload[slot, pl.ds(first, value.shape[0])].astype(F32)
        (red.put_near, red.put_far)[i](k, first, total)

    out_own = local(r.outb.at[pl.ds(0, size)], r.out.at[l.y], r.ld.at[8])
    out_far = remote(r.outb.at[pl.ds(size, size)], r.out.at[l.y], *(a.at[0] for a in r.sems("ou")), l.far)
    cot_own = local(r.cot.at[l.y], r.cotb.at[pl.ds(0, size)], r.ld.at[0])
    cot_far = remote(r.cot.at[1 - l.y], r.cotb.at[pl.ds(size, size)], *(a.at[0] for a in r.sems("ct")), l.far)

    def order(i):
        return 2 * (i % 2) + i // 2

    def ffn_phase(wo, gh, a_ref, b_ref, hid, unit, hl, ht, r1, wbuf):
        acc, gf = r.gm, hl

        def load_weights(s, buf):
            return local(r.wall.at[pl.ds(1, 3), s], wbuf.at[buf], r.wl.at[buf])

        def start_weights(s, buf):
            if s:
                load_weights(s, buf).start()
            else:
                local(r.wall.at[pl.ds(1, 2), 0], wbuf.at[buf, pl.ds(0, 2)], r.wl.at[buf]).start()
                local(r.wdown, wbuf.at[buf, 2], r.wl.at[buf]).start()

        lx = local(r.mixed, acc, r.ld.at[1])
        lo = local(r.wall.at[0, pl.ds(0, 4), pl.ds(3 * qk, qk)], wo, r.ld.at[2])
        lc = local(r.ctx, r.ctxb, r.ld.at[3])
        lx.start()
        start_weights(0, 0)
        start_weights(2, 1)
        for c in (cot_own, lo, lc):
            c.start()
        l.greet()
        cot_far.start()
        red.clear_padding()
        sv[...] = jnp.zeros_like(sv)
        lx.wait()
        u1, s1 = norm_forward(acc[...])
        unit[...] = u1
        r1[...] = s1
        h1 = u1 * vec(r.gain_one) + vec(r.shift_one)
        acc[...] = h1 + vec(r.b_down)
        hl[...] = h1.astype(BF)
        ht[...] = h1.T.astype(BF)

        def forward(i, carry):
            s, buf = order(i), i % 2
            load_weights(s, buf).wait()
            for half in range(2):
                at = slice(half * size, (half + 1) * size)
                gate = dot(hl[at], wbuf[buf, 0]) + r.biases[s, 1:2, :]
                up = dot(hl[at], wbuf[buf, 1]) + r.biases[s, 2:3, :]
                cdf, pdf = gelu_parts(gate)
                act = gate * cdf
                a_ref[s, at] = act.astype(BF)
                b_ref[s, at] = (up * (cdf + gate * pdf)).astype(BF)
                hidden = (act * up).astype(BF)
                hid[s, at] = hidden
                acc[at] += dot(hidden, wbuf[buf, 2])

            @pl.when(i < 2)
            def _():
                load_weights(order(i + 2), buf).start()

            return carry

        lax.fori_loop(0, 4, forward, 0)
        u2, s2 = norm_forward(acc[...])
        out = u2 * vec(r.gain_two) + vec(r.shift_two)
        r.outb[...] = out.astype(BF)
        out_far.start()
        cot_own.wait()
        cot_far.wait_recv()
        cot = r.cotb[...].astype(F32)
        g2 = norm_backward(cot, u2, s2, vec(r.gain_two))
        sv[6:7, :] = jnp.sum(cot * u2, axis=0, keepdims=True)
        sv[7:8, :] = jnp.sum(cot, axis=0, keepdims=True)
        sv[5:6, :] = jnp.sum(g2, axis=0, keepdims=True)
        gh[...] = g2
        gf[...] = g2.astype(BF)
        for i, s in ((1, 3), (0, 1)):
            r.cstage[DOWN % stages, i] = dot(hid[s], gf[...], TN).astype(BF)
            core_copy(DOWN, i).start()

        def backward(s, buf):
            load = None
            g_hidden = dot(gf[...], wbuf[buf, 2], NT)
            g_gate = (g_hidden * b_ref[s].astype(F32)).astype(BF)
            g_up = (g_hidden * a_ref[s].astype(F32)).astype(BF)
            row = ROW_GU + 2 * l.quarter(s)
            sv[pl.ds(row, 1), :] = jnp.sum(g_gate.astype(F32), axis=0, keepdims=True)
            sv[pl.ds(row + 1, 1), :] = jnp.sum(g_up.astype(F32), axis=0, keepdims=True)
            gh[...] += dot(g_gate, wbuf[buf, 0], NT)
            gh[...] += dot(g_up, wbuf[buf, 1], NT)
            return g_gate, g_up

        for i, s, buf in ((1, 3, 1), (0, 1, 0)):
            g_gate, g_up = backward(s, buf)
            start_weights(s - 1, buf)
            for k, g in ((GATE, g_gate), (UP, g_up)):
                room(k, i)
                r.cstage[k % stages, i] = dot(ht[...], g).astype(BF)
                core_copy(k, i).start()
            start_fetch(DOWN, i)
            value = dot(hid[s - 1], gf[...], TN)
            fetch(DOWN, i).wait()
            merge(DOWN, i, 0, value)
            for u in range(min(AHEAD, red.split)):
                if (u > 0) == (i == 0):
                    red.start_y(u)
        for i, s, buf in ((1, 2, 1), (0, 0, 0)):
            load_weights(s, buf).wait()
            for k in (GATE, UP):
                start_fetch(k, i)
            g_gate, g_up = backward(s, buf)
            for k, g in ((GATE, g_gate), (UP, g_up)):
                value = dot(ht[...], g)
                fetch(k, i).wait()
                merge(k, i, 0, value)
            pump.until(POINTS[1 - i])
        lc.wait()
        lo.wait()
        g_h1 = gh[...]
        unit_one = unit[...]
        sv[3:4, :] = jnp.sum(g_h1 * unit_one, axis=0, keepdims=True)
        sv[4:5, :] = jnp.sum(g_h1, axis=0, keepdims=True)
        gm = norm_backward(g_h1, unit_one, r1[...], vec(r.gain_one))
        sv[2:3, :] = jnp.sum(gm, axis=0, keepdims=True)
        r.gm[...] = gm
        ga = gm.astype(BF)
        r.cotb[...] = ga
        for s in range(4):
            r.gctx[s] = dot(wo[s], ga, NT).astype(BF)

    v = pltpu.VMEM
    pl.run_scoped(
        ffn_phase,
        v((4, qk, width), BF),
        v((rows, width), F32),
        v((4, rows, width), BF),
        v((4, rows, width), BF),
        v((4, rows, width), BF),
        v((rows, width), F32),
        v((rows, width), BF),
        v((width, rows), BF),
        v((rows, 1), F32),
        v((2, 3, width, width), BF),
    )

    def attention_phase(wq, qkvb, kvb, xl, dist, dqkv, dkvo, dkvs):
        lq = local(r.qkv, qkvb, r.ld.at[4])
        lk = local(r.kvp, kvb, r.ld.at[5])
        lw = local(r.wall.at[0, pl.ds(0, 4), pl.ds(0, 3 * qk)], wq, r.ld.at[6])
        lx = local(r.xlow, xl, r.ld.at[7])
        lq.start()
        lk.start()
        fill_distance(firsts, size, dist)

        def other(s):
            return s + 1 - 2 * (s % 2)

        def send(s):
            return remote(dkvs.at[s], r.dkvr.at[other(s)], *(a.at[s] for a in r.sems("dk")), l.core)

        def arrived(s):
            return remote(dkvs.at[other(s)], r.dkvr.at[s], *(a.at[other(s)] for a in r.sems("dk")), l.core)

        lq.wait()
        lk.wait()

        def head(first, h, carry):
            s, j = h // heads_dev, h % heads_dev

            def span(first):
                return pl.ds(pl.multiple_of(first + j * HEAD_DIM, HEAD_DIM), HEAD_DIM)

            qt = qkvb[s, span(0), :] * BF(HEAD_DIM**-0.5)
            q = qt.T
            dot_t = r.gctx[s, span(0), :]
            do = dot_t.T
            slope = r.slopes[l.quarter(s) * heads_dev + j]
            lse = r.lse[pl.ds(h, 1), :]
            keys = (qkvb[s, span(qk), :], kvb[s, span(0), :])
            values = (qkvb[s, span(2 * qk), :], kvb[s, span(qk), :])
            probs = [
                jnp.exp(dot(key, qt, TN) - slope * dist[i * rows : (i + 1) * rows] - lse)
                for i, key in enumerate(keys)
            ]
            g_probs = [dot(value, dot_t, TN) for value in values]
            inner = sum(jnp.sum(p * g, axis=0, keepdims=True) for p, g in zip(probs, g_probs))
            g_scores = [(p * (g - inner)).astype(BF) for p, g in zip(probs, g_probs)]
            dq = sum(dot(key, g) for key, g in zip(keys, g_scores))
            dqkv[s, span(0), :] = (dq * HEAD_DIM**-0.5).astype(BF)
            dk = [dot(g, q).T for g in g_scores]
            dv = [dot(p.astype(BF), do).T for p in probs]
            dkvo[s, span(0), :] = dk[0]
            dkvo[s, span(qk), :] = dv[0]
            dkvs[s, span(0), :] = dk[1].astype(BF)
            dkvs[s, span(qk), :] = dv[1].astype(BF)

            @pl.when(j == heads_dev - 1)
            def _():
                send(s).start()

            if first:

                @pl.when(h == first)
                def _():
                    lw.start()
                    lx.start()

            else:

                @pl.when(h == 1)
                def _():
                    start_fetch(ATTN, 1)
                    finish_attn(1, 2)

            for at in range(first, first + HEADS // 2):
                time = HEAD_TIMES[0 if first else 1] + HEAD_TIMES[2] * (at + 1 - first)
                if pump.due(time):

                    @pl.when(h == at)
                    def _(time=time):
                        pump.until(time)

            return carry

        def collect(s):
            arrived(s).wait_recv()
            dqkv[s, qk:, :] = (dkvo[s] + r.dkvr[s].astype(F32)).astype(BF)
            g = dqkv[s]
            sv[pl.ds(ROW_QV + l.quarter(s), 1), : 3 * qk] = dot(jnp.ones((8, rows), BF), g, NT)[0:1]
            r.gm[...] += dot(g, wq[s], TN)

        def attn_parts(s):
            return ((0, dot(dqkv[s], xl[...])), (3 * qk, dot(r.ctxb[s], r.cotb[...])))

        def send_attn(i, s):
            room(ATTN, i)
            for at, value in attn_parts(s):
                r.cstage[ATTN % stages, i, pl.ds(at, value.shape[0])] = value.astype(BF)
            core_copy(ATTN, i).start()

        def finish_attn(i, s):
            parts = attn_parts(s)
            fetch(ATTN, i).wait()
            for at, value in parts:
                merge(ATTN, i, at, value)

        lax.fori_loop(HEADS // 2, HEADS, partial(head, HEADS // 2), 0)
        lw.wait()
        lx.wait()
        collect(3)
        send_attn(1, 3)
        collect(2)
        pump.until(POINTS[2])
        lax.fori_loop(0, HEADS // 2, partial(head, 0), 0)
        collect(1)
        send_attn(0, 1)
        collect(0)
        pump.until(POINTS[3])
        start_fetch(ATTN, 0)
        g_entered = r.gm[...]
        total = jnp.sum(g_entered, axis=0, keepdims=True)
        second = sum(
            jnp.sum(
                jnp.where(second_segment(l, size, r, i), g_entered[i * size : (i + 1) * size], 0.0),
                axis=0,
                keepdims=True,
            )
            for i in range(2)
        )
        sv[0:1, :] = total - second
        sv[1:2, :] = second
        small.start(0)

        finish_attn(0, 0)
        for s in range(4):
            send(s).wait_send()

    pl.run_scoped(
        attention_phase,
        v((4, 3 * qk, width), BF),
        v((4, 3 * qk, rows), BF),
        v((4, 2 * qk, rows), BF),
        v((rows, width), BF),
        v((2 * rows, rows), F32),
        v((4, 3 * qk, rows), BF),
        v((4, 2 * qk, rows), F32),
        v((4, 2 * qk, rows), BF),
    )

    tok_own = local(r.gm.at[pl.ds(0, size)], r.gtok.at[l.y], r.ld.at[9])
    r.cload[0, :size] = r.gm[size:].astype(BF)
    tok_far = remote(r.cload.at[0, pl.ds(0, size)], r.ggot, *(a.at[0] for a in r.sems("gt")), l.far)
    out_own.start()
    tok_own.start()
    pump.after_y = tok_far.start
    for i in range(small.levels):
        total = small.add(i)
        pump.until(POINTS[3] + 12.0 * (i + 1))
    pump.until(None)
    r.sums[...] = total
    tok_far.wait_recv()
    r.gm[size:] = r.ggot[...].astype(F32)
    tok_got = local(r.gm.at[pl.ds(size, size)], r.gtok.at[1 - l.y], r.ld.at[10])
    tok_got.start()
    for u in range(red.units):
        red.finish(u)
    for k in range(4 - stages, 4):
        for i in range(2):
            core_copy(k, i).wait_send()
    small.finish()
    cot_far.wait_send()
    out_far.wait()
    tok_far.wait_send()
    for c in (out_own, tok_own, tok_got):
        c.wait()


AHEAD = 2
HEAD_TIMES = (33.0, 52.0, 2.3)
POINTS = (19.0, 26.0, 52.0, 71.0)
READY = (7.2, 18.0, 20.0, 57.0)


def schedule(units):
    unit = 84.0 / units
    free = {"y": 0.0, "x": 0.0, "z": 0.0}
    waiting, order = [], []
    split = units // 4

    def use(link, at, cost):
        free[link] = max(free[link], at) + cost
        return free[link] + 2.5

    def start_y(u, at):
        waiting.append((use("y", max(at, READY[u // split]), unit), u, "step_x"))

    for u in range(min(AHEAD, units)):
        start_y(u, 0.0)
        if u >= split:
            order.append((READY[u // split], "start_y", u))
    now = 0.0
    while waiting:
        waiting.sort()
        at, u, step = waiting.pop(0)
        now = max(now, at)
        order.append((now, step, u))
        now += 0.5
        if step == "step_x":
            if u + AHEAD < units:
                order.append((max(now, READY[(u + AHEAD) // split]), "start_y", u + AHEAD))
                start_y(u + AHEAD, now)
            waiting.append((use("x", now, unit / 2), u, "step_z"))
        elif step == "step_z":
            waiting.append((use("z", now, unit / 2), u, "step_own"))
        elif step == "step_own":
            waiting.append((use("z", now, unit / 2), u, "step_on"))
        else:
            use("x", now, unit / 2)
    return sorted(order, key=lambda o: o[0])


class Pump:
    def __init__(self, red, order):
        self.red, self.order, self.after_y = red, list(order), None

    def due(self, time):
        return bool(self.order) and (time is None or self.order[0][0] <= time)

    def until(self, time):
        while self.due(time):
            _, step, u = self.order.pop(0)
            getattr(self.red, step)(u)
            if step == "step_x" and u == self.red.units - 1:
                self.after_y()


def leave_layer(ndp, inputs, cot):
    wall = inputs[6]
    rows, width = inputs[0].shape
    nm = wall.shape[0]
    size = rows // 2
    qk = HEADS // 4 * HEAD_DIM
    na = ndp // 2
    split = 3 if width % (48 * ndp) == 0 else 1
    stages = 2 if split > 1 else 1
    units = nm * split
    unit = width // split
    cr = chunk_rows(ndp, unit)
    n = Names()
    v = pltpu.VMEM
    n.add("near", v((nm, split, na, 2, cr, width), BF))
    n.add("far", v((nm, split, unit, width), BF))
    n.add("ybuf", v((nm, split, unit, width), BF))
    n.add("xbuf", v((units, na, cr, width), BF))
    n.add("zbuf", v((units, na - 1, cr, width), BF))
    n.add("own", v((units, cr, width), BF))
    n.add("cstage", v((stages, 2, width, width), BF))
    n.add("cload", v((2, width, width), BF))
    n.add("ctxb", v((4, qk, rows), BF))
    n.add("gctx", v((4, qk, rows), BF))
    n.add("cotb", v((rows, width), BF))
    n.add("outb", v((rows, width), BF))
    n.add("gm", v((rows, width), F32))
    n.add("ggot", v((size, width), BF))
    n.add("dkvr", v((4, 2 * qk, rows), BF))
    levels = 3 + (na - 1).bit_length()
    n.add("smine", v((levels, SMALL_ROWS, width), F32))
    n.add("sgot", v((levels, SMALL_ROWS, width), F32))
    n.add("ld", dma(11))
    n.add("cl", dma(2))
    n.add("wl", dma(2))
    n.add("rown", dma(units))
    n.pair("co", nm, 2)
    n.pair("ct", 1)
    n.pair("ou", 1)
    n.pair("gt", 1)
    n.pair("dk", 4)
    n.pair("sm", levels)
    n.pair("ry", units)
    n.pair("rx", units)
    n.pair("rz", units, na - 1)
    n.pair("rgz", units, na - 1)
    n.pair("rgx", units)
    shape = jax.ShapeDtypeStruct
    fin, *others = pl.pallas_call(
        partial(leave_kernel, ndp, LEAVE_IN + LEAVE_OUT + n.names),
        in_specs=[ANY, ANY, ANY, ANY, ANY, VMEM, ANY, VMEM, ANY, *[VMEM] * 5, ANY, SMEM, SMEM, SMEM],
        out_specs=[ANY, VMEM, ANY, ANY, ANY],
        out_shape=[
            shape((nm, split, na, 2, cr, width), BF),
            shape((SMALL_ROWS, width), F32),
            shape(cot.shape, BF),
            shape(cot.shape, F32),
            shape((nm, 2, width, width), BF),
        ],
        scratch_shapes=n.shapes,
        compiler_params=pltpu.CompilerParams(
            collective_id=1, has_side_effects=True, vmem_limit_bytes=VMEM_LIMIT
        ),
    )(*inputs)
    return fin.reshape(nm, -1, width), *others


FINISH_IN = ["fin", "sums", "got", "gtok"]
FINISH_OUT = ["output", "g_tokens", "table", "g_qkv", "g_bqv", "g_out", "g_bout", "g_gain1", "g_shift1"]
FINISH_OUT += ["g_gu", "g_bgu", "g_down", "g_bdown", "g_gain2", "g_shift2"]
SUM_ROWS = {"g_bout": 2, "g_gain1": 3, "g_shift1": 4, "g_bdown": 5, "g_gain2": 6, "g_shift2": 7}


def finish_kernel(*refs):
    r = Refs(FINISH_IN + FINISH_OUT, refs)
    step, last = pl.program_id(0), pl.num_programs(0) - 1
    t = lax.axis_index("tensor")
    qk = r.g_bqv.shape[1]
    first_out = 3 * pl.num_programs(0) // 4
    r.output[...] = r.got[...]
    r.g_tokens[...] = r.gtok[...]
    r.g_gu[:, 0, :] = r.fin[GATE].astype(F32)
    r.g_gu[:, 1, :] = r.fin[UP].astype(F32)
    r.g_down[...] = r.fin[DOWN].astype(F32)

    @pl.when(step < first_out)
    def _():
        r.g_qkv[...] = r.fin[ATTN].astype(F32)

    @pl.when(step >= first_out)
    def _():
        r.g_out[...] = r.fin[ATTN].astype(F32)

    @pl.when(step == last)
    def _():
        r.table[...] = r.sums[0:2, :]
        for name, row in SUM_ROWS.items():
            getattr(r, name)[...] = r.sums[row]

    for quarter in range(4):

        @pl.when((step == last) & (t == quarter))
        def _(quarter=quarter):
            first, row = ROW_GU + 2 * quarter, ROW_QV + quarter
            r.g_bgu[...] = r.sums[first : first + 2, :]
            r.g_bqv[0:1, :] = r.sums[row : row + 1, :qk]
            r.g_bqv[1:2, :] = r.sums[row : row + 1, 2 * qk : 3 * qk]


def finish_layer(fin, sums, out, gtok):
    nm, width = fin.shape[0], fin.shape[2]
    seqs, size = out.shape[:2]
    qk = width // 4
    shape = jax.ShapeDtypeStruct
    whole = lambda *dims: pl.BlockSpec(dims, lambda i: (0,) * len(dims))
    steps = 4
    blk = width // steps
    rows_of = lambda: pl.BlockSpec((seqs, size // steps, width), lambda i: (0, i, 0))
    vector = (whole(width), shape((width,), F32))
    outs = {
        "output": (rows_of(), shape(out.shape, out.dtype)),
        "g_tokens": (rows_of(), shape(gtok.shape, gtok.dtype)),
        "table": (whole(2, width), shape((2, width), F32)),
        "g_qkv": (pl.BlockSpec((blk, width), lambda i: (jnp.minimum(i, 2), 0)), shape((3 * qk, width), F32)),
        "g_bqv": (whole(2, qk), shape((2, qk), F32)),
        "g_out": (pl.BlockSpec((blk, width), lambda i: (jnp.maximum(i - 3, 0), 0)), shape((qk, width), F32)),
        "g_gu": (pl.BlockSpec((blk, 2, width), lambda i: (i, 0, 0)), shape((width, 2, width), F32)),
        "g_bgu": (whole(2, width), shape((2, width), F32)),
        "g_down": (pl.BlockSpec((blk, width), lambda i: (i, 0)), shape((width, width), F32)),
        **{name: vector for name in SUM_ROWS},
    }
    return pl.pallas_call(
        finish_kernel,
        grid=(steps,),
        in_specs=[
            pl.BlockSpec((nm, blk, width), lambda i: (0, i, 0)),
            whole(*sums.shape),
            rows_of(),
            rows_of(),
        ],
        out_specs=[outs[name][0] for name in FINISH_OUT],
        out_shape=[outs[name][1] for name in FINISH_OUT],
        compiler_params=pltpu.CompilerParams(vmem_limit_bytes=VMEM_LIMIT),
    )(fin, sums, out, gtok)


def per_device(
    tokens,
    type_ids,
    boundary,
    token_type_rows,
    query_key_value_weight,
    b_qv,
    output_weight,
    b_out,
    gain_one,
    shift_one,
    gate_up_weight,
    gate_up_bias,
    down_weight,
    b_down,
    gain_two,
    shift_two,
    cotangent,
):
    ndp = lax.axis_size("dp")
    width, three, qk = query_key_value_weight.shape
    wqkv = query_key_value_weight.transpose(1, 2, 0).reshape(three * qk, width)
    slopes = jnp.asarray([2.0 ** (-8.0 * (h + 1) / HEADS) for h in range(HEADS)], F32)
    first = enter_layer(
        ndp,
        (
            tokens,
            wqkv,
            output_weight,
            gate_up_weight,
            down_weight,
            b_qv,
            gate_up_bias,
            b_out,
            token_type_rows,
            type_ids,
            boundary,
            slopes,
        ),
    )
    vectors = (gain_one, shift_one, b_down, gain_two, shift_two)
    fin, sums, out, gtok, _ = leave_layer(
        ndp, (*first, down_weight, *vectors, cotangent, type_ids, boundary, slopes), cotangent
    )
    results = list(finish_layer(fin, sums, out, gtok))
    at = FINISH_OUT.index("g_qkv")
    results[at] = results[at].reshape(three, qk, width).transpose(2, 0, 1)
    return tuple(results)


def solution(mesh):
    in_specs = (
        P("dp", "tensor", None),
        P("dp", None),
        P("dp"),
        P(),
        P(None, None, "tensor"),
        P(None, "tensor"),
        P("tensor", None),
        P(),
        P(),
        P(),
        P(None, None, "tensor"),
        P(None, "tensor"),
        P("tensor", None),
        P(),
        P(),
        P(),
        P("dp", "tensor", None),
    )
    out_specs = (
        P("dp", "tensor", None),
        P("dp", "tensor", None),
        P(),
        P(None, None, "tensor"),
        P(None, "tensor"),
        P("tensor", None),
        P(),
        P(),
        P(),
        P(None, None, "tensor"),
        P(None, "tensor"),
        P("tensor", None),
        P(),
        P(),
        P(),
    )
    return jax.shard_map(
        per_device, mesh=mesh, in_specs=in_specs, out_specs=out_specs, check_vma=False
    )
```

```python
from functools import partial

import jax
import jax.numpy as jnp
from jax import lax
from jax.experimental import pallas as pl
from jax.experimental.pallas import tpu as pltpu
from jax.sharding import PartitionSpec as P

HEADS = 12
HEAD_DIM = 64
EPSILON = 1e-05
VMEM_LIMIT = 255 * 2**18
MESH = pl.DeviceIdType.MESH
BF = jnp.bfloat16
F32 = jnp.float32
NT = (((1,), (1,)), ((), ()))
TN = (((0,), (0,)), ((), ()))
NN = (((1,), (0,)), ((), ()))
DIRECT = (3,)


def dot(a, b, dims=NN):
    return lax.dot_general(a, b, dims, preferred_element_type=F32)


def remote(src, dst, send, recv, to):
    return pltpu.make_async_remote_copy(
        src_ref=src, dst_ref=dst, send_sem=send, recv_sem=recv, device_id=to, device_id_type=MESH
    )


def local(src, dst, sem):
    return pltpu.make_async_copy(src, dst, sem)


def dma(*shape):
    return pltpu.SemaphoreType.DMA(shape)


def chunk_rows(ndp, rows):
    return -(-rows // (16 * ndp)) * 16


class Links:
    def __init__(self, ndp):
        self.ndp = ndp
        self.na = ndp // 2
        self.dp = lax.axis_index("dp")
        self.t = lax.axis_index("tensor")
        self.a = self.dp // 2
        self.b = lax.rem(self.dp, 2)
        self.y = self.t // 2
        self.c = lax.rem(self.t, 2)
        self.core = (self.dp, 2 * self.y + 1 - self.c)
        self.far = (self.dp, 2 * (1 - self.y) + self.c)
        self.cross = (self.dp, 2 * (1 - self.y) + 1 - self.c)
        self.pair = (2 * self.a + 1 - self.b, self.t)

    def up(self, off):
        return lax.rem(self.a + off, self.na)

    def down(self, off):
        return lax.rem(self.a + self.na - off, self.na)

    def column(self, off):
        return (2 * self.up(off) + self.b, self.t)

    def quarter(self, s):
        return 2 * lax.rem(self.y + s // 2, 2) + lax.rem(self.c + s % 2, 2)

    def greet(self):
        barrier = pltpu.get_barrier_semaphore()
        others = [self.core, self.far, self.cross, self.pair]
        others += [self.column(o) for o in range(1, self.na)]
        for other in others:
            pl.semaphore_signal(barrier, inc=1, device_id=other, device_id_type=MESH)
        pl.semaphore_wait(barrier, len(others))


class Gather:
    def __init__(self, links, own, place, sems, rows):
        self.l, self.own, self.place, self.s = links, own, place, sems
        self.cr = rows // links.ndp
        self.fits = rows % (16 * links.ndp) == 0

    def relayed(self, m):
        return self.fits and m not in DIRECT

    def share(self, ref, d):
        return ref.at[pl.ds(pl.multiple_of(d * self.cr, 16), self.cr)]

    def pair_of(self, name, m, i=None):
        s, r = self.s[name]
        return (s.at[m], r.at[m]) if i is None else (s.at[m, i], r.at[m, i])

    def core(self, m):
        return remote(self.own(m), self.place(m, 1), *self.pair_of("c", m), self.l.core)

    def core_far(self, m):
        return remote(self.place(m, 2), self.place(m, 3), *self.pair_of("cf", m), self.l.core)

    def over_y(self, m):
        src, dst = self.own(m), self.place(m, 2)
        if self.relayed(m):
            src, dst = self.share(src, self.l.dp), self.share(dst, self.l.dp)
        return remote(src, dst, *self.pair_of("y", m), self.l.far)

    def over_x(self, m, off):
        at = self.share(self.place(m, 2), 2 * self.l.down(off) + self.l.b)
        return remote(at, at, *self.pair_of("x", m, off), self.l.pair)

    def over_z(self, m, off):
        at = self.share(self.place(m, 2), self.l.dp)
        return remote(at, at, *self.pair_of("z", m, off - 1), self.l.column(off))

    def step_spread(self, m):
        if self.relayed(m):
            self.over_y(m).wait_recv()
            self.over_x(m, 0).start()
            for off in range(1, self.l.na):
                self.over_z(m, off).start()

    def step_on(self, m):
        if self.relayed(m):
            for off in range(1, self.l.na):
                self.over_z(m, off).wait_recv()
                self.over_x(m, off).start()

    def step_core(self, m):
        if self.relayed(m):
            for off in range(self.l.na):
                self.over_x(m, off).wait_recv()
        else:
            self.over_y(m).wait_recv()
        self.core_far(m).start()

    def finish(self, m):
        self.core(m).wait_send()
        self.over_y(m).wait_send()
        self.core_far(m).wait_send()
        if self.relayed(m):
            for off in range(self.l.na):
                self.over_x(m, off).wait_send()
            for off in range(1, self.l.na):
                self.over_z(m, off).wait_send()


class Reducer:
    def __init__(self, links, refs, sems):
        self.l = links
        self.near, self.far, self.ybuf, self.xbuf, self.zbuf, self.own, self.fin = refs
        self.s = sems
        self.split = self.near.shape[1]
        self.cr = self.near.shape[4]
        self.rows = self.far.shape[2]
        self.units = self.near.shape[0] * self.split

    def block(self, u):
        return u // self.split, u % self.split

    def shares(self, first, count):
        for row in range(first, first + count, self.cr):
            j, inside = row // self.rows, row % self.rows // self.cr
            yield j, inside // 2, inside % 2, row

    def put_near(self, k, first, value):
        for j, i, b, row in self.shares(first, value.shape[0]):
            self.near[k, j, i, b] = value[row - first : row - first + self.cr].astype(BF)

    def put_far(self, k, first, value):
        for row in range(first, first + value.shape[0], self.cr):
            at = pl.ds(row % self.rows, self.cr)
            self.far[k, row // self.rows, at] = value[row - first : row - first + self.cr].astype(BF)

    def clear_padding(self):
        for i in range(self.rows // self.cr // 2, self.l.na):
            self.near[:, :, i] = jnp.zeros_like(self.near[:, :, i])

    def copy_y(self, u):
        s, r = self.s["y"]
        return remote(self.far.at[self.block(u)], self.ybuf.at[self.block(u)], s.at[u], r.at[u], self.l.far)

    def copy_x(self, u):
        s, r = self.s["x"]
        k, j = self.block(u)
        return remote(self.near.at[k, j, :, 1 - self.l.b], self.xbuf.at[u], s.at[u], r.at[u], self.l.pair)

    def copy_z(self, u, off):
        s, r = self.s["z"]
        k, j = self.block(u)
        src = self.near.at[k, j, self.l.up(off), self.l.b]
        return remote(src, self.zbuf.at[u, off - 1], s.at[u, off - 1], r.at[u, off - 1], self.l.column(off))

    def place(self, u):
        k, j = self.block(u)
        return self.fin.at[k, j, self.l.a, self.l.b]

    def copy_gz(self, u, off):
        s, r = self.s["gz"]
        return remote(self.own.at[u], self.place(u), s.at[u, off - 1], r.at[u, off - 1], self.l.column(off))

    def copy_gx(self, u):
        s, r = self.s["gx"]
        k, j = self.block(u)
        at = self.fin.at[k, j, :, self.l.b]
        return remote(at, at, s.at[u], r.at[u], self.l.pair)

    def copy_own(self, u):
        return local(self.own.at[u], self.place(u), self.s["own"].at[u])

    def start_y(self, u):
        self.copy_y(u).start()

    def step_x(self, u):
        self.copy_y(u).wait_recv()
        k, j = self.block(u)
        for row in range(0, self.rows, self.cr):
            i = row // self.cr
            share = self.near.at[k, j, i // 2, i % 2]
            share[...] = (share[...].astype(F32) + self.ybuf[k, j, row : row + self.cr].astype(F32)).astype(BF)
        self.copy_x(u).start()

    def step_z(self, u):
        self.copy_x(u).wait_recv()
        k, j = self.block(u)
        for i in range(self.l.na):
            share = self.near.at[k, j, i, self.l.b]
            share[...] = (share[...].astype(F32) + self.xbuf[u, i].astype(F32)).astype(BF)
        for off in range(1, self.l.na):
            self.copy_z(u, off).start()

    def step_own(self, u):
        k, j = self.block(u)
        total = self.near[k, j, self.l.a, self.l.b].astype(F32)
        for off in range(1, self.l.na):
            self.copy_z(u, off).wait_recv()
            total = total + self.zbuf[u, off - 1].astype(F32)
        self.spread(u, total)

    def spread(self, u, total):
        self.own[u] = total.astype(BF)
        for off in range(1, self.l.na):
            self.copy_gz(u, off).start()
        self.copy_own(u).start()

    def step_on(self, u):
        self.copy_own(u).wait()
        for off in range(1, self.l.na):
            self.copy_gz(u, off).wait_recv()
        self.copy_gx(u).start()

    def finish(self, u):
        self.copy_y(u).wait_send()
        self.copy_x(u).wait_send()
        for off in range(1, self.l.na):
            self.copy_z(u, off).wait_send()
            self.copy_gz(u, off).wait_send()
        self.copy_gx(u).wait()


class SmallSum:
    def __init__(self, links, mine, got, sems):
        self.l, self.mine, self.got = links, mine, got
        self.ss, self.rs = sems
        self.levels = got.shape[0]

    def partner(self, i):
        if i < 3:
            return (self.l.core, self.l.far, self.l.pair)[i]
        step = 2 ** (i - 3)
        a = self.l.a + step - 2 * step * lax.rem(self.l.a // step, 2)
        return (2 * a + self.l.b, self.l.t)

    def swap(self, i):
        return remote(self.mine.at[i], self.got.at[i], self.ss.at[i], self.rs.at[i], self.partner(i))

    def start(self, i):
        self.swap(i).start()

    def add(self, i):
        self.swap(i).wait_recv()
        total = self.mine[i] + self.got[i]
        if i + 1 < self.levels:
            self.mine[i + 1] = total
            self.start(i + 1)
        return total

    def finish(self):
        for i in range(self.levels):
            self.swap(i).wait_send()


def positions(links, size):
    y, c = links.y, links.c
    return [(2 * y + c) * size, (2 * (1 - y) + c) * size, (2 * y + 1 - c) * size, (2 * (1 - y) + 1 - c) * size]


def fill_distance(firsts, size, dist_ref):
    for kb, key in enumerate(firsts):
        for qb, query in enumerate(firsts[:2]):
            row = lax.broadcasted_iota(jnp.int32, (size, size), 0) + key
            col = lax.broadcasted_iota(jnp.int32, (size, size), 1) + query
            dist_ref[kb * size : (kb + 1) * size, qb * size : (qb + 1) * size] = jnp.abs(row - col).astype(F32)


def second_segment(links, size, r, block):
    y = links.y
    place = lax.broadcasted_iota(jnp.int32, (size, 1), 0) + positions(links, size)[block]
    return jnp.where(place >= r.boundary[y], r.type_ids[y, 1], r.type_ids[y, 0]) == 1


def mean(a):
    return jnp.mean(a, axis=-1, keepdims=True)


def norm_forward(values):
    centered = values - mean(values)
    scale = lax.rsqrt(mean(centered * centered) + EPSILON)
    return centered * scale, scale


def norm_backward(grad, unit, scale, gain):
    n = grad * gain
    return scale * (n - mean(n) - unit * mean(n * unit))


def gelu_parts(gate):
    e = jnp.exp(gate * gate * -0.5)
    t = 1.0 / (1.0 + jnp.abs(gate) * (0.3275911 * 0.5**0.5))
    poly = t * (
        0.5 * 0.254829592
        + t * (0.5 * -0.284496736 + t * (0.5 * 1.421413741 + t * (0.5 * -1.453152027 + t * (0.5 * 1.061405429))))
    )
    tail = poly * e
    return jnp.where(gate < 0, tail, 1.0 - tail), e * 0.3989422804014327


class Names:
    def __init__(self):
        self.names, self.shapes = [], []

    def add(self, name, shape):
        self.names.append(name)
        self.shapes.append(shape)

    def pair(self, name, *shape):
        self.add(name + "_s", dma(*shape))
        self.add(name + "_r", dma(*shape))


ANY = pl.BlockSpec(memory_space=pl.ANY)
VMEM = pl.BlockSpec(memory_space=pltpu.VMEM)
SMEM = pl.BlockSpec(memory_space=pltpu.SMEM)


class Refs:
    def __init__(self, names, refs):
        self.__dict__.update(zip(names, refs))

    def sems(self, name):
        return getattr(self, name + "_s"), getattr(self, name + "_r")


ENTER_IN = ["tokens", "wqkv", "wout", "wgu", "wdown", "b_qv", "b_gu", "b_out", "table"]
ENTER_IN += ["type_ids", "boundary", "slopes"]
ENTER_OUT = ["mixed", "xlow", "qkv", "kvp", "ctx", "lse", "wall", "biases"]
MATRICES = 4


def enter_kernel(ndp, names, *refs):
    r = Refs(names, refs)
    l = Links(ndp)
    nm, width = MATRICES, r.wdown.shape[1]
    size = r.tokens.shape[1]
    rows = 2 * size
    heads_dev = HEADS // 4
    qk = heads_dev * HEAD_DIM
    firsts = positions(l, size)

    def place(m, s):
        return r.wa.at[s] if m == 0 else r.wall.at[m, s]

    def own(m):
        return (r.wa.at[0], r.gu.at[0], r.gu.at[1], r.wdown)[m]

    g = Gather(l, own, place, {n: r.sems("g" + n) for n in ("c", "cf", "y", "x", "z")}, width)
    tok_own = local(r.tokens.at[l.y], r.tok.at[pl.ds(0, size)], r.ld.at[0])
    wa_own = [
        local(r.wqkv, r.wa.at[0, pl.ds(0, 3 * qk)], r.ld.at[1]),
        local(r.wout, r.wa.at[0, pl.ds(3 * qk, qk)], r.ld.at[2]),
    ]
    gu_own = local(r.wgu, r.graw, r.ld.at[3])
    for c in (*wa_own, tok_own, gu_own):
        c.start()
    tok_far = remote(r.tokens.at[1 - l.y], r.tok.at[pl.ds(size, size)], *(a.at[0] for a in r.sems("tk")), l.far)
    bias_to = [
        remote(r.biases.at[0], r.biases.at[s], *(a.at[s] for a in r.sems("bi")), to)
        for s, to in ((1, l.core), (2, l.far), (3, l.cross))
    ]

    def kv_send(s):
        other = s + 1 - 2 * (s % 2)
        src = r.qkvb.at[s, pl.ds(qk, 2 * qk)]
        return remote(src, r.kvb.at[other], *(a.at[s] for a in r.sems("kv")), l.core)

    def kv_wait(s):
        other = s + 1 - 2 * (s % 2)
        src = r.qkvb.at[other, pl.ds(qk, 2 * qk)]
        return remote(src, r.kvb.at[s], *(a.at[other] for a in r.sems("kv")), l.core)

    r.biases[0] = jnp.zeros_like(r.biases[0])
    r.biases[0, 0:1, :qk] = r.b_qv[0:1]
    r.biases[0, 0:1, 2 * qk : 3 * qk] = r.b_qv[1:2]
    r.biases[0, 1:3, :] = r.b_gu[...]
    l.greet()
    for c in wa_own:
        c.wait()
    g.over_y(0).start()
    g.core(0).start()
    for b in bias_to:
        b.start()

    def enter(block):
        at = pl.ds(block * size, size)
        second = second_segment(l, size, r, block)
        x = r.tok[at].astype(F32) + jnp.where(second, r.table[1:2], r.table[0:1])
        r.xb[at] = x
        r.xl[at] = x.astype(BF)

    def project(s, block):
        at = slice(block * size, (block + 1) * size)
        column = r.biases[s].T[: 3 * qk, 0:1]
        part = dot(r.wa[s, : 3 * qk], r.xl[at], NT) + column
        r.qkvb[s, :, at] = part.astype(BF)

    tok_own.wait()
    enter(0)
    project(0, 0)
    tok_far.start()
    for b in bias_to:
        b.wait_recv()
    g.core(0).wait_recv()
    project(1, 0)
    g.step_spread(0)
    gu_own.wait()
    for i in range(2):
        r.gu[i] = r.graw[:, i, :]
    gu_out = local(r.gu, r.wall.at[pl.ds(1, 2), 0], r.ld.at[4])
    gu_out.start()
    for m in (1, 2):
        g.over_y(m).start()
    fill_distance(firsts, size, r.dist)
    tok_far.wait_recv()
    g.over_y(3).start()
    enter(1)
    x_out = local(r.xl, r.xlow, r.ld.at[5])
    x_out.start()
    for s in (0, 1):
        project(s, 1)
        kv_send(s).start()
    g.step_on(0)
    for m in range(1, nm):
        g.core(m).start()

    def head(ticks, h, carry):
        s, j = h // heads_dev, h % heads_dev

        @pl.when(j == 0)
        def _():
            kv_wait(s).wait_recv()

        def lines(ref, first):
            return ref[s, pl.ds(pl.multiple_of(first + j * HEAD_DIM, HEAD_DIM), HEAD_DIM), :]

        q = lines(r.qkvb, 0) * BF(HEAD_DIM**-0.5)
        slope = r.slopes[l.quarter(s) * heads_dev + j]
        scores = [
            dot(key, q, TN) - slope * r.dist[i * rows : (i + 1) * rows]
            for i, key in enumerate((lines(r.qkvb, qk), lines(r.kvb, 0)))
        ]
        top = jnp.maximum(*(jnp.max(a, axis=0, keepdims=True) for a in scores))
        probs = [jnp.exp(a - top) for a in scores]
        total = sum(jnp.sum(a, axis=0, keepdims=True) for a in probs)
        values = (lines(r.qkvb, 2 * qk), lines(r.kvb, qk))
        out = sum(dot(v, p.astype(BF)) for v, p in zip(values, probs))
        r.ctxb[s, pl.ds(pl.multiple_of(j * HEAD_DIM, HEAD_DIM), HEAD_DIM), :] = (out * (1.0 / total)).astype(BF)
        r.lse[pl.ds(h, 1), :] = top + jnp.log(total)
        for at, steps in ticks.items():

            @pl.when(h == at)
            def _(steps=steps):
                for step in steps:
                    step()

        return carry

    lax.fori_loop(
        0,
        HEADS // 2,
        partial(
            head,
            {
                1: [partial(g.step_spread, 1), partial(g.step_spread, 2)],
                5: [partial(g.step_core, 0)],
            },
        ),
        0,
    )
    g.core_far(0).wait_recv()
    for s in (2, 3):
        for block in range(2):
            project(s, block)
        kv_send(s).start()
    wa_out = local(r.wa, r.wall.at[0], r.ld.at[6])
    wa_out.start()
    lax.fori_loop(
        HEADS // 2,
        HEADS,
        partial(head, {7: [partial(g.step_on, 1)], 8: [partial(g.step_on, 2)]}),
        0,
    )
    outs = [
        local(r.qkvb, r.qkv, r.ld.at[7]),
        local(r.kvb, r.kvp, r.ld.at[8]),
        local(r.ctxb, r.ctx, r.ld.at[9]),
    ]
    for o in outs:
        o.start()
    g.step_core(3)
    for s in range(4):
        part = dot(r.ctxb[s], r.wa[s, 3 * qk :], TN)
        r.xb[...] += part + r.b_out[...].reshape(1, width) if s == 0 else part
    mixed_out = local(r.xb, r.mixed, r.ld.at[10])
    mixed_out.start()
    g.step_core(1)
    g.step_core(2)
    for m in range(1, nm):
        g.core(m).wait_recv()
        g.core_far(m).wait_recv()
    for m in range(nm):
        g.finish(m)
    for s in range(4):
        kv_send(s).wait_send()
    tok_far.wait_send()
    for b in bias_to:
        b.wait_send()
    for o in outs + [gu_out, x_out, wa_out, mixed_out]:
        o.wait()


def enter_layer(ndp, inputs):
    tokens, width = inputs[0], inputs[0].shape[2]
    size = tokens.shape[1]
    rows = 2 * size
    qk = HEADS // 4 * HEAD_DIM
    na = ndp // 2
    nm = MATRICES
    n = Names()
    n.add("wa", pltpu.VMEM((4, width, width), BF))
    n.add("graw", pltpu.VMEM((width, 2, width), BF))
    n.add("gu", pltpu.VMEM((2, width, width), BF))
    n.add("tok", pltpu.VMEM((rows, width), BF))
    n.add("xb", pltpu.VMEM((rows, width), F32))
    n.add("xl", pltpu.VMEM((rows, width), BF))
    n.add("qkvb", pltpu.VMEM((4, 3 * qk, rows), BF))
    n.add("kvb", pltpu.VMEM((4, 2 * qk, rows), BF))
    n.add("ctxb", pltpu.VMEM((4, qk, rows), BF))
    n.add("dist", pltpu.VMEM((2 * rows, rows), F32))
    n.add("ld", dma(11))
    n.pair("tk", 1)
    n.pair("bi", 4)
    n.pair("kv", 4)
    n.pair("gc", nm)
    n.pair("gcf", nm)
    n.pair("gy", nm)
    n.pair("gx", nm, na)
    n.pair("gz", nm, na - 1)
    shape = jax.ShapeDtypeStruct
    return pl.pallas_call(
        partial(enter_kernel, ndp, ENTER_IN + ENTER_OUT + n.names),
        in_specs=[ANY, ANY, ANY, ANY, ANY, VMEM, VMEM, VMEM, VMEM, SMEM, SMEM, SMEM],
        out_specs=[ANY, ANY, ANY, ANY, ANY, VMEM, ANY, VMEM],
        out_shape=[
            shape((rows, width), F32),
            shape((rows, width), BF),
            shape((4, 3 * qk, rows), BF),
            shape((4, 2 * qk, rows), BF),
            shape((4, qk, rows), BF),
            shape((HEADS, rows), F32),
            shape((nm, 4, width, width), BF),
            shape((4, 8, width), F32),
        ],
        scratch_shapes=n.shapes,
        compiler_params=pltpu.CompilerParams(
            collective_id=0, has_side_effects=True, vmem_limit_bytes=VMEM_LIMIT
        ),
    )(*inputs)


LEAVE_IN = ["mixed", "xlow", "qkv", "kvp", "ctx", "lse", "wall", "biases", "wdown"]
LEAVE_IN += ["gain_one", "shift_one", "b_down", "gain_two", "shift_two"]
LEAVE_IN += ["cot", "type_ids", "boundary", "slopes"]
LEAVE_OUT = ["fin", "sums", "out", "gtok", "cbuf"]
DOWN, GATE, UP, ATTN = range(4)
ROW_GU, ROW_QV, SMALL_ROWS = 8, 16, 24


def leave_kernel(ndp, names, *refs):
    r = Refs(names, refs)
    l = Links(ndp)
    rows, width = r.mixed.shape
    size = rows // 2
    heads_dev = HEADS // 4
    qk = heads_dev * HEAD_DIM
    firsts = positions(l, size)
    stages = r.cstage.shape[0]
    red = Reducer(
        l,
        (r.near, r.far, r.ybuf, r.xbuf, r.zbuf, r.own, r.fin),
        {**{n: r.sems("r" + n) for n in ("y", "x", "z", "gz", "gx")}, "own": r.rown},
    )
    pump = Pump(red, schedule(red.units))
    small = SmallSum(l, r.smine, r.sgot, r.sems("sm"))
    sv = r.smine.at[0]

    def vec(ref):
        return ref[...].reshape(1, width)

    def core_copy(k, i):
        src = r.cstage.at[k % stages, i]
        return remote(src, r.cbuf.at[k, i], *(a.at[k, i] for a in r.sems("co")), l.core)

    def fetch(k, i):
        slot = (1 - i, 0, 1, 1 - i)[k]
        return local(r.cbuf.at[k, i], r.cload.at[slot], r.cl.at[slot])

    def room(k, i):
        if k >= stages:
            core_copy(k - stages, i).wait_send()

    def start_fetch(k, i):
        core_copy(k, i).wait_recv()
        fetch(k, i).start()

    def merge(k, i, first, value):
        slot = (1 - i, 0, 1, 1 - i)[k]
        total = value + r.cload[slot, pl.ds(first, value.shape[0])].astype(F32)
        (red.put_near, red.put_far)[i](k, first, total)

    out_own = local(r.outb.at[pl.ds(0, size)], r.out.at[l.y], r.ld.at[8])
    out_far = remote(r.outb.at[pl.ds(size, size)], r.out.at[l.y], *(a.at[0] for a in r.sems("ou")), l.far)
    cot_own = local(r.cot.at[l.y], r.cotb.at[pl.ds(0, size)], r.ld.at[0])
    cot_far = remote(r.cot.at[1 - l.y], r.cotb.at[pl.ds(size, size)], *(a.at[0] for a in r.sems("ct")), l.far)

    def order(i):
        return 2 * (i % 2) + i // 2

    def ffn_phase(wo, gh, a_ref, b_ref, hid, unit, hl, ht, r1, wbuf):
        acc, gf = r.gm, hl

        def load_weights(s, buf):
            return local(r.wall.at[pl.ds(1, 3), s], wbuf.at[buf], r.wl.at[buf])

        def start_weights(s, buf):
            if s:
                load_weights(s, buf).start()
            else:
                local(r.wall.at[pl.ds(1, 2), 0], wbuf.at[buf, pl.ds(0, 2)], r.wl.at[buf]).start()
                local(r.wdown, wbuf.at[buf, 2], r.wl.at[buf]).start()

        lx = local(r.mixed, acc, r.ld.at[1])
        lo = local(r.wall.at[0, pl.ds(0, 4), pl.ds(3 * qk, qk)], wo, r.ld.at[2])
        lc = local(r.ctx, r.ctxb, r.ld.at[3])
        lx.start()
        start_weights(0, 0)
        start_weights(2, 1)
        for c in (cot_own, lo, lc):
            c.start()
        l.greet()
        cot_far.start()
        red.clear_padding()
        sv[...] = jnp.zeros_like(sv)
        lx.wait()
        u1, s1 = norm_forward(acc[...])
        unit[...] = u1
        r1[...] = s1
        h1 = u1 * vec(r.gain_one) + vec(r.shift_one)
        acc[...] = h1 + vec(r.b_down)
        hl[...] = h1.astype(BF)
        ht[...] = h1.T.astype(BF)

        def forward(i, carry):
            s, buf = order(i), i % 2
            load_weights(s, buf).wait()
            for half in range(2):
                at = slice(half * size, (half + 1) * size)
                gate = dot(hl[at], wbuf[buf, 0]) + r.biases[s, 1:2, :]
                up = dot(hl[at], wbuf[buf, 1]) + r.biases[s, 2:3, :]
                cdf, pdf = gelu_parts(gate)
                act = gate * cdf
                a_ref[s, at] = act.astype(BF)
                b_ref[s, at] = (up * (cdf + gate * pdf)).astype(BF)
                hidden = (act * up).astype(BF)
                hid[s, at] = hidden
                acc[at] += dot(hidden, wbuf[buf, 2])

            @pl.when(i < 2)
            def _():
                load_weights(order(i + 2), buf).start()

            return carry

        lax.fori_loop(0, 4, forward, 0)
        u2, s2 = norm_forward(acc[...])
        out = u2 * vec(r.gain_two) + vec(r.shift_two)
        r.outb[...] = out.astype(BF)
        out_far.start()
        cot_own.wait()
        cot_far.wait_recv()
        cot = r.cotb[...].astype(F32)
        g2 = norm_backward(cot, u2, s2, vec(r.gain_two))
        sv[6:7, :] = jnp.sum(cot * u2, axis=0, keepdims=True)
        sv[7:8, :] = jnp.sum(cot, axis=0, keepdims=True)
        sv[5:6, :] = jnp.sum(g2, axis=0, keepdims=True)
        gh[...] = g2
        gf[...] = g2.astype(BF)
        for i, s in ((1, 3), (0, 1)):
            r.cstage[DOWN % stages, i] = dot(hid[s], gf[...], TN).astype(BF)
            core_copy(DOWN, i).start()

        def backward(s, buf):
            load = None
            g_hidden = dot(gf[...], wbuf[buf, 2], NT)
            g_gate = (g_hidden * b_ref[s].astype(F32)).astype(BF)
            g_up = (g_hidden * a_ref[s].astype(F32)).astype(BF)
            row = ROW_GU + 2 * l.quarter(s)
            sv[pl.ds(row, 1), :] = jnp.sum(g_gate.astype(F32), axis=0, keepdims=True)
            sv[pl.ds(row + 1, 1), :] = jnp.sum(g_up.astype(F32), axis=0, keepdims=True)
            gh[...] += dot(g_gate, wbuf[buf, 0], NT)
            gh[...] += dot(g_up, wbuf[buf, 1], NT)
            return g_gate, g_up

        for i, s, buf in ((1, 3, 1), (0, 1, 0)):
            start_fetch(DOWN, i)
            value = dot(hid[s - 1], gf[...], TN)
            fetch(DOWN, i).wait()
            merge(DOWN, i, 0, value)
            for u in range(min(AHEAD, red.split)):
                if (u > 0) == (i == 0):
                    red.start_y(u)
            g_gate, g_up = backward(s, buf)
            start_weights(s - 1, buf)
            for k, g in ((GATE, g_gate), (UP, g_up)):
                room(k, i)
                r.cstage[k % stages, i] = dot(ht[...], g).astype(BF)
                core_copy(k, i).start()
        for i, s, buf in ((1, 2, 1), (0, 0, 0)):
            load_weights(s, buf).wait()
            for k in (GATE, UP):
                start_fetch(k, i)
            g_gate, g_up = backward(s, buf)
            for k, g in ((GATE, g_gate), (UP, g_up)):
                value = dot(ht[...], g)
                fetch(k, i).wait()
                merge(k, i, 0, value)
            pump.until(POINTS[1 - i])
        lc.wait()
        lo.wait()
        g_h1 = gh[...]
        unit_one = unit[...]
        sv[3:4, :] = jnp.sum(g_h1 * unit_one, axis=0, keepdims=True)
        sv[4:5, :] = jnp.sum(g_h1, axis=0, keepdims=True)
        gm = norm_backward(g_h1, unit_one, r1[...], vec(r.gain_one))
        sv[2:3, :] = jnp.sum(gm, axis=0, keepdims=True)
        r.gm[...] = gm
        ga = gm.astype(BF)
        r.cotb[...] = ga
        for s in range(4):
            r.gctx[s] = dot(wo[s], ga, NT).astype(BF)

    v = pltpu.VMEM
    pl.run_scoped(
        ffn_phase,
        v((4, qk, width), BF),
        v((rows, width), F32),
        v((4, rows, width), BF),
        v((4, rows, width), BF),
        v((4, rows, width), BF),
        v((rows, width), F32),
        v((rows, width), BF),
        v((width, rows), BF),
        v((rows, 1), F32),
        v((2, 3, width, width), BF),
    )

    def attention_phase(wq, qkvb, kvb, xl, dist, dqkv, dkvo, dkvs):
        lq = local(r.qkv, qkvb, r.ld.at[4])
        lk = local(r.kvp, kvb, r.ld.at[5])
        lw = local(r.wall.at[0, pl.ds(0, 4), pl.ds(0, 3 * qk)], wq, r.ld.at[6])
        lx = local(r.xlow, xl, r.ld.at[7])
        lq.start()
        lk.start()
        fill_distance(firsts, size, dist)

        def other(s):
            return s + 1 - 2 * (s % 2)

        def send(s):
            return remote(dkvs.at[s], r.dkvr.at[other(s)], *(a.at[s] for a in r.sems("dk")), l.core)

        def arrived(s):
            return remote(dkvs.at[other(s)], r.dkvr.at[s], *(a.at[other(s)] for a in r.sems("dk")), l.core)

        lq.wait()
        lk.wait()

        def head(first, h, carry):
            s, j = h // heads_dev, h % heads_dev

            def span(first):
                return pl.ds(pl.multiple_of(first + j * HEAD_DIM, HEAD_DIM), HEAD_DIM)

            qt = qkvb[s, span(0), :] * BF(HEAD_DIM**-0.5)
            q = qt.T
            dot_t = r.gctx[s, span(0), :]
            do = dot_t.T
            slope = r.slopes[l.quarter(s) * heads_dev + j]
            lse = r.lse[pl.ds(h, 1), :]
            keys = (qkvb[s, span(qk), :], kvb[s, span(0), :])
            values = (qkvb[s, span(2 * qk), :], kvb[s, span(qk), :])
            probs = [
                jnp.exp(dot(key, qt, TN) - slope * dist[i * rows : (i + 1) * rows] - lse)
                for i, key in enumerate(keys)
            ]
            g_probs = [dot(value, dot_t, TN) for value in values]
            inner = sum(jnp.sum(p * g, axis=0, keepdims=True) for p, g in zip(probs, g_probs))
            g_scores = [(p * (g - inner)).astype(BF) for p, g in zip(probs, g_probs)]
            dq = sum(dot(key, g) for key, g in zip(keys, g_scores))
            dqkv[s, span(0), :] = (dq * HEAD_DIM**-0.5).astype(BF)
            dk = [dot(g, q).T for g in g_scores]
            dv = [dot(p.astype(BF), do).T for p in probs]
            dkvo[s, span(0), :] = dk[0]
            dkvo[s, span(qk), :] = dv[0]
            dkvs[s, span(0), :] = dk[1].astype(BF)
            dkvs[s, span(qk), :] = dv[1].astype(BF)

            @pl.when(j == heads_dev - 1)
            def _():
                send(s).start()

            if first:

                @pl.when(h == first)
                def _():
                    lw.start()
                    lx.start()

            else:

                @pl.when(h == 1)
                def _():
                    start_fetch(ATTN, 1)
                    finish_attn(1, 2)

            for at in range(first, first + HEADS // 2):
                time = HEAD_TIMES[0 if first else 1] + HEAD_TIMES[2] * (at + 1 - first)
                if pump.due(time):

                    @pl.when(h == at)
                    def _(time=time):
                        pump.until(time)

            return carry

        def collect(s):
            arrived(s).wait_recv()
            dqkv[s, qk:, :] = (dkvo[s] + r.dkvr[s].astype(F32)).astype(BF)
            g = dqkv[s]
            sv[pl.ds(ROW_QV + l.quarter(s), 1), : 3 * qk] = dot(jnp.ones((8, rows), BF), g, NT)[0:1]
            r.gm[...] += dot(g, wq[s], TN)

        def attn_parts(s):
            return ((0, dot(dqkv[s], xl[...])), (3 * qk, dot(r.ctxb[s], r.cotb[...])))

        def send_attn(i, s):
            room(ATTN, i)
            for at, value in attn_parts(s):
                r.cstage[ATTN % stages, i, pl.ds(at, value.shape[0])] = value.astype(BF)
            core_copy(ATTN, i).start()

        def finish_attn(i, s):
            parts = attn_parts(s)
            fetch(ATTN, i).wait()
            for at, value in parts:
                merge(ATTN, i, at, value)

        lax.fori_loop(HEADS // 2, HEADS, partial(head, HEADS // 2), 0)
        lw.wait()
        lx.wait()
        collect(3)
        send_attn(1, 3)
        collect(2)
        pump.until(POINTS[2])
        lax.fori_loop(0, HEADS // 2, partial(head, 0), 0)
        collect(1)
        send_attn(0, 1)
        collect(0)
        pump.until(POINTS[3])
        start_fetch(ATTN, 0)
        g_entered = r.gm[...]
        total = jnp.sum(g_entered, axis=0, keepdims=True)
        second = sum(
            jnp.sum(
                jnp.where(second_segment(l, size, r, i), g_entered[i * size : (i + 1) * size], 0.0),
                axis=0,
                keepdims=True,
            )
            for i in range(2)
        )
        sv[0:1, :] = total - second
        sv[1:2, :] = second
        small.start(0)

        finish_attn(0, 0)
        for s in range(4):
            send(s).wait_send()

    pl.run_scoped(
        attention_phase,
        v((4, 3 * qk, width), BF),
        v((4, 3 * qk, rows), BF),
        v((4, 2 * qk, rows), BF),
        v((rows, width), BF),
        v((2 * rows, rows), F32),
        v((4, 3 * qk, rows), BF),
        v((4, 2 * qk, rows), F32),
        v((4, 2 * qk, rows), BF),
    )

    tok_own = local(r.gm.at[pl.ds(0, size)], r.gtok.at[l.y], r.ld.at[9])
    r.cload[0, :size] = r.gm[size:].astype(BF)
    tok_far = remote(r.cload.at[0, pl.ds(0, size)], r.ggot, *(a.at[0] for a in r.sems("gt")), l.far)
    out_own.start()
    tok_own.start()
    pump.after_y = tok_far.start
    for i in range(small.levels):
        total = small.add(i)
        pump.until(POINTS[3] + 12.0 * (i + 1))
    pump.until(None)
    r.sums[...] = total
    tok_far.wait_recv()
    r.gm[size:] = r.ggot[...].astype(F32)
    tok_got = local(r.gm.at[pl.ds(size, size)], r.gtok.at[1 - l.y], r.ld.at[10])
    tok_got.start()
    for u in range(red.units):
        red.finish(u)
    for k in range(4 - stages, 4):
        for i in range(2):
            core_copy(k, i).wait_send()
    small.finish()
    cot_far.wait_send()
    out_far.wait()
    tok_far.wait_send()
    for c in (out_own, tok_own, tok_got):
        c.wait()


AHEAD = 2
HEAD_TIMES = (34.0, 53.0, 2.3)
POINTS = (20.0, 27.0, 53.0, 72.0)
READY = (4.0, 19.0, 21.0, 58.0)


def schedule(units):
    unit = 84.0 / units
    free = {"y": 0.0, "x": 0.0, "z": 0.0}
    waiting, order = [], []
    split = units // 4

    def use(link, at, cost):
        free[link] = max(free[link], at) + cost
        return free[link] + 2.0

    def start_y(u, at):
        waiting.append((use("y", max(at, READY[u // split]), unit), u, "step_x"))

    for u in range(min(AHEAD, units)):
        start_y(u, 0.0)
        if u >= split:
            order.append((READY[u // split], "start_y", u))
    now = 0.0
    while waiting:
        waiting.sort()
        at, u, step = waiting.pop(0)
        now = max(now, at)
        order.append((now, step, u))
        now += 0.5
        if step == "step_x":
            if u + AHEAD < units:
                order.append((max(now, READY[(u + AHEAD) // split]), "start_y", u + AHEAD))
                start_y(u + AHEAD, now)
            waiting.append((use("x", now, unit / 2), u, "step_z"))
        elif step == "step_z":
            waiting.append((use("z", now, unit / 2), u, "step_own"))
        elif step == "step_own":
            waiting.append((use("z", now, unit / 2), u, "step_on"))
        else:
            use("x", now, unit / 2)
    return sorted(order, key=lambda o: o[0])


class Pump:
    def __init__(self, red, order):
        self.red, self.order, self.after_y = red, list(order), None

    def due(self, time):
        return bool(self.order) and (time is None or self.order[0][0] <= time)

    def until(self, time):
        while self.due(time):
            _, step, u = self.order.pop(0)
            getattr(self.red, step)(u)
            if step == "step_x" and u == self.red.units - 1:
                self.after_y()


def leave_layer(ndp, inputs, cot):
    wall = inputs[6]
    rows, width = inputs[0].shape
    nm = wall.shape[0]
    size = rows // 2
    qk = HEADS // 4 * HEAD_DIM
    na = ndp // 2
    split = 3 if width % (48 * ndp) == 0 else 1
    stages = 2 if split > 1 else 1
    units = nm * split
    unit = width // split
    cr = chunk_rows(ndp, unit)
    n = Names()
    v = pltpu.VMEM
    n.add("near", v((nm, split, na, 2, cr, width), BF))
    n.add("far", v((nm, split, unit, width), BF))
    n.add("ybuf", v((nm, split, unit, width), BF))
    n.add("xbuf", v((units, na, cr, width), BF))
    n.add("zbuf", v((units, na - 1, cr, width), BF))
    n.add("own", v((units, cr, width), BF))
    n.add("cstage", v((stages, 2, width, width), BF))
    n.add("cload", v((2, width, width), BF))
    n.add("ctxb", v((4, qk, rows), BF))
    n.add("gctx", v((4, qk, rows), BF))
    n.add("cotb", v((rows, width), BF))
    n.add("outb", v((rows, width), BF))
    n.add("gm", v((rows, width), F32))
    n.add("ggot", v((size, width), BF))
    n.add("dkvr", v((4, 2 * qk, rows), BF))
    levels = 3 + (na - 1).bit_length()
    n.add("smine", v((levels, SMALL_ROWS, width), F32))
    n.add("sgot", v((levels, SMALL_ROWS, width), F32))
    n.add("ld", dma(11))
    n.add("cl", dma(2))
    n.add("wl", dma(2))
    n.add("rown", dma(units))
    n.pair("co", nm, 2)
    n.pair("ct", 1)
    n.pair("ou", 1)
    n.pair("gt", 1)
    n.pair("dk", 4)
    n.pair("sm", levels)
    n.pair("ry", units)
    n.pair("rx", units)
    n.pair("rz", units, na - 1)
    n.pair("rgz", units, na - 1)
    n.pair("rgx", units)
    shape = jax.ShapeDtypeStruct
    fin, *others = pl.pallas_call(
        partial(leave_kernel, ndp, LEAVE_IN + LEAVE_OUT + n.names),
        in_specs=[ANY, ANY, ANY, ANY, ANY, VMEM, ANY, VMEM, ANY, *[VMEM] * 5, ANY, SMEM, SMEM, SMEM],
        out_specs=[ANY, VMEM, ANY, ANY, ANY],
        out_shape=[
            shape((nm, split, na, 2, cr, width), BF),
            shape((SMALL_ROWS, width), F32),
            shape(cot.shape, BF),
            shape(cot.shape, F32),
            shape((nm, 2, width, width), BF),
        ],
        scratch_shapes=n.shapes,
        compiler_params=pltpu.CompilerParams(
            collective_id=1, has_side_effects=True, vmem_limit_bytes=VMEM_LIMIT
        ),
    )(*inputs)
    return fin.reshape(nm, -1, width), *others


FINISH_IN = ["fin", "sums", "got", "gtok"]
FINISH_OUT = ["output", "g_tokens", "table", "g_qkv", "g_bqv", "g_out", "g_bout", "g_gain1", "g_shift1"]
FINISH_OUT += ["g_gu", "g_bgu", "g_down", "g_bdown", "g_gain2", "g_shift2"]
SUM_ROWS = {"g_bout": 2, "g_gain1": 3, "g_shift1": 4, "g_bdown": 5, "g_gain2": 6, "g_shift2": 7}


def finish_kernel(*refs):
    r = Refs(FINISH_IN + FINISH_OUT, refs)
    step, last = pl.program_id(0), pl.num_programs(0) - 1
    t = lax.axis_index("tensor")
    qk = r.g_bqv.shape[1]
    first_out = 3 * pl.num_programs(0) // 4
    r.output[...] = r.got[...]
    r.g_tokens[...] = r.gtok[...]
    r.g_gu[:, 0, :] = r.fin[GATE].astype(F32)
    r.g_gu[:, 1, :] = r.fin[UP].astype(F32)
    r.g_down[...] = r.fin[DOWN].astype(F32)

    @pl.when(step < first_out)
    def _():
        r.g_qkv[...] = r.fin[ATTN].astype(F32)

    @pl.when(step >= first_out)
    def _():
        r.g_out[...] = r.fin[ATTN].astype(F32)

    @pl.when(step == last)
    def _():
        r.table[...] = r.sums[0:2, :]
        for name, row in SUM_ROWS.items():
            getattr(r, name)[...] = r.sums[row]

    for quarter in range(4):

        @pl.when((step == last) & (t == quarter))
        def _(quarter=quarter):
            first, row = ROW_GU + 2 * quarter, ROW_QV + quarter
            r.g_bgu[...] = r.sums[first : first + 2, :]
            r.g_bqv[0:1, :] = r.sums[row : row + 1, :qk]
            r.g_bqv[1:2, :] = r.sums[row : row + 1, 2 * qk : 3 * qk]


def finish_layer(fin, sums, out, gtok):
    nm, width = fin.shape[0], fin.shape[2]
    seqs, size = out.shape[:2]
    qk = width // 4
    shape = jax.ShapeDtypeStruct
    whole = lambda *dims: pl.BlockSpec(dims, lambda i: (0,) * len(dims))
    steps = 4
    blk = width // steps
    rows_of = lambda: pl.BlockSpec((seqs, size // steps, width), lambda i: (0, i, 0))
    vector = (whole(width), shape((width,), F32))
    outs = {
        "output": (rows_of(), shape(out.shape, out.dtype)),
        "g_tokens": (rows_of(), shape(gtok.shape, gtok.dtype)),
        "table": (whole(2, width), shape((2, width), F32)),
        "g_qkv": (pl.BlockSpec((blk, width), lambda i: (jnp.minimum(i, 2), 0)), shape((3 * qk, width), F32)),
        "g_bqv": (whole(2, qk), shape((2, qk), F32)),
        "g_out": (pl.BlockSpec((blk, width), lambda i: (jnp.maximum(i - 3, 0), 0)), shape((qk, width), F32)),
        "g_gu": (pl.BlockSpec((blk, 2, width), lambda i: (i, 0, 0)), shape((width, 2, width), F32)),
        "g_bgu": (whole(2, width), shape((2, width), F32)),
        "g_down": (pl.BlockSpec((blk, width), lambda i: (i, 0)), shape((width, width), F32)),
        **{name: vector for name in SUM_ROWS},
    }
    return pl.pallas_call(
        finish_kernel,
        grid=(steps,),
        in_specs=[
            pl.BlockSpec((nm, blk, width), lambda i: (0, i, 0)),
            whole(*sums.shape),
            rows_of(),
            rows_of(),
        ],
        out_specs=[outs[name][0] for name in FINISH_OUT],
        out_shape=[outs[name][1] for name in FINISH_OUT],
        compiler_params=pltpu.CompilerParams(vmem_limit_bytes=VMEM_LIMIT),
    )(fin, sums, out, gtok)


def per_device(
    tokens,
    type_ids,
    boundary,
    token_type_rows,
    query_key_value_weight,
    b_qv,
    output_weight,
    b_out,
    gain_one,
    shift_one,
    gate_up_weight,
    gate_up_bias,
    down_weight,
    b_down,
    gain_two,
    shift_two,
    cotangent,
):
    ndp = lax.axis_size("dp")
    width, three, qk = query_key_value_weight.shape
    wqkv = query_key_value_weight.transpose(1, 2, 0).reshape(three * qk, width)
    slopes = jnp.asarray([2.0 ** (-8.0 * (h + 1) / HEADS) for h in range(HEADS)], F32)
    first = enter_layer(
        ndp,
        (
            tokens,
            wqkv,
            output_weight,
            gate_up_weight,
            down_weight,
            b_qv,
            gate_up_bias,
            b_out,
            token_type_rows,
            type_ids,
            boundary,
            slopes,
        ),
    )
    vectors = (gain_one, shift_one, b_down, gain_two, shift_two)
    fin, sums, out, gtok, _ = leave_layer(
        ndp, (*first, down_weight, *vectors, cotangent, type_ids, boundary, slopes), cotangent
    )
    results = list(finish_layer(fin, sums, out, gtok))
    at = FINISH_OUT.index("g_qkv")
    results[at] = results[at].reshape(three, qk, width).transpose(2, 0, 1)
    return tuple(results)


def solution(mesh):
    in_specs = (
        P("dp", "tensor", None),
        P("dp", None),
        P("dp"),
        P(),
        P(None, None, "tensor"),
        P(None, "tensor"),
        P("tensor", None),
        P(),
        P(),
        P(),
        P(None, None, "tensor"),
        P(None, "tensor"),
        P("tensor", None),
        P(),
        P(),
        P(),
        P("dp", "tensor", None),
    )
    out_specs = (
        P("dp", "tensor", None),
        P("dp", "tensor", None),
        P(),
        P(None, None, "tensor"),
        P(None, "tensor"),
        P("tensor", None),
        P(),
        P(),
        P(),
        P(None, None, "tensor"),
        P(None, "tensor"),
        P("tensor", None),
        P(),
        P(),
        P(),
    )
    return jax.shard_map(
        per_device, mesh=mesh, in_specs=in_specs, out_specs=out_specs, check_vma=False
    )
```
